32 devices in a mesh: fsdp: 16 (over z, y, x), tp: 2 (over core).
Axes of the slice: x: 2, y: 2, z: 4, core: 2. Of those that a mesh axis runs over, the one named last changes fastest.
Arguments:
- hidden: bfloat16 [16384, 1408], P(('fsdp', 'tp')), may hold values from -6 to 6
- skip_rows: bfloat16 [16384, 1408], P(('fsdp', 'tp')), may hold values from -6 to 6
- timestep: bfloat16 [16, 1408], P('fsdp'), may hold values from -6 to 6
- text: bfloat16 [5328, 1024], P('fsdp'), may hold values from -6 to 6
- grid_pos: int32 [16384, 2], P('fsdp'), may hold values from 0 to 62, as said below
- cotangent: bfloat16 [16384, 1408], P(('fsdp', 'tp')), may hold values from -6 to 6
- skip_weight: float32 [2816, 1408], P(('fsdp', 'tp')), may hold values from -0.109375 to 0.109375
- shift_weight: float32 [1408, 1408], P(('fsdp', 'tp')), may hold values from -0.15625 to 0.15625
- qkv_weight: float32 [1408, 3, 1408], P('fsdp', None, 'tp'), may hold values from -0.15625 to 0.15625
- cross_query: float32 [1408, 1408], P('fsdp', 'tp'), may hold values from -0.15625 to 0.15625
- cross_kv: float32 [1024, 2, 1408], P('fsdp', None, 'tp'), may hold values from -0.1875 to 0.1875
- out_weight: float32 [2, 1408, 1408], P(None, 'tp', 'fsdp'), may hold values from -2 to 2
- up_weight: float32 [1408, 6144], P('fsdp', 'tp'), may hold values from -0.15625 to 0.15625
- down_weight: float32 [6144, 1408], P('tp', 'fsdp'), may hold values from -0.078125 to 0.078125
- column_bias: float32 [6, 2, 704], P(None, 'tp', 'fsdp'), may hold values from -2 to 2
- up_bias: float32 [2, 3072], P('tp', 'fsdp'), may hold values from -2 to 2
- skip_gain: float32 [2816], P(('fsdp', 'tp')), may hold values from 0.5 to 1.5
- skip_bias: float32 [2816], P(('fsdp', 'tp')), may hold values from -2 to 2
- norm_gains: float32 [3, 1408], P(None, ('fsdp', 'tp')), may hold values from 0.5 to 1.5
- row_biases: float32 [8, 1408], P(None, ('fsdp', 'tp')), may hold values from -2 to 2
- head_gains: float32 [4, 88], replicated, may hold values from 0.5 to 1.5
- head_biases: float32 [4, 88], replicated, may hold values from -2 to 2
Outputs:
- output: bfloat16 [16384, 1408], P(('fsdp', 'tp'))
- input_grad: float32 [16384, 1408], P(('fsdp', 'tp'))
- skip_grad: float32 [16384, 1408], P(('fsdp', 'tp'))
- text_grad: float32 [5328, 1024], P('fsdp', 'tp')
- skip_weight_grad: float32 [2816, 1408], P(('fsdp', 'tp'))
- shift_weight_grad: float32 [1408, 1408], P(('fsdp', 'tp'))
- qkv_weight_grad: float32 [1408, 3, 1408], P('fsdp', None, 'tp')
- cross_query_grad: float32 [1408, 1408], P('fsdp', 'tp')
- cross_kv_grad: float32 [1024, 2, 1408], P('fsdp', None, 'tp')
- out_weight_grad: float32 [2, 1408, 1408], P(None, 'tp', 'fsdp')
- up_weight_grad: float32 [1408, 6144], P('fsdp', 'tp')
- down_weight_grad: float32 [6144, 1408], P('tp', 'fsdp')
- column_bias_grad: float32 [6, 2, 704], P(None, 'tp', 'fsdp')
- up_bias_grad: float32 [2, 3072], P('tp', 'fsdp')
- skip_gain_grad: float32 [2816], P(('fsdp', 'tp'))
- skip_bias_grad: float32 [2816], P(('fsdp', 'tp'))
- norm_gains_grad: float32 [3, 1408], P(None, ('fsdp', 'tp'))
- row_biases_grad: float32 [8, 1408], P(None, ('fsdp', 'tp'))
- head_gains_grad: float32 [4, 88], replicated
- head_biases_grad: float32 [4, 88], replicated
The draws below stay inside these ranges and needn't reach their ends.
Inputs may be any that keep to these rules, and one draw needn't show every extreme that they name: `grid_pos`: within each image the tokens lie in raster order on a rectangle of whole rows, 32 tokens wide, in either orientation; both coordinates are shifted by one offset of 0 to 31 for that image, and some image has offset 0 and some offset 31.
All inputs are finite; a program needn't handle non-finite values.
Results may differ from the reference program's by a relative error of at most 0.02.
Values may be sent and summed in bfloat16 or wider, within the bound.
No kernel may reach another device: no remote copies, remote signals or barrier semaphores. Data moves between devices by JAX's collectives and lax.ppermute only.
A program may use at most 384 MiB of HBM per device.

```python
import jax
import jax.numpy as jnp
from jax import lax

HEAD_DIM = 88
D = 1408
FF = 6144
TD = 1024
TXT = 333
SEQ = 1024
IMAGES = 16
TOKENS = 16384
TEXT_ROWS = 5328
N_TP = 2


def draw_grid_pos(key, part):
    side_len = min(32, SEQ // 4)
    order = jnp.arange(SEQ, dtype=jnp.int32)
    upright = jnp.stack([order // side_len, order % side_len], axis=1)
    sideways = jnp.stack([order % side_len, order // side_len], axis=1)
    flip_key = jax.random.fold_in(key, 7)
    offset_key = jax.random.fold_in(key, 11)
    pick_key = jax.random.fold_in(key, 13)
    flipped = jax.random.randint(flip_key, (IMAGES, 1, 1), 0, 2)
    offsets = jax.random.randint(offset_key, (IMAGES, 1, 1), 0, 32)
    picked = jax.random.randint(pick_key, (), 0, IMAGES)
    image_ids = jnp.arange(IMAGES, dtype=jnp.int32)[:, None, None]
    offsets = jnp.where(image_ids == picked, 31, offsets)
    offsets = jnp.where(image_ids == (picked + 1) % IMAGES, 0, offsets)
    grid = jnp.where(flipped == 1, sideways[None], upright[None]) + offsets
    return grid.reshape(IMAGES * SEQ, 2).astype(jnp.int32)


def level_of(rng, shape, split, smallest, top_value):
    gain, own = 1.0, jax.random.fold_in(rng, 6)
    for axis_at, shards_of in split:
        heights = jnp.exp(jax.random.uniform(jax.random.fold_in(own, axis_at), (shards_of,), jnp.float32, smallest / len(split), top_value / len(split)))
        gain = gain * jnp.repeat(heights, shape[axis_at] // shards_of).reshape([-1 if axis == axis_at else 1 for axis in range(len(shape))])
    return gain


def gaussian(stream_key, dims, scale, bound, shards=(), held_as=jnp.bfloat16):
    values = scale * jax.random.normal(stream_key, dims, jnp.float32)
    if shards:
        values = values * level_of(stream_key, dims, shards, -0.22, 0.18)
    return jnp.clip(values, -bound, bound).astype(held_as)


def setup_inputs(seed: int = 0) -> dict:
    streams_of = jax.random.split(jax.random.key(seed), 23)
    hidden = gaussian(streams_of[0], (TOKENS, D), 1.0, 6.0, ((0, 32),))
    skip_rows = gaussian(streams_of[1], (TOKENS, D), 1.0, 6.0, ((0, 32),))
    timestep = gaussian(streams_of[2], (IMAGES, D), 1.0, 6.0, ((0, 16),))
    text = gaussian(streams_of[3], (TEXT_ROWS, TD), 1.0, 6.0, ((0, 16),))
    grid_pos = draw_grid_pos(jax.random.fold_in(streams_of[22], 71), 0)
    cotangent = gaussian(streams_of[5], (TOKENS, D), 1.0, 6.0, ((0, 32),))
    skip_weight = gaussian(streams_of[6], (2 * D, D), (2 * D) ** -0.5, 0.109375, ((0, 32),), jnp.float32)
    shift_weight = gaussian(streams_of[7], (D, D), D ** -0.5, 0.15625, ((0, 32),), jnp.float32)
    qkv_weight = gaussian(streams_of[8], (D, 3, D), D ** -0.5, 0.15625, ((0, 16), (2, 2)), jnp.float32)
    cross_query = gaussian(streams_of[9], (D, D), D ** -0.5, 0.15625, ((0, 16), (1, 2)), jnp.float32)
    cross_kv = gaussian(streams_of[10], (TD, 2, D), TD ** -0.5, 0.1875, ((0, 16), (2, 2)), jnp.float32)
    out_weight = gaussian(streams_of[11], (2, D, D), (max(D // 192, 2)) ** -0.5, 2.0, ((1, 2), (2, 16)), jnp.float32)
    up_weight = gaussian(streams_of[12], (D, FF), D ** -0.5, 0.15625, ((0, 16), (1, 2)), jnp.float32)
    down_weight = gaussian(streams_of[13], (FF, D), FF ** -0.5, 0.078125, ((0, 2), (1, 16)), jnp.float32)
    column_bias = gaussian(streams_of[14], (6, N_TP, D // N_TP), 0.3, 2.0, ((1, 2), (2, 16)), jnp.float32)
    up_bias = gaussian(streams_of[15], (N_TP, FF // N_TP), 0.3, 2.0, ((0, 2), (1, 16)), jnp.float32)
    skip_gain = jnp.clip(1.0 + 0.1 * jax.random.normal(streams_of[16], (2 * D,), jnp.float32), 0.5, 1.5)
    skip_bias = gaussian(streams_of[17], (2 * D,), 0.3, 2.0, ((0, 32),), jnp.float32)
    norm_gains = jnp.clip(1.0 + 0.1 * jax.random.normal(streams_of[18], (3, D), jnp.float32), 0.5, 1.5)
    row_biases = gaussian(streams_of[19], (8, D), 0.3, 2.0, ((1, 32),), jnp.float32)
    head_gains = jnp.clip(1.0 + 0.1 * jax.random.normal(streams_of[20], (4, HEAD_DIM), jnp.float32), 0.5, 1.5)
    head_biases = gaussian(streams_of[21], (4, HEAD_DIM), 0.3, 2.0, (), jnp.float32)
    return dict(hidden=hidden, skip_rows=skip_rows, timestep=timestep, text=text, grid_pos=grid_pos, cotangent=cotangent, skip_weight=skip_weight, shift_weight=shift_weight, qkv_weight=qkv_weight, cross_query=cross_query, cross_kv=cross_kv, out_weight=out_weight, up_weight=up_weight, down_weight=down_weight, column_bias=column_bias, up_bias=up_bias, skip_gain=skip_gain, skip_bias=skip_bias, norm_gains=norm_gains, row_biases=row_biases, head_gains=head_gains, head_biases=head_biases)


@jax.custom_vjp
def low(v):
    return lax.optimization_barrier(v.astype(jnp.bfloat16)).astype(jnp.float32)

@jax.custom_vjp
def low_back(v):
    return v

def low_keep(v):
    return (low(v), None)

def low_pass(kept, grad):
    return (grad,)

def back_keep(v):
    return (v, None)

def back_low(kept, grad):
    return (low(grad),)
low.defvjp(low_keep, low_pass)
low_back.defvjp(back_keep, back_low)
EPS_NORM = 1e-06
PRECISE = lax.Precision.HIGHEST

def layer_norm(values, scales, offsets):
    center = values - lax.optimization_barrier(jnp.mean(values, axis=-1, keepdims=True))
    spread = lax.optimization_barrier(jnp.mean(center * center, axis=-1, keepdims=True))
    return center * lax.rsqrt(spread + EPS_NORM) * scales + offsets

def head_norm(values, scales, offsets):
    row_count = values.shape[0]
    shaped = values.reshape(row_count, -1, HEAD_DIM)
    return layer_norm(shaped, scales, offsets).reshape(row_count, -1)

def rotary_tables(positions):
    quarter = HEAD_DIM // 4
    freqs = 10000.0 ** (-jnp.arange(quarter).astype(jnp.float32) / quarter)
    coords = positions.astype(jnp.float32)
    angles = jnp.concatenate([coords[:, 0:1] * freqs, coords[:, 1:2] * freqs], axis=1)
    angles = jnp.repeat(angles, 2, axis=1)
    return (jnp.cos(angles), jnp.sin(angles))

def rotate(values, cosine, sine):
    row_count = values.shape[0]
    head_count = values.shape[1] // HEAD_DIM
    paired = values.reshape(row_count, -1, 2)
    turned = jnp.stack([-paired[:, :, 1], paired[:, :, 0]], axis=2).reshape(row_count, -1)
    return values * jnp.tile(cosine, (1, head_count)) + turned * jnp.tile(sine, (1, head_count))

def gelu_tanh(values):
    return jax.nn.gelu(values, approximate=True)

def matmul(first_operand, second_operand):
    return jnp.dot(first_operand, second_operand, precision=PRECISE)

def attend(queries, keys, values):
    row_count = queries.shape[0]
    key_count = keys.shape[0]
    head_count = queries.shape[1] // HEAD_DIM
    block_rows = min(512, row_count)
    keys_heads = keys.reshape(key_count, head_count, HEAD_DIM)
    values_heads = values.reshape(key_count, head_count, HEAD_DIM)
    scaling = HEAD_DIM ** (-0.5)

    def one_block(query_block):
        query_heads = query_block.reshape(block_rows, head_count, HEAD_DIM)
        scores = low_back(jnp.einsum('qhd,khd->hqk', query_heads, keys_heads, precision=PRECISE) * scaling)
        shifted = scores - lax.optimization_barrier(jnp.max(scores, axis=-1, keepdims=True))
        exponent = jnp.exp(shifted)
        chances = exponent / lax.optimization_barrier(jnp.sum(exponent, axis=-1, keepdims=True))
        mixture = jnp.einsum('hqk,khd->qhd', low(chances), values_heads, precision=PRECISE)
        return mixture.reshape(block_rows, head_count * HEAD_DIM)
    blocks = queries.reshape(row_count // block_rows, block_rows, -1)
    return lax.map(jax.checkpoint(one_block), blocks).reshape(row_count, -1)

def block_forward(params, hidden_img, skip_img, text_img, time_row, positions):
    skip_weight, shift_weight, qkv_weight, cross_query, cross_kv, out_weight, up_weight, down_weight, column_bias, up_bias, skip_gain, skip_bias, norm_gains, row_biases, head_gains, head_biases = params
    skip_w = low(skip_weight)
    shift_w = low(shift_weight)
    qkv_w = low(qkv_weight).reshape(D, 3 * D)
    query_w = low(cross_query)
    pair_w = low(cross_kv).reshape(TD, 2 * D)
    proj_w = low(out_weight)
    up_w = low(up_weight)
    down_w = low(down_weight)
    col_b = low(column_bias).reshape(6, D)
    up_b = low(up_bias).reshape(FF)
    sgain = low(skip_gain)
    sbias = low(skip_bias)
    ngain = low(norm_gains)
    rbias = low(row_biases)
    joined = jnp.concatenate([hidden_img, skip_img], axis=1)
    normed_skip = low(layer_norm(joined, sgain, sbias))
    stream = low_back(matmul(normed_skip, skip_w)) + rbias[6]
    activated = low(jax.nn.silu(time_row))
    shift_row = matmul(activated, shift_w) + rbias[7]
    first_in = low(layer_norm(stream, ngain[0], rbias[0]) + shift_row)
    projected = low_back(matmul(first_in, qkv_w) + col_b[0:3].reshape(-1))
    cosine, sine = rotary_tables(positions)
    queries = low(rotate(head_norm(projected[:, :D], head_gains[0], head_biases[0]), cosine, sine))
    keys = low(rotate(head_norm(projected[:, D:2 * D], head_gains[1], head_biases[1]), cosine, sine))
    values = low(projected[:, 2 * D:])
    mixture = low(low_back(attend(queries, keys, values)))
    stream = stream + low_back(matmul(mixture, proj_w[0])) + rbias[3]
    second_in = low(layer_norm(stream, ngain[1], rbias[1]))
    cross_pre = low_back(matmul(second_in, query_w) + col_b[3])
    pair_pre = low_back(matmul(text_img, pair_w) + col_b[4:6].reshape(-1))
    cross_queries = low(rotate(head_norm(cross_pre, head_gains[2], head_biases[2]), cosine, sine))
    cross_keys = low(head_norm(pair_pre[:, :D], head_gains[3], head_biases[3]))
    cross_values = low(pair_pre[:, D:])
    cross_mixture = low(low_back(attend(cross_queries, cross_keys, cross_values)))
    stream = stream + low_back(matmul(cross_mixture, proj_w[1])) + rbias[4]
    third_in = low(layer_norm(stream, ngain[2], rbias[2]))
    hidden_pre = low_back(matmul(third_in, up_w) + up_b)
    hidden_act = low(gelu_tanh(hidden_pre))
    return stream + low_back(matmul(hidden_act, down_w)) + rbias[5]

def reference(hidden, skip_rows, timestep, text, grid_pos, cotangent, skip_weight, shift_weight, qkv_weight, cross_query, cross_kv, out_weight, up_weight, down_weight, column_bias, up_bias, skip_gain, skip_bias, norm_gains, row_biases, head_gains, head_biases):
    params = (skip_weight, shift_weight, qkv_weight, cross_query, cross_kv, out_weight, up_weight, down_weight, column_bias, up_bias, skip_gain, skip_bias, norm_gains, row_biases, head_gains, head_biases)
    zero_grads = jax.tree.map(jnp.zeros_like, params)

    def per_image(carry, image_index):
        token_start = (image_index * SEQ).astype(jnp.int32)
        text_start = (image_index * TXT).astype(jnp.int32)
        hidden_img = lax.dynamic_slice_in_dim(hidden, token_start, SEQ, 0).astype(jnp.float32)
        skip_img = lax.dynamic_slice_in_dim(skip_rows, token_start, SEQ, 0).astype(jnp.float32)
        cot_img = lax.dynamic_slice_in_dim(cotangent, token_start, SEQ, 0).astype(jnp.float32)
        text_img = lax.dynamic_slice_in_dim(text, text_start, TXT, 0).astype(jnp.float32)
        time_row = lax.dynamic_slice_in_dim(timestep, image_index.astype(jnp.int32), 1, 0).astype(jnp.float32)
        positions = lax.dynamic_slice_in_dim(grid_pos, token_start, SEQ, 0)

        def forward(params_in, hidden_in, skip_in, text_in):
            return block_forward(params_in, hidden_in, skip_in, text_in, time_row, positions)
        result, pullback = jax.vjp(forward, params, hidden_img, skip_img, text_img)
        param_grads, hidden_grads, skip_grads, text_grads = pullback(cot_img)
        carry = jax.tree.map(lambda total, extra: total + extra, carry, param_grads)
        return (carry, (result.astype(jnp.bfloat16), hidden_grads, skip_grads, text_grads))
    totals, stacked = lax.scan(per_image, zero_grads, jnp.arange(IMAGES, dtype=jnp.int32))
    output = stacked[0].reshape(TOKENS, D)
    input_grad = stacked[1].reshape(TOKENS, D)
    skip_grad = stacked[2].reshape(TOKENS, D)
    text_grad = stacked[3].reshape(TEXT_ROWS, TD)
    return (output, input_grad, skip_grad, text_grad, totals[0], totals[1], totals[2], totals[3], totals[4], totals[5], totals[6], totals[7], totals[8], totals[9], totals[10], totals[11], totals[12], totals[13], totals[14], totals[15])
```

```python
import jax
import jax.numpy as jnp
import numpy as np
from jax import lax
from jax.experimental import pallas as pl
from jax.experimental.pallas import tpu as pltpu
from jax.sharding import PartitionSpec as P

HEAD_DIM = 88
SEQ = 1024
EPS_NORM = 1e-06
PRECISE = lax.Precision.HIGHEST
BF = jnp.bfloat16
F32 = jnp.float32


def hop(values, mask):
    count = lax.axis_size("fsdp")
    return lax.ppermute(values, "fsdp", [(i, i ^ mask) for i in range(count)])


def swap(values):
    return lax.ppermute(values, "tp", [(0, 1), (1, 0)])


def far_masks(count):
    return [4 * j for j in range(1, count // 4)]


def natural_masks(count):
    return np.array([(p // (count // 4) % 2) + 2 * (p // (count // 2)) + 4 * (p % (count // 4)) for p in range(count)])


def order_from_masks(values, masks):
    place = np.argsort(masks)
    table = jnp.asarray(place, jnp.int32)
    count = len(masks)
    wanted = jnp.arange(count, dtype=jnp.int32) ^ lax.axis_index("fsdp")
    return jnp.take(values, jnp.take(table, wanted), axis=0)


def gather_small(values):
    count = lax.axis_size("fsdp")
    parts = [values] + [hop(values, m) for m in far_masks(count)]
    held = jnp.stack(parts, axis=0)
    held = jnp.concatenate([held, hop(held, 1)], axis=0)
    held = jnp.concatenate([held, hop(held, 2)], axis=0)
    return order_from_masks(held, natural_masks(count))


def reduce_small(blocks):
    count = blocks.shape[0]
    masks = jnp.asarray(natural_masks(count), jnp.int32)
    held = jnp.take(blocks, masks ^ lax.axis_index("fsdp"), axis=0)
    half = count // 2
    held = held[:half] + hop(held[half:], 2)
    quarter = count // 4
    held = held[:quarter] + hop(held[quarter:], 1)
    total = held[0]
    for j, m in enumerate(far_masks(count)):
        total = total + hop(held[j + 1], m)
    return total


def xor_split(blocks, order, me):
    count, rows, columns = blocks.shape
    quarter = count // 4
    first, second = order

    def kernel(me_ref, keep_in, send_in, keep_out, send_out):
        keep_out[...] = keep_in[...]
        send_out[...] = send_in[...]

    def mask_of(p):
        return ((p // quarter) << second) + 4 * (p % quarter)

    block = (1, rows, columns)
    return pl.pallas_call(
        kernel,
        grid_spec=pltpu.PrefetchScalarGridSpec(
            num_scalar_prefetch=1,
            grid=(count // 2,),
            in_specs=[
                pl.BlockSpec(block, lambda p, me: (me[0] ^ mask_of(p), 0, 0)),
                pl.BlockSpec(block, lambda p, me: (me[0] ^ (mask_of(p) + (1 << first)), 0, 0)),
            ],
            out_specs=[pl.BlockSpec(block, lambda p, me: (p, 0, 0))] * 2,
        ),
        out_shape=[jax.ShapeDtypeStruct((count // 2, rows, columns), blocks.dtype)] * 2,
        cost_estimate=pl.CostEstimate(flops=0, bytes_accessed=4 * blocks.size, transcendentals=0),
    )(me, blocks, blocks)


def pair_split(blocks, order, me):
    count = blocks.shape[0] // 2
    rows, columns = blocks.shape[1:]
    quarter = count // 4
    first, second = order

    def kernel(me_ref, own_in, other_in, own_out, other_out):
        own_out[...] = own_in[...]
        other_out[...] = other_in[...]

    def mask_of(p):
        return ((p // (2 * quarter)) << first) + ((p // quarter % 2) << second) + 4 * (p % quarter)

    block = (1, rows, columns)
    return pl.pallas_call(
        kernel,
        grid_spec=pltpu.PrefetchScalarGridSpec(
            num_scalar_prefetch=1,
            grid=(count,),
            in_specs=[
                pl.BlockSpec(block, lambda p, me: (2 * (me[0] ^ mask_of(p)) + me[1], 0, 0)),
                pl.BlockSpec(block, lambda p, me: (2 * (me[0] ^ mask_of(p)) + me[2], 0, 0)),
            ],
            out_specs=[pl.BlockSpec(block, lambda p, me: (p, 0, 0))] * 2,
        ),
        out_shape=[jax.ShapeDtypeStruct((count, rows, columns), blocks.dtype)] * 2,
        cost_estimate=pl.CostEstimate(flops=0, bytes_accessed=4 * blocks.size, transcendentals=0),
    )(me, blocks, blocks)


def plus(first, second):
    return (first.astype(F32) + second.astype(F32)).astype(BF)


def near_stages(keep, send, first, second):
    quarter = keep.shape[0] // 2
    received = hop(send, 1 << first)
    sent = plus(keep[quarter:], received[quarter:])
    kept = plus(keep[:quarter], received[:quarter])
    return kept, hop(sent, 1 << second)


def far_stage(pairs, count):
    totals = [kept[0].astype(F32) + received[0].astype(F32) for kept, received in pairs]
    for j, m in enumerate(far_masks(count)):
        sent = [plus(kept[j + 1], received[j + 1]) for kept, received in pairs]
        same = all(s.shape[0] == sent[0].shape[0] for s in sent)
        if same:
            got = hop(jnp.concatenate(sent, axis=-1), m)
            edges = np.cumsum([s.shape[-1] for s in sent])[:-1].tolist()
            got = jnp.split(got, edges, axis=-1)
        else:
            got = [hop(s, m) for s in sent]
        totals = [total + g.astype(F32) for total, g in zip(totals, got)]
    return totals


def reduce_pair(first_blocks, second_blocks, me):
    count = first_blocks.shape[0]
    pairs = []
    for blocks, order in ((first_blocks, (0, 1)), (second_blocks, (1, 0))):
        keep, send = xor_split(blocks, order, me)
        pairs.append(near_stages(keep, send, *order))
    return far_stage(pairs, count)


def cut_of(width):
    return 128 * ((width // 128 + 1) // 2)


def reduce_product(left, right, me):
    count = lax.axis_size("fsdp")
    cut = cut_of(right.shape[1])
    parts = [dot_first(left, v).astype(BF) for v in (right[:, :cut], right[:, cut:])]
    parts = [v.reshape(count, -1, v.shape[1]) for v in parts]
    return jnp.concatenate(reduce_pair(parts[0], parts[1], me), axis=-1)


def reduce_product_all(left, right, me):
    count = lax.axis_size("fsdp")
    cut = cut_of(right.shape[1])
    half = count // 2
    pairs = []
    for part, order in ((right[:, :cut], (0, 1)), (right[:, cut:], (1, 0))):
        grad = dot_first(left, part).astype(BF)
        own, other = pair_split(grad.reshape(2 * count, -1, grad.shape[1]), order, me)
        got = swap(other)
        pairs.append(near_stages(plus(own[:half], got[:half]), plus(own[half:], got[half:]), *order))
    return jnp.concatenate(far_stage(pairs, count), axis=-1)


def layer_norm(values, scales, offsets):
    center = values - jnp.mean(values, axis=-1, keepdims=True)
    spread = jnp.mean(center * center, axis=-1, keepdims=True)
    return center * lax.rsqrt(spread + EPS_NORM) * scales + offsets


def head_norm(values, scales, offsets):
    row_count = values.shape[0]
    shaped = values.reshape(row_count, -1, HEAD_DIM)
    return layer_norm(shaped, scales, offsets).reshape(row_count, -1)


def rotary_tables(positions):
    quarter = HEAD_DIM // 4
    freqs = 10000.0 ** (-jnp.arange(quarter).astype(F32) / quarter)
    coords = positions.astype(F32)
    angles = jnp.concatenate([coords[:, 0:1] * freqs, coords[:, 1:2] * freqs], axis=1)
    angles = jnp.repeat(angles, 2, axis=1)
    return (jnp.cos(angles), jnp.sin(angles))


def rotate(values, cosine, sine):
    row_count = values.shape[0]
    head_count = values.shape[1] // HEAD_DIM
    paired = values.reshape(row_count, -1, 2)
    turned = jnp.stack([-paired[:, :, 1], paired[:, :, 0]], axis=2).reshape(row_count, -1)
    return values * jnp.tile(cosine, (1, head_count)) + turned * jnp.tile(sine, (1, head_count))


def plain_dot(first_operand, second_operand):
    return jnp.dot(first_operand, second_operand, preferred_element_type=F32)


def dot_first(first_operand, second_operand):
    return lax.dot_general(first_operand, second_operand, (((0,), (0,)), ((), ())), preferred_element_type=F32)


def dot_last(first_operand, second_operand):
    return lax.dot_general(first_operand, second_operand, (((1,), (1,)), ((), ())), preferred_element_type=F32)


def norm_parts(values):
    center = values - jnp.mean(values, axis=-1, keepdims=True)
    spread = jnp.mean(center * center, axis=-1, keepdims=True)
    inverse = lax.rsqrt(spread + EPS_NORM)
    return center * inverse, inverse


def norm_backward(grad, values, scales):
    normed, inverse = norm_parts(values)
    scaled = grad * scales
    result = inverse * (
        scaled
        - jnp.mean(scaled, axis=-1, keepdims=True)
        - normed * jnp.mean(scaled * normed, axis=-1, keepdims=True)
    )
    return result, jnp.sum(grad * normed, axis=0), jnp.sum(grad, axis=0)


def split_heads(values, image_count):
    return values.reshape(image_count, values.shape[0] // image_count, -1, HEAD_DIM)


def attention_forward(queries, keys, values, image_count):
    query_heads = split_heads(queries, image_count)
    key_heads = split_heads(keys, image_count)
    value_heads = split_heads(values, image_count)
    query_len = query_heads.shape[1]
    block_rows = min(512, query_len)
    scaling = HEAD_DIM ** (-0.5)
    outputs = []
    totals = []
    for offset_row in range(0, query_len, block_rows):
        query_piece = query_heads[:, offset_row : offset_row + block_rows]
        scores = jnp.einsum("iqhd,ikhd->ihqk", query_piece, key_heads, preferred_element_type=F32) * scaling
        row_peak = jnp.max(scores, axis=-1, keepdims=True)
        exponent = jnp.exp(scores - row_peak)
        summed = jnp.sum(exponent, axis=-1, keepdims=True)
        chances = exponent / summed
        outputs.append(jnp.einsum("ihqk,ikhd->iqhd", chances.astype(BF), value_heads, preferred_element_type=F32))
        totals.append(row_peak + jnp.log(summed))
    mixture = jnp.concatenate(outputs, axis=1).reshape(queries.shape[0], -1)
    return (mixture, totals)


def attention_backward(grad_mix, queries, keys, values, totals, image_count):
    query_heads = split_heads(queries, image_count)
    key_heads = split_heads(keys, image_count)
    value_heads = split_heads(values, image_count)
    grad_heads = split_heads(grad_mix, image_count)
    query_len = query_heads.shape[1]
    block_rows = min(512, query_len)
    scaling = HEAD_DIM ** (-0.5)
    grad_keys = jnp.zeros(key_heads.shape, F32)
    grad_values = jnp.zeros(value_heads.shape, F32)
    grad_queries = []
    for index_blk, offset_row in enumerate(range(0, query_len, block_rows)):
        query_piece = query_heads[:, offset_row : offset_row + block_rows]
        grad_piece = grad_heads[:, offset_row : offset_row + block_rows]
        scores = jnp.einsum("iqhd,ikhd->ihqk", query_piece, key_heads, preferred_element_type=F32) * scaling
        chances = jnp.exp(scores - totals[index_blk])
        grad_values = grad_values + jnp.einsum(
            "ihqk,iqhd->ikhd", chances.astype(BF), grad_piece, preferred_element_type=F32
        )
        grad_chance = jnp.einsum("iqhd,ikhd->ihqk", grad_piece, value_heads, preferred_element_type=F32)
        grad_score = chances * (grad_chance - jnp.sum(grad_chance * chances, axis=-1, keepdims=True))
        grad_low = grad_score.astype(BF)
        grad_queries.append(jnp.einsum("ihqk,ikhd->iqhd", grad_low, key_heads, preferred_element_type=F32) * scaling)
        grad_keys = (
            grad_keys + jnp.einsum("ihqk,iqhd->ikhd", grad_low, query_piece, preferred_element_type=F32) * scaling
        )
    query_grad = jnp.concatenate(grad_queries, axis=1).reshape(queries.shape[0], -1)
    return (query_grad, grad_keys.reshape(keys.shape[0], -1), grad_values.reshape(values.shape[0], -1))


def with_other(values):
    return jnp.concatenate([values, swap(values)], axis=0)


def branch_sum(operand, product, rows_local):
    sent = swap(product(operand[rows_local:]).astype(BF))
    return product(operand[:rows_local]) + sent.astype(F32)


def body(
    hidden,
    skip_rows,
    timestep,
    text,
    grid_pos,
    cotangent,
    skip_weight,
    shift_weight,
    qkv_weight,
    cross_query,
    cross_kv,
    out_weight,
    up_weight,
    down_weight,
    column_bias,
    up_bias,
    skip_gain,
    skip_bias,
    norm_gains,
    row_biases,
    head_gains,
    head_biases,
):
    count = lax.axis_size("fsdp")
    f_index = lax.axis_index("fsdp")
    t_index = lax.axis_index("tp")
    me = jnp.stack([f_index, t_index, 1 - t_index]).astype(jnp.int32)
    rows_local, model_width = hidden.shape
    image_count = timestep.shape[0]
    shard_rows = cross_query.shape[0]
    local_width = cross_query.shape[1]
    ff_local = up_weight.shape[1]
    text_width = cross_kv.shape[0] * count
    own_images = max(image_count // 2, 1)
    first_image = t_index * (image_count // 2)

    activated_own = jax.nn.silu(timestep.astype(F32)).astype(BF)
    small_parts = [column_bias, up_bias, skip_gain, skip_bias, norm_gains, row_biases]
    small = jnp.concatenate([p.astype(BF).reshape(-1) for p in small_parts] + [activated_own.reshape(-1)])
    small_own = gather_small(small)
    small_other = swap(small_own)
    first_is_own = t_index == 0
    small_both = jnp.stack(
        [jnp.where(first_is_own, small_own, small_other), jnp.where(first_is_own, small_other, small_own)], axis=1
    )
    edges = np.cumsum([0] + [p.size for p in small_parts])
    own_f = small_own.astype(F32)
    both_f = small_both.astype(F32)
    column_slice = column_bias.shape[2]
    col_bf = (
        own_f[:, edges[0] : edges[1]].reshape(count, 6, column_slice).transpose(1, 0, 2).reshape(6, local_width)
    )
    up_bf = own_f[:, edges[1] : edges[2]].reshape(-1)
    sgain_f = both_f[:, :, edges[2] : edges[3]].reshape(-1)
    sbias_f = both_f[:, :, edges[3] : edges[4]].reshape(-1)
    ngain_f = both_f[:, :, edges[4] : edges[5]].reshape(count, 2, 3, -1).transpose(2, 0, 1, 3).reshape(3, model_width)
    rbias_f = both_f[:, :, edges[5] : edges[6]].reshape(count, 2, 8, -1).transpose(2, 0, 1, 3).reshape(8, model_width)
    activated = small_own[:, edges[6] :].reshape(count * image_count, model_width)

    skip_w = lax.all_gather(skip_weight.astype(BF), ("fsdp", "tp"), axis=0, tiled=True)
    qkv_w = lax.all_gather(qkv_weight.astype(BF).reshape(shard_rows, -1), "fsdp", axis=0, tiled=True)
    out_t = out_weight.astype(BF).transpose(2, 0, 1).reshape(shard_rows, -1)
    proj_t = lax.all_gather(out_t, "fsdp", axis=0, tiled=True)
    self_t = proj_t[:, :local_width]
    cross_t = proj_t[:, local_width:]
    pair_w = lax.all_gather(cross_kv.astype(BF).reshape(cross_kv.shape[0], -1), "fsdp", axis=0, tiled=True)
    query_w = lax.all_gather(cross_query.astype(BF), "fsdp", axis=0, tiled=True)
    up_w = lax.all_gather(up_weight.astype(BF), "fsdp", axis=0, tiled=True)
    down_t = lax.all_gather(down_weight.astype(BF).T, "fsdp", axis=0, tiled=True)

    device_index = f_index * 2 + t_index
    shift_rows = shift_weight.shape[0]
    activated_cut = lax.dynamic_slice_in_dim(activated, device_index * shift_rows, shift_rows, 1)
    shift_term = plain_dot(activated_cut, shift_weight.astype(BF))
    shift_term = shift_term + swap(shift_term)
    shift_image = reduce_small(shift_term.reshape(count, -1)).reshape(image_count, model_width) + rbias_f[7]
    shift_own = lax.dynamic_slice_in_dim(shift_image, first_image, own_images, 0)
    shift_tokens = jnp.repeat(shift_own, rows_local // own_images, axis=0)

    text_shift = first_image

    def roll_images(values, shift):
        if image_count == 1:
            return values
        shaped = values.reshape(image_count, -1, values.shape[-1])
        return jnp.roll(shaped, shift, axis=0).reshape(values.shape)

    text_in = roll_images(text, -text_shift)
    pos_own = lax.dynamic_slice_in_dim(grid_pos, t_index * rows_local, rows_local, 0)
    pos_other = lax.dynamic_slice_in_dim(grid_pos, (1 - t_index) * rows_local, rows_local, 0)
    positions = jnp.concatenate([pos_own, pos_other], axis=0)

    joined = jnp.concatenate([hidden, skip_rows], axis=1).astype(F32)
    normed_skip = layer_norm(joined, sgain_f, sbias_f).astype(BF)
    stream_zero = plain_dot(normed_skip, skip_w) + rbias_f[6]
    first_in = with_other((layer_norm(stream_zero, ngain_f[0], rbias_f[0]) + shift_tokens).astype(BF))
    grad_ffn = with_other(cotangent)
    projected = plain_dot(first_in, qkv_w) + col_bf[0:3].reshape(-1)
    cosine, sine = rotary_tables(positions)

    def rotary_prep(values, scales, offsets):
        return rotate(head_norm(values, scales, offsets), cosine, sine)

    queries_f, query_pull = jax.vjp(rotary_prep, projected[:, :local_width], head_gains[0], head_biases[0])
    keys_f, key_pull = jax.vjp(
        rotary_prep, projected[:, local_width : 2 * local_width], head_gains[1], head_biases[1]
    )
    queries = queries_f.astype(BF)
    keys = keys_f.astype(BF)
    values = projected[:, 2 * local_width :].astype(BF)
    mixture_f, self_totals = attention_forward(queries, keys, values, image_count)
    mixture = mixture_f.astype(BF)
    stream_one = stream_zero + branch_sum(mixture, lambda v: dot_last(v, self_t), rows_local) + rbias_f[3]
    second_in = with_other(layer_norm(stream_one, ngain_f[1], rbias_f[1]).astype(BF))
    cross_pre = plain_dot(second_in, query_w) + col_bf[3].reshape(-1)
    pair_pre = plain_dot(text_in, pair_w) + col_bf[4:6].reshape(-1)
    cross_q_f, cross_q_pull = jax.vjp(rotary_prep, cross_pre, head_gains[2], head_biases[2])
    cross_k_f, cross_k_pull = jax.vjp(head_norm, pair_pre[:, :local_width], head_gains[3], head_biases[3])
    cross_queries = cross_q_f.astype(BF)
    cross_keys = cross_k_f.astype(BF)
    cross_values = pair_pre[:, local_width:].astype(BF)
    cross_mix_f, cross_totals = attention_forward(cross_queries, cross_keys, cross_values, image_count)
    cross_mixture = cross_mix_f.astype(BF)
    stream_two = stream_one + branch_sum(cross_mixture, lambda v: dot_last(v, cross_t), rows_local) + rbias_f[4]
    third_in = with_other(layer_norm(stream_two, ngain_f[2], rbias_f[2]).astype(BF))
    hidden_pre = plain_dot(third_in, up_w) + up_bf

    def gelu_tanh(v):
        return jax.nn.gelu(v, approximate=True)

    gelu_f, gelu_pull = jax.vjp(gelu_tanh, hidden_pre)
    hidden_act = gelu_f.astype(BF)
    stream_three = stream_two + branch_sum(hidden_act, lambda v: dot_last(v, down_t), rows_local) + rbias_f[5]
    output = stream_three.astype(BF)

    def blocks_of(grad):
        return grad.reshape(count, -1, grad.shape[-1])

    grad_three = cotangent.astype(F32)
    sent_down = reduce_product(grad_ffn, hidden_act, me).T
    grad_act = plain_dot(grad_ffn, down_t)
    grad_pre = gelu_pull(grad_act)[0].astype(BF)
    grad_upb = jnp.sum(grad_pre, axis=0, dtype=F32)
    grad_third = branch_sum(grad_pre, lambda v: dot_last(v, up_w), rows_local)
    sent_up = reduce_product(third_in, grad_pre, me)
    stream_grad, third_gain, third_bias = norm_backward(grad_third, stream_two, ngain_f[2])
    grad_two = grad_three + stream_grad
    grad_cross = with_other(grad_two.astype(BF))
    grad_cmix = plain_dot(grad_cross, cross_t).astype(BF)
    grad_cproj = dot_first(grad_cross, cross_mixture).astype(BF)
    cq_grad, ck_grad, cv_grad = attention_backward(
        grad_cmix, cross_queries, cross_keys, cross_values, cross_totals, image_count
    )
    cross_pre_grad, head_gain_two, head_bias_two = cross_q_pull(cq_grad)
    cross_key_grad, head_gain_three, head_bias_three = cross_k_pull(ck_grad)
    grad_cq = cross_pre_grad.astype(BF)
    grad_ck = cross_key_grad.astype(BF)
    grad_cv = cv_grad.astype(BF)
    grad_pair = jnp.concatenate([grad_ck, grad_cv], axis=1)
    grad_second = branch_sum(grad_cq, lambda v: dot_last(v, query_w), rows_local)
    grad_query_w = dot_first(second_in, grad_cq).astype(BF)
    sent_cproj, sent_query = reduce_pair(blocks_of(grad_cproj), blocks_of(grad_query_w), me)
    grad_k_w = dot_first(text_in, grad_ck).astype(BF)
    grad_v_w = dot_first(text_in, grad_cv).astype(BF)
    sent_k, sent_v = reduce_pair(blocks_of(grad_k_w), blocks_of(grad_v_w), me)
    text_half = text_width // 2
    pair_own = lax.dynamic_slice_in_dim(pair_w, t_index * text_half, text_half, 0)
    pair_other = lax.dynamic_slice_in_dim(pair_w, (1 - t_index) * text_half, text_half, 0)
    text_grad = dot_last(grad_pair, pair_own) + swap(dot_last(grad_pair, pair_other).astype(BF)).astype(F32)
    text_grad = roll_images(text_grad, text_shift)
    stream_grad, second_gain, second_bias = norm_backward(grad_second, stream_one, ngain_f[1])
    grad_one = grad_two + stream_grad
    grad_self = with_other(grad_one.astype(BF))
    grad_mix = plain_dot(grad_self, self_t).astype(BF)
    grad_sproj = dot_first(grad_self, mixture).astype(BF)
    query_grad, key_grad, value_grad = attention_backward(grad_mix, queries, keys, values, self_totals, image_count)
    query_pre_grad, head_gain_zero, head_bias_zero = query_pull(query_grad)
    key_pre_grad, head_gain_one, head_bias_one = key_pull(key_grad)
    grad_q = query_pre_grad.astype(BF)
    grad_k = key_pre_grad.astype(BF)
    grad_v = value_grad.astype(BF)
    grad_qkv = jnp.concatenate([grad_q, grad_k, grad_v], axis=1)
    grad_first = branch_sum(grad_qkv, lambda v: dot_last(v, qkv_w), rows_local)
    grad_wv = dot_first(first_in, grad_v).astype(BF)
    grad_wq = dot_first(first_in, grad_q).astype(BF)
    grad_wk = dot_first(first_in, grad_k).astype(BF)
    sent_sproj, sent_wv = reduce_pair(blocks_of(grad_sproj), blocks_of(grad_wv), me)
    sent_wq, sent_wk = reduce_pair(blocks_of(grad_wq), blocks_of(grad_wk), me)
    stream_grad, first_gain, first_bias = norm_backward(grad_first, stream_zero, ngain_f[0])
    grad_zero = grad_one + stream_grad
    grad_low_zero = grad_zero.astype(BF)
    sent_skip = reduce_product_all(normed_skip, grad_low_zero, me)
    grad_normed = dot_last(grad_low_zero, skip_w)
    joined_grad, skip_gain_part, skip_bias_part = norm_backward(grad_normed, joined, sgain_f)
    input_grad = joined_grad[:, :model_width]
    skip_grad = joined_grad[:, model_width:]

    shift_sums = jnp.sum(grad_first.reshape(own_images, -1, model_width), axis=1)
    if image_count == 1:
        shift_local = shift_sums
    else:
        shift_local = lax.dynamic_update_slice_in_dim(
            jnp.zeros((image_count, model_width), F32), shift_sums, first_image, 0
        )
    shift_local = shift_local + swap(shift_local)
    shift_all = gather_small(shift_local.reshape(-1)).reshape(count * image_count, model_width)
    sent_shift = lax.dot_general(
        activated_cut.astype(F32), shift_all, (((0,), (0,)), ((), ())), precision=PRECISE
    )

    grad_gains = jnp.stack([first_gain, second_gain, third_gain], axis=0)
    grad_biases = jnp.stack(
        [
            first_bias,
            second_bias,
            third_bias,
            jnp.sum(grad_one, axis=0),
            jnp.sum(grad_two, axis=0),
            jnp.sum(grad_three, axis=0),
            jnp.sum(grad_zero, axis=0),
            first_bias,
        ],
        axis=0,
    )
    grad_colb = jnp.concatenate(
        [
            jnp.sum(grad_qkv, axis=0, dtype=F32).reshape(3, local_width),
            jnp.sum(grad_cq, axis=0, dtype=F32).reshape(1, local_width),
            jnp.sum(grad_pair, axis=0, dtype=F32).reshape(2, local_width),
        ],
        axis=0,
    )
    head_part = jnp.concatenate(
        [
            jnp.stack([head_gain_zero, head_gain_one, head_gain_two, head_gain_three], axis=0).reshape(-1),
            jnp.stack([head_bias_zero, head_bias_one, head_bias_two, head_bias_three], axis=0).reshape(-1),
        ]
    )

    def by_device(values):
        shaped = values.reshape(values.shape[0], count, 2, -1).transpose(2, 1, 0, 3)
        return shaped.reshape(2, count, -1)

    shared = jnp.concatenate(
        [
            by_device(skip_gain_part[None]),
            by_device(skip_bias_part[None]),
            by_device(grad_gains),
            by_device(grad_biases),
            jnp.broadcast_to(head_part, (2, count, head_part.shape[0])),
        ],
        axis=-1,
    )
    shared_own = lax.dynamic_index_in_dim(shared, t_index, 0, keepdims=False)
    shared_other = lax.dynamic_index_in_dim(shared, 1 - t_index, 0, keepdims=False)
    shared_sum = shared_own + swap(shared_other)
    colb_blocks = grad_colb.reshape(6, count, -1).transpose(1, 0, 2).reshape(count, -1)
    upb_blocks = grad_upb.reshape(count, -1)
    small_sum = reduce_small(jnp.concatenate([shared_sum, colb_blocks, upb_blocks], axis=-1))
    lengths = [skip_gain.size, skip_bias.size, norm_gains.size, row_biases.size, head_gains.size, head_biases.size]
    lengths += [column_bias.size, up_bias.size]
    cuts = np.cumsum([0] + lengths)
    pieces = [small_sum[cuts[i] : cuts[i + 1]] for i in range(len(lengths))]

    sent_qkv = jnp.stack([sent_wq, sent_wk, sent_wv], axis=1)
    sent_pair = jnp.stack([sent_k, sent_v], axis=1)
    sent_proj = jnp.stack([sent_sproj.T, sent_cproj.T], axis=0)
    return (
        output,
        input_grad,
        skip_grad,
        text_grad,
        sent_skip,
        sent_shift,
        sent_qkv,
        sent_query,
        sent_pair,
        sent_proj,
        sent_up,
        sent_down,
        pieces[6].reshape(column_bias.shape),
        pieces[7].reshape(up_bias.shape),
        pieces[0],
        pieces[1],
        pieces[2].reshape(norm_gains.shape),
        pieces[3].reshape(row_biases.shape),
        pieces[4].reshape(head_gains.shape),
        pieces[5].reshape(head_biases.shape),
    )


def solution(mesh):
    in_specs = (
        P(("fsdp", "tp"), None),
        P(("fsdp", "tp"), None),
        P("fsdp", None),
        P("fsdp", None),
        P("fsdp", None),
        P(("fsdp", "tp"), None),
        P(("fsdp", "tp"), None),
        P(("fsdp", "tp"), None),
        P("fsdp", None, "tp"),
        P("fsdp", "tp"),
        P("fsdp", None, "tp"),
        P(None, "tp", "fsdp"),
        P("fsdp", "tp"),
        P("tp", "fsdp"),
        P(None, "tp", "fsdp"),
        P("tp", "fsdp"),
        P(("fsdp", "tp")),
        P(("fsdp", "tp")),
        P(None, ("fsdp", "tp")),
        P(None, ("fsdp", "tp")),
        P(),
        P(),
    )
    out_specs = (
        P(("fsdp", "tp"), None),
        P(("fsdp", "tp"), None),
        P(("fsdp", "tp"), None),
        P("fsdp", "tp"),
        P(("fsdp", "tp"), None),
        P(("fsdp", "tp"), None),
        P("fsdp", None, "tp"),
        P("fsdp", "tp"),
        P("fsdp", None, "tp"),
        P(None, "tp", "fsdp"),
        P("fsdp", "tp"),
        P("tp", "fsdp"),
        P(None, "tp", "fsdp"),
        P("tp", "fsdp"),
        P(("fsdp", "tp")),
        P(("fsdp", "tp")),
        P(None, ("fsdp", "tp")),
        P(None, ("fsdp", "tp")),
        P(),
        P(),
    )
    return jax.shard_map(body, mesh=mesh, in_specs=in_specs, out_specs=out_specs, check_vma=False)
```

```python
import functools

import jax
import jax.numpy as jnp
import numpy as np
from jax import lax
from jax.experimental import pallas as pl
from jax.experimental.pallas import tpu as pltpu
from jax.sharding import PartitionSpec as P

HEAD_DIM = 88
SEQ = 1024
EPS_NORM = 1e-06
PRECISE = lax.Precision.HIGHEST
BF = jnp.bfloat16
F32 = jnp.float32
LOG2E = 1.4426950408889634
UP_ORDER = (1, 2)
DOWN_ORDER = (4, 2, 1)
VMEM_LIMIT = 56 * 1024 * 1024


def hop(values, mask):
    count = lax.axis_size("fsdp")
    return lax.ppermute(values, "fsdp", [(i, i ^ mask) for i in range(count)])


def swap(values):
    return lax.ppermute(values, "tp", [(0, 1), (1, 0)])


def far_masks(count):
    return [4 * j for j in range(1, count // 4)]


def natural_masks(count):
    return np.array([(p // (count // 4) % 2) + 2 * (p // (count // 2)) + 4 * (p % (count // 4)) for p in range(count)])


def order_from_masks(values, masks):
    place = np.argsort(masks)
    table = jnp.asarray(place, jnp.int32)
    count = len(masks)
    wanted = jnp.arange(count, dtype=jnp.int32) ^ lax.axis_index("fsdp")
    return jnp.take(values, jnp.take(table, wanted), axis=0)


def gather_small(values):
    count = lax.axis_size("fsdp")
    parts = [values] + [hop(values, m) for m in far_masks(count)]
    held = jnp.stack(parts, axis=0)
    held = jnp.concatenate([held, hop(held, 1)], axis=0)
    held = jnp.concatenate([held, hop(held, 2)], axis=0)
    return order_from_masks(held, natural_masks(count))


def reduce_small(blocks):
    count = blocks.shape[0]
    masks = jnp.asarray(natural_masks(count), jnp.int32)
    held = jnp.take(blocks, masks ^ lax.axis_index("fsdp"), axis=0)
    half = count // 2
    held = held[:half] + hop(held[half:], 2)
    quarter = count // 4
    held = held[:quarter] + hop(held[quarter:], 1)
    total = held[0]
    for j, m in enumerate(far_masks(count)):
        total = total + hop(held[j + 1], m)
    return total


ANYWHERE = pl.BlockSpec(memory_space=pl.ANY)


def steps_of(order, count):
    return tuple(order) + tuple(1 << b for b in range(30) if 1 << b < count and 1 << b not in order)


def near_mask(position, order):
    top = len(order) - 1
    return sum(((position >> (top - k)) & 1) * bit for k, bit in enumerate(order))


def place_of(mask, order):
    top = len(order) - 1
    return sum(((mask >> (bit.bit_length() - 1)) & 1) << (top - k) for k, bit in enumerate(order))


def halve(arrays, order, me, after=(), paired=False):
    count = arrays[0].shape[0] // (2 if paired else 1)
    rows, columns = arrays[0].shape[1:]
    order = steps_of(order, count)
    many = len(arrays)
    total = 2 * count if paired else count
    half = total // 2

    def kernel(me_ref, *refs):
        sources = refs[:many]
        low, high, held, in_sems, out_sems = refs[many + len(after) :]
        own = me_ref[0]

        def load(p, k):
            block = own ^ near_mask(p % count, order)
            if paired:
                block = 2 * block + me_ref[1 + p // count]
            return pltpu.make_async_copy(sources[k].at[block], held.at[p, k], in_sems.at[p])

        def store(p):
            target = low if p < half else high
            return pltpu.make_async_copy(held.at[p], target.at[p % half], out_sems.at[p])

        for p in list(range(half, total)) + list(range(half)):
            for k in range(many):
                load(p, k).start()
        for p in list(range(half, total)) + list(range(half)):
            for k in range(many):
                load(p, k).wait()
            store(p).start()
        for p in range(total):
            store(p).wait()

    moved = total * many * rows * columns
    shape = jax.ShapeDtypeStruct((half, many, rows, columns), arrays[0].dtype)
    return pl.pallas_call(
        kernel,
        grid_spec=pltpu.PrefetchScalarGridSpec(
            num_scalar_prefetch=1,
            grid=(1,),
            in_specs=[ANYWHERE] * (many + len(after)),
            out_specs=[ANYWHERE] * 2,
            scratch_shapes=[
                pltpu.VMEM((total, many, rows, columns), arrays[0].dtype),
                pltpu.SemaphoreType.DMA((total,)),
                pltpu.SemaphoreType.DMA((total,)),
            ],
        ),
        out_shape=[shape, shape],
        compiler_params=pltpu.CompilerParams(vmem_limit_bytes=VMEM_LIMIT),
        cost_estimate=pl.CostEstimate(flops=0, bytes_accessed=4 * moved, transcendentals=0),
    )(me, *arrays, *after)


def pin(values, after):
    def kernel(in_ref, *refs):
        refs[-1][...] = in_ref[...]

    whole = pl.BlockSpec(values.shape, lambda: (0,) * values.ndim)
    return pl.pallas_call(
        kernel,
        in_specs=[whole] + [ANYWHERE] * len(after),
        out_specs=whole,
        out_shape=jax.ShapeDtypeStruct(values.shape, values.dtype),
        cost_estimate=pl.CostEstimate(flops=0, bytes_accessed=4 * values.size, transcendentals=0),
    )(values, *after)


def tile_of(columns):
    return columns // 4 if columns % 512 == 0 else columns // 2 if columns % 256 == 0 else columns


def add_near(kept, received, after=(), part=None):
    doubled, many, rows, columns = kept.shape[-4:]
    quarter = doubled // 2
    tile = columns // 2 if columns % 256 == 0 else columns

    def kernel(kept_low, kept_high, got_low, got_high, *refs):
        low, high = refs[len(after) :]
        for out, first, second in ((low, kept_low, got_low), (high, kept_high, got_high)):
            total = first[...].astype(F32) + second[...].astype(F32)
            out[...] = total.reshape(out.shape).astype(kept.dtype)

    block = (1, many, rows, tile)

    def spec(shift):
        if part is None:
            return pl.BlockSpec(block, lambda i, j: (i + shift, 0, 0, j))
        return pl.BlockSpec((1, *block), lambda i, j: (part, i + shift, 0, 0, j))

    out_spec = pl.BlockSpec(block, lambda i, j: (i, 0, 0, j))
    shape = jax.ShapeDtypeStruct((quarter, many, rows, columns), kept.dtype)
    size = doubled * many * rows * columns
    return pl.pallas_call(
        kernel,
        grid=(quarter, columns // tile),
        in_specs=[spec(0), spec(quarter), spec(0), spec(quarter)] + [ANYWHERE] * len(after),
        out_specs=[out_spec] * 2,
        out_shape=[shape, shape],
        compiler_params=pltpu.CompilerParams(vmem_limit_bytes=VMEM_LIMIT),
        cost_estimate=pl.CostEstimate(flops=size, bytes_accessed=6 * size, transcendentals=0),
    )(kept, kept, received, received, *after)


def add_far(pairs, after=()):
    quarter, many, _, columns = pairs[0][0].shape
    heights = [pair[0].shape[2] for pair in pairs]
    rows = max(heights)
    half = quarter // 2
    parts = len(pairs)
    tile = tile_of(columns)
    arrays = [array for pair in pairs for array in pair]
    kind = arrays[0].dtype

    def kernel(*refs):
        outs = refs[2 * parts + len(after) :]
        for j in range(quarter):
            for p in range(parts):
                total = refs[2 * p][j].astype(F32) + refs[2 * p + 1][j].astype(F32)
                if heights[p] < rows:
                    total = jnp.concatenate([total, jnp.zeros((1, rows - heights[p], tile), F32)], axis=1)
                outs[j // half][p, j % half] = total.astype(kind)

    in_specs = [
        pl.BlockSpec((quarter, 1, height, tile), lambda k, i: (0, k, 0, i)) for height in heights for _ in range(2)
    ]
    out_spec = pl.BlockSpec((parts, half, 1, rows, tile), lambda k, i: (0, 0, k, 0, i))
    shape = (parts, half, many, rows, columns)
    size = parts * quarter * many * rows * columns
    return pl.pallas_call(
        kernel,
        grid=(many, columns // tile),
        in_specs=in_specs + [ANYWHERE] * len(after),
        out_specs=[out_spec] * 2,
        out_shape=[jax.ShapeDtypeStruct(shape, kind)] * 2,
        compiler_params=pltpu.CompilerParams(vmem_limit_bytes=VMEM_LIMIT),
        cost_estimate=pl.CostEstimate(flops=size, bytes_accessed=6 * size, transcendentals=0),
    )(*arrays, *after)


def add_halves(kept, received, after=()):
    parts, quarter, many, rows, columns = kept.shape
    half = quarter // 2

    def kernel(kept_ref, got_ref, *refs):
        outs = refs[len(after) :]
        for j in range(quarter):
            total = kept_ref[:, j].astype(F32) + got_ref[:, j].astype(F32)
            outs[j // half][:, j % half] = total.astype(kept.dtype)

    tile = tile_of(columns)
    in_spec = pl.BlockSpec((parts, quarter, 1, rows, tile), lambda k, i: (0, 0, k, 0, i))
    out_spec = pl.BlockSpec((parts, half, 1, rows, tile), lambda k, i: (0, 0, k, 0, i))
    shape = jax.ShapeDtypeStruct((parts, half, many, rows, columns), kept.dtype)
    return pl.pallas_call(
        kernel,
        grid=(many, columns // tile),
        in_specs=[in_spec] * 2 + [ANYWHERE] * len(after),
        out_specs=[out_spec] * 2,
        out_shape=[shape] * 2,
        compiler_params=pltpu.CompilerParams(vmem_limit_bytes=VMEM_LIMIT),
        cost_estimate=pl.CostEstimate(flops=kept.size, bytes_accessed=6 * kept.size, transcendentals=0),
    )(kept, received, *after)


class FarSum:
    def __init__(self, pairs, after=()):
        self.low, self.high = add_far(pairs, after)
        self.mask = 4
        self.got = hop(self.high, self.mask)

    def step(self, after=()):
        self.low, self.high = add_halves(self.low, self.got, after)
        self.mask *= 2
        self.got = hop(self.high, self.mask)

    def total(self):
        while self.low.shape[1] > 1:
            self.step()
        return self.low[:, 0].astype(F32) + self.got[:, 0].astype(F32)


class Chain:
    def __init__(self, halves, order):
        self.order = steps_of(order, lax.axis_size("fsdp"))
        self.low, self.high = halves
        self.at = 0
        self.got = hop(self.high, self.order[0])

    def step(self, after=()):
        self.low, self.high = add_near(self.low, self.got, after)
        self.at += 1
        self.got = hop(self.high, self.order[self.at])

    def total(self):
        while self.low.shape[0] > 1:
            self.step()
        return self.low[0].astype(F32) + self.got[0].astype(F32)


def join(first, second, after=()):
    count = first.shape[0]
    shape = (2 * count, *first.shape[1:])

    def kernel(first_ref, second_ref, *refs):
        out, held, sems = refs[len(after) :]

        def load(k):
            return pltpu.make_async_copy((first_ref, second_ref)[k], held.at[pl.ds(k * count, count)], sems.at[0, k])

        def store(k):
            part = pl.ds(k * count, count)
            return pltpu.make_async_copy(held.at[part], out.at[part], sems.at[1, k])

        for k in range(2):
            load(k).start()
        for k in range(2):
            load(k).wait()
            store(k).start()
        for k in range(2):
            store(k).wait()

    return pl.pallas_call(
        kernel,
        in_specs=[ANYWHERE] * (2 + len(after)),
        out_specs=ANYWHERE,
        out_shape=jax.ShapeDtypeStruct(shape, first.dtype),
        scratch_shapes=[pltpu.VMEM(shape, first.dtype), pltpu.SemaphoreType.DMA((2, 2))],
        compiler_params=pltpu.CompilerParams(vmem_limit_bytes=VMEM_LIMIT),
        cost_estimate=pl.CostEstimate(flops=0, bytes_accessed=8 * first.size, transcendentals=0),
    )(first, second, *after)


def products(groups, me, after=(), paired=False, tile=None):
    devices = lax.axis_size("fsdp")
    total = 2 * devices if paired else devices
    half = total // 2
    lefts, rights = [], []
    plan = []
    for order, terms in groups:
        column = 0
        steps = []
        for left, right, turned, start, width in terms:
            for array, known in ((left, lefts), (right, rights)):
                if not any(array is other for other in known):
                    known.append(array)
            which = [k for k, other in enumerate(lefts) if other is left][0]
            where = [k for k, other in enumerate(rights) if other is right][0]
            steps.append((which, where, turned, start, width, column))
            column += width
        plan.append((steps_of(order, devices), steps, terms[0][0].shape[1], column))

    def kernel(me_ref, *refs):
        left_refs = refs[: len(lefts)]
        right_refs = refs[len(lefts) : len(lefts) + len(rights)]
        rest = refs[len(lefts) + len(rights) + len(after) :]
        outs = rest[: 2 if paired else 2 * len(plan)]
        sums = rest[len(outs)]
        turned_lefts = rest[len(outs) + 1 :]
        own = me_ref[0]

        @pl.when(pl.program_id(0) == 0)
        def _():
            for k, ref in enumerate(left_refs):
                turned_lefts[k][...] = ref[...].T

        for g, (order, steps, rows, columns) in enumerate(plan):
            height = rows // total
            for which, where, turned, start, width, column in steps:
                if turned:
                    value = lax.dot_general(
                        turned_lefts[which][...],
                        right_refs[where][start : start + width, :],
                        (((1,), (1,)), ((), ())),
                        preferred_element_type=F32,
                    )
                elif tile:
                    value = jnp.dot(turned_lefts[which][...], right_refs[where][...], preferred_element_type=F32)
                else:
                    value = jnp.dot(
                        turned_lefts[which][...],
                        right_refs[where][:, start : start + width],
                        preferred_element_type=F32,
                    )
                width = tile or width
                sums[:rows, column : column + width] = value
            columns = tile or columns
            for b in range(total):
                block = sums[b * height : (b + 1) * height, :columns].astype(BF)
                if paired:
                    place = place_of(own ^ (b // 2), order)
                    upper = me_ref[1] != b % 2
                else:
                    place = place_of(own ^ b, order)
                    upper = place >= half
                    place = place % half

                @pl.when(upper)
                def _(g=g, block=block, place=place):
                    if paired:
                        outs[1][g, place, 0] = block
                    else:
                        outs[2 * g + 1][place, 0] = block

                @pl.when(jnp.logical_not(upper))
                def _(g=g, block=block, place=place):
                    if paired:
                        outs[0][g, place, 0] = block
                    else:
                        outs[2 * g][place, 0] = block

    once = pl.Buffered(1)
    left_specs = [pl.BlockSpec(a.shape, lambda i, me: (0, 0), pipeline_mode=once) for a in lefts]
    if tile:
        tiles = plan[0][3] // tile
        right_specs = [pl.BlockSpec((rights[0].shape[0], tile), lambda i, me: (0, i))]
        rows = plan[0][2] // total
        out_specs = [pl.BlockSpec((half, 1, rows, tile), lambda i, me: (0, 0, 0, i))] * 2
        shapes = [(half, 1, rows, plan[0][3])] * 2
    else:
        tiles = 1
        right_specs = [pl.BlockSpec(a.shape, lambda i, me: (0, 0), pipeline_mode=once) for a in rights]
        if paired:
            shapes = [(len(plan), half, 1, plan[0][2] // total, plan[0][3])] * 2
        else:
            shapes = [(half, 1, rows // total, columns) for _, _, rows, columns in plan for _ in range(2)]
        out_specs = [
            pl.BlockSpec(shape, lambda i, me, n=len(shape): (0,) * n, pipeline_mode=once) for shape in shapes
        ]
    flops = sum(2 * left.shape[0] * rows * columns for (_, _, rows, columns), left in zip(plan, [lefts[0]] * len(plan)))
    moved = sum(2 * a.size for a in lefts + rights) + sum(2 * int(np.prod(shape)) for shape in shapes)
    return pl.pallas_call(
        kernel,
        grid_spec=pltpu.PrefetchScalarGridSpec(
            num_scalar_prefetch=1,
            grid=(tiles,),
            in_specs=left_specs + right_specs + [ANYWHERE] * len(after),
            out_specs=out_specs,
            scratch_shapes=[
                pltpu.VMEM((max(p[2] for p in plan), tile or max(p[3] for p in plan)), F32)
            ]
            + [pltpu.VMEM(a.shape[::-1], BF) for a in lefts],
        ),
        out_shape=[jax.ShapeDtypeStruct(shape, BF) for shape in shapes],
        compiler_params=pltpu.CompilerParams(vmem_limit_bytes=VMEM_LIMIT),
        cost_estimate=pl.CostEstimate(flops=flops, bytes_accessed=moved, transcendentals=0),
    )(me, *lefts, *rights, *after)


def stack_near(halves, cut, after=()):
    half, rows, columns = halves[0].shape
    ranges = ((0, cut), (cut, columns - cut))

    def kernel(*refs):
        outs = refs[2 + len(after) : 4 + len(after)]
        held = refs[4 + len(after) : 6 + len(after)]
        sems = refs[-1]

        def load(p, k):
            source = refs[p].at[:, :, pl.ds(ranges[k][0], ranges[k][1])]
            return pltpu.make_async_copy(source, held[k].at[pl.ds(p * half, half)], sems.at[p, k])

        def store(p, k):
            part = pl.ds(p * half, half)
            return pltpu.make_async_copy(held[k].at[part], outs[k].at[part], sems.at[p, 2 + k])

        steps = [(p, k) for p in range(2) for k in range(2)]
        for step in steps:
            load(*step).start()
        for step in steps:
            load(*step).wait()
            store(*step).start()
        for step in steps:
            store(*step).wait()

    shapes = [(2 * half, rows, width) for _, width in ranges]
    return pl.pallas_call(
        kernel,
        in_specs=[ANYWHERE] * (2 + len(after)),
        out_specs=[ANYWHERE] * 2,
        out_shape=[jax.ShapeDtypeStruct(shape, BF) for shape in shapes],
        scratch_shapes=[pltpu.VMEM(shape, BF) for shape in shapes] + [pltpu.SemaphoreType.DMA((2, 4))],
        compiler_params=pltpu.CompilerParams(vmem_limit_bytes=VMEM_LIMIT),
        cost_estimate=pl.CostEstimate(flops=0, bytes_accessed=8 * half * rows * columns, transcendentals=0),
    )(*halves, *after)


def assemble(low, high, order, me, after=()):
    half, rows, columns = low.shape
    count = 2 * half
    order = steps_of(order, count)

    def kernel(me_ref, *refs):
        out, held, in_sems, out_sems = refs[2 + len(after) :]
        own = me_ref[0]

        def load(k):
            return pltpu.make_async_copy(refs[k], held.at[k], in_sems.at[k])

        def store(k, p):
            block = own ^ near_mask(k * half + p, order)
            return pltpu.make_async_copy(held.at[k, p], out.at[block], out_sems.at[k, p])

        for k in range(2):
            load(k).start()
        for k in range(2):
            load(k).wait()
            for p in range(half):
                store(k, p).start()
        for k in range(2):
            for p in range(half):
                store(k, p).wait()

    return pl.pallas_call(
        kernel,
        grid_spec=pltpu.PrefetchScalarGridSpec(
            num_scalar_prefetch=1,
            grid=(1,),
            in_specs=[ANYWHERE] * (2 + len(after)),
            out_specs=ANYWHERE,
            scratch_shapes=[
                pltpu.VMEM((2, half, rows, columns), BF),
                pltpu.SemaphoreType.DMA((2,)),
                pltpu.SemaphoreType.DMA((2, half)),
            ],
        ),
        out_shape=jax.ShapeDtypeStruct((count, rows, columns), BF),
        compiler_params=pltpu.CompilerParams(vmem_limit_bytes=VMEM_LIMIT),
        cost_estimate=pl.CostEstimate(flops=0, bytes_accessed=4 * count * rows * columns, transcendentals=0),
    )(me, low, high, *after)


def cut_of(width):
    return 128 * ((width // 128 + 1) // 2)


class Gather:
    def __init__(self, shard, cut, after=()):
        self.cut = cut
        self.held = (pin(shard, after) if after else shard)[None]
        self.mask = lax.axis_size("fsdp") // 2
        self.far = hop(self.held, self.mask)

    def double(self, after=()):
        self.held = join(self.held, self.far, after)
        self.mask //= 2
        self.far = hop(self.held, self.mask)

    def spread(self, after=()):
        while self.mask > 4:
            self.double(after)
        self.parts = stack_near((self.held, self.far), self.cut, after)
        self.near = [hop(self.parts[0], 1), hop(self.parts[1], 2)]

    def widen(self, after=()):
        self.low = [join(part, near, after) for part, near in zip(self.parts, self.near)]
        self.high = [hop(self.low[0], 2), hop(self.low[1], 1)]

    def finish(self, k, me, after=()):
        return assemble(self.low[k], self.high[k], ((2, 1), (1, 2))[k], me, after)


def weave(own, other, me):
    count, rows, _ = own[0].shape
    widths = [v.shape[2] for v in own]
    starts = [0, widths[0]]

    def kernel(me_ref, *refs):
        out, held, in_sems, out_sem = refs[4:]

        def load(k):
            target = held.at[:, me_ref[1 + k // 2], :, pl.ds(starts[k % 2], widths[k % 2])]
            return pltpu.make_async_copy(refs[k], target, in_sems.at[k])

        for k in range(4):
            load(k).start()
        for k in range(4):
            load(k).wait()
        store = pltpu.make_async_copy(held, out, out_sem)
        store.start()
        store.wait()

    shape = (count, 2, rows, sum(widths))
    whole = pl.pallas_call(
        kernel,
        grid_spec=pltpu.PrefetchScalarGridSpec(
            num_scalar_prefetch=1,
            grid=(1,),
            in_specs=[ANYWHERE] * 4,
            out_specs=ANYWHERE,
            scratch_shapes=[
                pltpu.VMEM(shape, BF),
                pltpu.SemaphoreType.DMA((4,)),
                pltpu.SemaphoreType.DMA,
            ],
        ),
        out_shape=jax.ShapeDtypeStruct(shape, BF),
        compiler_params=pltpu.CompilerParams(vmem_limit_bytes=VMEM_LIMIT),
        cost_estimate=pl.CostEstimate(flops=0, bytes_accessed=8 * count * rows * sum(widths), transcendentals=0),
    )(me, *own, *other)
    return whole.reshape(2 * count * rows, sum(widths))


def layer_norm(values, scales, offsets):
    center = values - jnp.mean(values, axis=-1, keepdims=True)
    spread = jnp.mean(center * center, axis=-1, keepdims=True)
    return center * lax.rsqrt(spread + EPS_NORM) * scales + offsets


def plain_dot(first_operand, second_operand):
    return jnp.dot(first_operand, second_operand, preferred_element_type=F32)


def dot_first(first_operand, second_operand):
    return lax.dot_general(first_operand, second_operand, (((0,), (0,)), ((), ())), preferred_element_type=F32)


def dot_last(first_operand, second_operand):
    return lax.dot_general(first_operand, second_operand, (((1,), (1,)), ((), ())), preferred_element_type=F32)


def turned_dot(first_operand, second_operand):
    return lax.dot_general(first_operand, second_operand, (((0,), (1,)), ((), ())), preferred_element_type=F32)


def fold_rows(values):
    return jnp.sum(values.reshape(-1, 8, values.shape[-1]), axis=0)


def row_block(rows):
    return 128 if rows % 128 == 0 else rows


def norm_back(partial, received, stream, gain, residual, images, after=()):
    rows, width = stream.shape
    block = row_block(rows)
    per_image = rows // images // block

    def kernel(partial_ref, received_ref, stream_ref, gain_ref, residual_ref, *refs):
        out_ref, low_ref, sums_ref = refs[len(after) :]
        grad = partial_ref[...] + received_ref[...].astype(F32)
        values = stream_ref[...]
        center = values - jnp.mean(values, axis=-1, keepdims=True)
        inverse = lax.rsqrt(jnp.mean(center * center, axis=-1, keepdims=True) + EPS_NORM)
        normed = center * inverse
        scaled = grad * gain_ref[...]
        result = residual_ref[...].astype(F32) + inverse * (
            scaled
            - jnp.mean(scaled, axis=-1, keepdims=True)
            - normed * jnp.mean(scaled * normed, axis=-1, keepdims=True)
        )
        out_ref[...] = result
        low_ref[...] = result.astype(BF)

        @pl.when(pl.program_id(0) % per_image == 0)
        def _():
            sums_ref[...] = jnp.zeros_like(sums_ref)

        sums_ref[0, 0] += fold_rows(grad * normed)
        sums_ref[0, 1] += fold_rows(grad)
        sums_ref[0, 2] += fold_rows(result)

    rows_spec = pl.BlockSpec((block, width), lambda i: (i, 0))
    return pl.pallas_call(
        kernel,
        grid=(rows // block,),
        in_specs=[rows_spec, rows_spec, rows_spec, pl.BlockSpec((1, width), lambda i: (0, 0)), rows_spec]
        + [ANYWHERE] * len(after),
        out_specs=[rows_spec, rows_spec, pl.BlockSpec((1, 3, 8, width), lambda i: (i // per_image, 0, 0, 0))],
        out_shape=[
            jax.ShapeDtypeStruct((rows, width), F32),
            jax.ShapeDtypeStruct((rows, width), BF),
            jax.ShapeDtypeStruct((images, 3, 8, width), F32),
        ],
        compiler_params=pltpu.CompilerParams(vmem_limit_bytes=VMEM_LIMIT),
        cost_estimate=pl.CostEstimate(flops=20 * rows * width, bytes_accessed=20 * rows * width, transcendentals=0),
    )(partial, received, stream, gain.reshape(1, -1), residual, *after)


def joined_back(grad, first, second, gain, after=()):
    rows, width = first.shape
    block = row_block(rows)

    def kernel(grad_ref, first_ref, second_ref, gain_ref, *refs):
        first_out, second_out, sums_ref = refs[len(after) :]
        parts = [slice(0, width), slice(width, 2 * width)]
        values = [first_ref[...].astype(F32), second_ref[...].astype(F32)]
        grads = [grad_ref[:, p] for p in parts]

        def mean(arrays):
            return sum(jnp.sum(a, axis=-1, keepdims=True) for a in arrays) * (0.5 / width)

        middle = mean(values)
        center = [v - middle for v in values]
        inverse = lax.rsqrt(mean([c * c for c in center]) + EPS_NORM)
        normed = [c * inverse for c in center]
        scaled = [g * gain_ref[:, p] for g, p in zip(grads, parts)]
        mean_scaled = mean(scaled)
        mean_product = mean([a * n for a, n in zip(scaled, normed)])
        results = [inverse * (a - mean_scaled - n * mean_product) for a, n in zip(scaled, normed)]
        first_out[...] = results[0]
        second_out[...] = results[1]

        @pl.when(pl.program_id(0) == 0)
        def _():
            sums_ref[...] = jnp.zeros_like(sums_ref)

        for p, g, n in zip(parts, grads, normed):
            sums_ref[0, :, p] += fold_rows(g * n)
            sums_ref[1, :, p] += fold_rows(g)

    rows_spec = pl.BlockSpec((block, width), lambda i: (i, 0))
    both_spec = pl.BlockSpec((block, 2 * width), lambda i: (i, 0))
    return pl.pallas_call(
        kernel,
        grid=(rows // block,),
        in_specs=[both_spec, rows_spec, rows_spec, pl.BlockSpec((1, 2 * width), lambda i: (0, 0))]
        + [ANYWHERE] * len(after),
        out_specs=[rows_spec, rows_spec, pl.BlockSpec((2, 8, 2 * width), lambda i: (0, 0, 0))],
        out_shape=[
            jax.ShapeDtypeStruct((rows, width), F32),
            jax.ShapeDtypeStruct((rows, width), F32),
            jax.ShapeDtypeStruct((2, 8, 2 * width), F32),
        ],
        compiler_params=pltpu.CompilerParams(vmem_limit_bytes=VMEM_LIMIT),
        cost_estimate=pl.CostEstimate(flops=40 * rows * width, bytes_accessed=20 * rows * width, transcendentals=0),
    )(grad, first, second, gain.reshape(1, -1), *after)


GELU_SCALE = 0.7978845608028654
GELU_CUBE = 0.044715


def first_layer(rows_in, weight, bias, after=()):
    rows, depth = rows_in.shape
    width = weight.shape[1]
    tile = 512 if width % 512 == 0 else width
    block = 1024 if rows % 1024 == 0 else rows
    step = 256 if block % 256 == 0 else block

    def kernel(rows_ref, weight_ref, bias_ref, *refs):
        act_ref, slope_ref = refs[len(after) :]
        for start in range(0, block, step):
            part = pl.ds(start, step)
            h = jnp.dot(rows_ref[part, :], weight_ref[...], preferred_element_type=F32) + bias_ref[...]
            square = h * h
            t = jnp.tanh(GELU_SCALE * h * (1.0 + GELU_CUBE * square))
            both = 0.5 * (1.0 + t)
            act_ref[part, :] = (h * both).astype(BF)
            slope = both + 0.5 * h * (1.0 - t * t) * (GELU_SCALE * (1.0 + 3.0 * GELU_CUBE * square))
            slope_ref[part, :] = slope.astype(BF)

    out_spec = pl.BlockSpec((block, tile), lambda m, n: (m, n))
    shape = jax.ShapeDtypeStruct((rows, width), BF)
    return pl.pallas_call(
        kernel,
        grid=(rows // block, width // tile),
        in_specs=[
            pl.BlockSpec((block, depth), lambda m, n: (m, 0)),
            pl.BlockSpec((depth, tile), lambda m, n: (0, n)),
            pl.BlockSpec((1, tile), lambda m, n: (0, n)),
        ]
        + [ANYWHERE] * len(after),
        out_specs=[out_spec] * 2,
        out_shape=[shape] * 2,
        compiler_params=pltpu.CompilerParams(vmem_limit_bytes=VMEM_LIMIT),
        cost_estimate=pl.CostEstimate(
            flops=2 * rows * depth * width, bytes_accessed=2 * depth * width + 4 * rows * width, transcendentals=rows * width
        ),
    )(rows_in, weight, bias.reshape(1, -1), *after)


def first_layer_back(grad, weight, slope, after=()):
    rows, depth = grad.shape
    width = weight.shape[1]
    tile = 512 if width % 512 == 0 else width
    block = 1024 if rows % 1024 == 0 else rows
    step = 256 if block % 256 == 0 else block

    def kernel(grad_ref, weight_ref, slope_ref, *refs):
        out_ref, sums_ref = refs[len(after) :]

        @pl.when(pl.program_id(1) == 0)
        def _():
            sums_ref[...] = jnp.zeros_like(sums_ref)

        for start in range(0, block, step):
            part = pl.ds(start, step)
            value = jnp.dot(grad_ref[part, :], weight_ref[...], preferred_element_type=F32)
            low = (value * slope_ref[part, :].astype(F32)).astype(BF)
            out_ref[part, :] = low
            sums_ref[...] += fold_rows(low.astype(F32))

    return pl.pallas_call(
        kernel,
        grid=(width // tile, rows // block),
        in_specs=[
            pl.BlockSpec((block, depth), lambda n, m: (m, 0)),
            pl.BlockSpec((depth, tile), lambda n, m: (0, n)),
            pl.BlockSpec((block, tile), lambda n, m: (m, n)),
        ]
        + [ANYWHERE] * len(after),
        out_specs=[pl.BlockSpec((block, tile), lambda n, m: (m, n)), pl.BlockSpec((8, tile), lambda n, m: (0, n))],
        out_shape=[jax.ShapeDtypeStruct((rows, width), BF), jax.ShapeDtypeStruct((8, width), F32)],
        compiler_params=pltpu.CompilerParams(vmem_limit_bytes=VMEM_LIMIT),
        cost_estimate=pl.CostEstimate(
            flops=2 * rows * depth * width, bytes_accessed=2 * depth * width + 4 * rows * width, transcendentals=0
        ),
    )(grad, weight, slope, *after)


def head_parts(values):
    center = values - jnp.sum(values, axis=0, keepdims=True) * (1.0 / HEAD_DIM)
    spread = jnp.sum(center * center, axis=0, keepdims=True) * (1.0 / HEAD_DIM)
    inverse = lax.rsqrt(spread + EPS_NORM)
    return center * inverse, inverse


def turn(values, up_table, down_table):
    up = pltpu.roll(values, HEAD_DIM - 1, 0)
    down = pltpu.roll(values, 1, 0)
    return up * up_table + down * down_table


def head_forward(values, gain, offset, tables):
    normed, _ = head_parts(values)
    result = normed * gain + offset
    if tables is not None:
        result = result * tables[0] + turn(result, tables[1], tables[2])
    return result.astype(BF)


def fold_lanes(values):
    total = values[:, :128]
    for start in range(128, values.shape[1], 128):
        total = total + values[:, start : start + 128]
    return total


def head_backward(grad, values, gain, tables):
    if tables is not None:
        grad = grad * tables[0] - turn(grad, tables[1], tables[2])
    normed, inverse = head_parts(values)
    scaled = grad * gain
    mean_scaled = jnp.sum(scaled, axis=0, keepdims=True) * (1.0 / HEAD_DIM)
    mean_product = jnp.sum(scaled * normed, axis=0, keepdims=True) * (1.0 / HEAD_DIM)
    result = inverse * (scaled - mean_scaled - normed * mean_product)
    return result, fold_lanes(grad * normed), fold_lanes(grad)


def score_mask(scores, valid):
    if valid == scores.shape[0]:
        return scores
    row = lax.broadcasted_iota(jnp.int32, scores.shape, 0)
    return jnp.where(row < valid, scores, -1e30)


CHUNK = 256


def attend_kernel(valid, turned, waits, q_ref, k_ref, v_ref, gain_ref, bias_ref, tab_ref, *refs):
    out_ref, lse_ref, q_s, kt_s, v_s = refs[waits:]
    scaling = HEAD_DIM ** (-0.5)
    tables = (tab_ref[0], tab_ref[1], tab_ref[2])
    q_s[...] = head_forward(q_ref[0, 0], gain_ref[0], bias_ref[0], tables)
    keys = head_forward(k_ref[0, 0], gain_ref[1], bias_ref[1], tables if turned else None)
    kt_s[...] = keys.T
    v_s[...] = v_ref[0, 0].astype(BF)
    for start in range(0, q_s.shape[1], CHUNK):
        cols = pl.ds(start, CHUNK)
        scores = jnp.dot(kt_s[...], q_s[:, cols], preferred_element_type=F32)
        scores = score_mask(scores, valid)
        peak = jnp.max(scores, axis=0, keepdims=True)
        exponent = jnp.exp2((scores - peak) * (scaling * LOG2E))
        summed = jnp.sum(exponent, axis=0, keepdims=True)
        mixed = jnp.dot(v_s[...], exponent.astype(BF), preferred_element_type=F32)
        out_ref[0, :, cols] = (mixed * (1.0 / summed)).astype(BF)
        lse_ref[0, :, cols] = peak * scaling + jnp.log(summed)


def head_specs(lead, length):
    return pl.BlockSpec((1, 1, HEAD_DIM, length), lambda i, h: (lead, h, 0, i))


def attend(q_pre, k_pre, v_pre, leads, gains, biases, tables, valid, turned, after=()):
    heads = q_pre.shape[1]
    images = q_pre.shape[3] // SEQ
    key_len = k_pre.shape[3] // images
    per_head = pl.BlockSpec((2, HEAD_DIM, 1), lambda i, h: (0, 0, 0))
    work = images * heads * SEQ * key_len
    return pl.pallas_call(
        functools.partial(attend_kernel, valid, turned, len(after)),
        grid=(images, heads),
        in_specs=[
            head_specs(leads[0], SEQ),
            head_specs(leads[1], key_len),
            head_specs(leads[2], key_len),
            per_head,
            per_head,
            pl.BlockSpec((3, HEAD_DIM, SEQ), lambda i, h: (0, 0, i)),
        ]
        + [ANYWHERE] * len(after),
        out_specs=[
            pl.BlockSpec((1, HEAD_DIM, SEQ), lambda i, h: (h, 0, i)),
            pl.BlockSpec((1, 1, SEQ), lambda i, h: (h, 0, i)),
        ],
        out_shape=[
            jax.ShapeDtypeStruct((heads, HEAD_DIM, images * SEQ), BF),
            jax.ShapeDtypeStruct((heads, 1, images * SEQ), F32),
        ],
        scratch_shapes=[
            pltpu.VMEM((HEAD_DIM, SEQ), BF),
            pltpu.VMEM((key_len, HEAD_DIM), BF),
            pltpu.VMEM((HEAD_DIM, key_len), BF),
        ],
        compiler_params=pltpu.CompilerParams(vmem_limit_bytes=VMEM_LIMIT),
        cost_estimate=pl.CostEstimate(flops=4 * work * 128, bytes_accessed=12 * q_pre.size, transcendentals=work),
    )(q_pre, k_pre, v_pre, gains, biases, tables, *after)


def attend_back_kernel(
    valid, turned, joint, waits, q_ref, k_ref, v_ref, mix_ref, lse_ref, gain_ref, bias_ref, tab_ref, *rest
):
    rest = rest[waits:]
    if joint:
        g_ref, sums_ref, cols_ref, q_s, k_s, kt_s, vt_s, dq_s, dk_s, dv_s = rest
    else:
        gq_ref, gkv_ref, sums_ref, cols_ref, q_s, k_s, kt_s, vt_s, dq_s, dk_s, dv_s = rest
    scaling = HEAD_DIM ** (-0.5)
    tables = (tab_ref[0], tab_ref[1], tab_ref[2])
    key_tables = tables if turned else None
    q_s[...] = head_forward(q_ref[0, 0], gain_ref[0], bias_ref[0], tables)
    keys = head_forward(k_ref[0, 0], gain_ref[1], bias_ref[1], key_tables)
    k_s[...] = keys
    kt_s[...] = keys.T
    vt_s[...] = v_ref[0, 0].astype(BF).T
    last = (((1,), (1,)), ((), ()))
    for start in range(0, q_s.shape[1], CHUNK):
        cols = pl.ds(start, CHUNK)
        scores = jnp.dot(kt_s[...], q_s[:, cols], preferred_element_type=F32)
        scores = score_mask(scores, valid)
        chances = jnp.exp2(scores * (scaling * LOG2E) - lse_ref[0, :, cols] * LOG2E)
        grad_mix = mix_ref[0, :, cols]
        grad_chance = jnp.dot(vt_s[...], grad_mix, preferred_element_type=F32)
        row_sum = jnp.sum(grad_chance * chances, axis=0, keepdims=True)
        grad_low = (chances * (grad_chance - row_sum)).astype(BF)
        dq_s[:, cols] = jnp.dot(k_s[...], grad_low, preferred_element_type=F32) * scaling
        key_term = lax.dot_general(q_s[:, cols], grad_low, last, preferred_element_type=F32) * scaling
        value_term = lax.dot_general(grad_mix, chances.astype(BF), last, preferred_element_type=F32)
        if start == 0:
            dk_s[...] = key_term
            dv_s[...] = value_term
        else:
            dk_s[...] += key_term
            dv_s[...] += value_term
    grad_q, gain_q, bias_q = head_backward(dq_s[...], q_ref[0, 0], gain_ref[0], tables)
    grad_k, gain_k, bias_k = head_backward(dk_s[...], k_ref[0, 0], gain_ref[1], key_tables)
    outs = [grad_q.astype(BF), grad_k.astype(BF), dv_s[...].astype(BF)]
    if joint:
        for j in range(3):
            g_ref[j, 0] = outs[j]
    else:
        gq_ref[0, 0] = outs[0]
        gkv_ref[0, 0] = outs[1]
        gkv_ref[1, 0] = outs[2]

    @pl.when((pl.program_id(0) == 0) & (pl.program_id(1) == 0))
    def _():
        sums_ref[...] = jnp.zeros_like(sums_ref)

    for j, part in enumerate((gain_q, gain_k, bias_q, bias_k)):
        sums_ref[j] += part
    for j, part in enumerate(outs):
        cols_ref[0, j, 0] = fold_lanes(part.astype(F32))


def attend_back(q_pre, k_pre, v_pre, leads, grad_mix, lse, gains, biases, tables, valid, turned, joint, after=()):
    heads = q_pre.shape[1]
    images = q_pre.shape[3] // SEQ
    key_len = k_pre.shape[3] // images
    per_head = pl.BlockSpec((2, HEAD_DIM, 1), lambda i, h: (0, 0, 0))
    work = images * heads * SEQ * key_len
    grads = [(3, SEQ)] if joint else [(1, SEQ), (2, key_len)]
    return pl.pallas_call(
        functools.partial(attend_back_kernel, valid, turned, joint, len(after)),
        grid=(images, heads),
        in_specs=[
            head_specs(leads[0], SEQ),
            head_specs(leads[1], key_len),
            head_specs(leads[2], key_len),
            pl.BlockSpec((1, HEAD_DIM, SEQ), lambda i, h: (h, 0, i)),
            pl.BlockSpec((1, 1, SEQ), lambda i, h: (h, 0, i)),
            per_head,
            per_head,
            pl.BlockSpec((3, HEAD_DIM, SEQ), lambda i, h: (0, 0, i)),
        ]
        + [ANYWHERE] * len(after),
        out_specs=[
            pl.BlockSpec((size, 1, HEAD_DIM, length), lambda i, h: (0, h, 0, i)) for size, length in grads
        ]
        + [
            pl.BlockSpec((4, HEAD_DIM, 128), lambda i, h: (0, 0, 0)),
            pl.BlockSpec((1, 3, 1, HEAD_DIM, 128), lambda i, h: (i, 0, h, 0, 0)),
        ],
        out_shape=[jax.ShapeDtypeStruct((size, heads, HEAD_DIM, images * length), BF) for size, length in grads]
        + [
            jax.ShapeDtypeStruct((4, HEAD_DIM, 128), F32),
            jax.ShapeDtypeStruct((images, 3, heads, HEAD_DIM, 128), F32),
        ],
        scratch_shapes=[
            pltpu.VMEM((HEAD_DIM, SEQ), BF),
            pltpu.VMEM((HEAD_DIM, key_len), BF),
            pltpu.VMEM((key_len, HEAD_DIM), BF),
            pltpu.VMEM((key_len, HEAD_DIM), BF),
            pltpu.VMEM((HEAD_DIM, SEQ), F32),
            pltpu.VMEM((HEAD_DIM, key_len), F32),
            pltpu.VMEM((HEAD_DIM, key_len), F32),
        ],
        compiler_params=pltpu.CompilerParams(vmem_limit_bytes=VMEM_LIMIT),
        cost_estimate=pl.CostEstimate(flops=10 * work * 128, bytes_accessed=20 * q_pre.size, transcendentals=work),
    )(q_pre, k_pre, v_pre, grad_mix, lse, gains, biases, tables, *after)


def rotary_columns(positions):
    quarter = HEAD_DIM // 4
    freqs = 10000.0 ** (-jnp.arange(quarter).astype(F32) / quarter)
    coords = positions.astype(F32).T
    angles = jnp.concatenate([freqs[:, None] * coords[0:1], freqs[:, None] * coords[1:2]], axis=0)
    angles = jnp.repeat(angles, 2, axis=0)
    even = (jnp.arange(HEAD_DIM) % 2 == 0)[:, None]
    sine = jnp.sin(angles)
    return jnp.stack([jnp.cos(angles), jnp.where(even, -sine, 0.0), jnp.where(even, 0.0, sine)])


def with_other(values):
    return jnp.concatenate([values, swap(values)], axis=0)


def branch_sum(operand, weight, rows_local):
    sent = swap(dot_last(operand[rows_local:], weight).astype(BF))
    return dot_last(operand[:rows_local], weight) + sent.astype(F32)


def branch_parts(operand, weight, rows_local):
    sent = swap(dot_last(operand[rows_local:], weight).astype(BF))
    return dot_last(operand[:rows_local], weight), sent


def turned_branch_parts(operand, weight, rows_local):
    sent = swap(turned_dot(operand[:, rows_local:], weight).astype(BF))
    return turned_dot(operand[:, :rows_local], weight), sent


def turned_branch_sum(operand, weight, rows_local):
    sent = swap(turned_dot(operand[:, rows_local:], weight).astype(BF))
    return turned_dot(operand[:, :rows_local], weight) + sent.astype(F32)


def body(
    hidden,
    skip_rows,
    timestep,
    text,
    grid_pos,
    cotangent,
    skip_weight,
    shift_weight,
    qkv_weight,
    cross_query,
    cross_kv,
    out_weight,
    up_weight,
    down_weight,
    column_bias,
    up_bias,
    skip_gain,
    skip_bias,
    norm_gains,
    row_biases,
    head_gains,
    head_biases,
):
    count = lax.axis_size("fsdp")
    f_index = lax.axis_index("fsdp")
    t_index = lax.axis_index("tp")
    me = jnp.stack([f_index, t_index, 1 - t_index]).astype(jnp.int32)
    rows_local, model_width = hidden.shape
    image_count = timestep.shape[0]
    shard_rows = cross_query.shape[0]
    local_width = cross_query.shape[1]
    ff_local = up_weight.shape[1]
    text_width = cross_kv.shape[0] * count
    own_images = max(image_count // 2, 1)
    first_image = t_index * (image_count // 2)

    skip_gather = Gather(skip_weight.astype(BF), cut_of(model_width))

    activated_own = jax.nn.silu(timestep.astype(F32)).astype(BF)
    small_parts = [column_bias, up_bias, skip_gain, skip_bias, norm_gains, row_biases]
    small = jnp.concatenate([p.astype(BF).reshape(-1) for p in small_parts] + [activated_own.reshape(-1)])
    small_own = gather_small(small)
    small_other = swap(small_own)
    first_is_own = t_index == 0
    small_both = jnp.stack(
        [jnp.where(first_is_own, small_own, small_other), jnp.where(first_is_own, small_other, small_own)], axis=1
    )
    edges = np.cumsum([0] + [p.size for p in small_parts])
    own_f = small_own.astype(F32)
    both_f = small_both.astype(F32)
    column_slice = column_bias.shape[2]
    col_bf = (
        own_f[:, edges[0] : edges[1]].reshape(count, 6, column_slice).transpose(1, 0, 2).reshape(6, local_width)
    )
    up_bf = own_f[:, edges[1] : edges[2]].reshape(-1)
    sgain_f = both_f[:, :, edges[2] : edges[3]].reshape(-1)
    sbias_f = both_f[:, :, edges[3] : edges[4]].reshape(-1)
    ngain_f = both_f[:, :, edges[4] : edges[5]].reshape(count, 2, 3, -1).transpose(2, 0, 1, 3).reshape(3, model_width)
    rbias_f = both_f[:, :, edges[5] : edges[6]].reshape(count, 2, 8, -1).transpose(2, 0, 1, 3).reshape(8, model_width)
    activated = small_own[:, edges[6] :].reshape(count * image_count, model_width)

    attention_shard = jnp.concatenate(
        [qkv_weight.astype(BF).reshape(shard_rows, -1), cross_query.astype(BF)], axis=1
    )
    attention_gather = Gather(attention_shard, 2 * local_width)
    skip_gather.double()
    skip_gather.spread()
    attention_gather.double((skip_gather.parts[0],))
    skip_gather.widen((attention_gather.held,))
    out_t = out_weight.astype(BF).transpose(2, 0, 1).reshape(shard_rows, -1)
    pair_shard = cross_kv.astype(BF).reshape(shard_rows, -1)
    branch_gather = Gather(jnp.concatenate([out_t, pair_shard], axis=1), 2 * local_width, (skip_gather.low[0],))
    skip_own = [skip_gather.finish(k, me, (branch_gather.held,)) for k in range(2)]
    skip_w = weave(skip_own, [swap(v) for v in skip_own], me)
    attention_gather.spread((skip_own[1],))
    branch_gather.double((attention_gather.parts[0],))

    device_index = f_index * 2 + t_index
    shift_rows = shift_weight.shape[0]
    activated_cut = lax.dynamic_slice_in_dim(activated, device_index * shift_rows, shift_rows, 1)
    shift_term = plain_dot(activated_cut, shift_weight.astype(BF))
    shift_term = shift_term + swap(shift_term)
    shift_image = reduce_small(shift_term.reshape(count, -1)).reshape(image_count, model_width) + rbias_f[7]
    shift_own = lax.dynamic_slice_in_dim(shift_image, first_image, own_images, 0)
    shift_tokens = jnp.repeat(shift_own, rows_local // own_images, axis=0)

    text_shift = first_image

    def roll_images(values, shift):
        if image_count == 1:
            return values
        shaped = values.reshape(image_count, -1, values.shape[-1])
        return jnp.roll(shaped, shift, axis=0).reshape(values.shape)

    text_len = text.shape[0] // image_count
    text_pad = 128 * ((text_len + 127) // 128)
    text_in = roll_images(text, -text_shift).reshape(image_count, text_len, -1)
    text_in = jnp.pad(text_in, ((0, 0), (0, text_pad - text_len), (0, 0))).reshape(image_count * text_pad, -1)
    pos_own = lax.dynamic_slice_in_dim(grid_pos, t_index * rows_local, rows_local, 0)
    pos_other = lax.dynamic_slice_in_dim(grid_pos, (1 - t_index) * rows_local, rows_local, 0)
    tables = rotary_columns(jnp.concatenate([pos_own, pos_other], axis=0))
    gains_column = head_gains[:, :, None]
    biases_column = head_biases[:, :, None]
    heads = local_width // HEAD_DIM

    def by_head(values, lead):
        return values.reshape(lead, heads, HEAD_DIM, values.shape[-1])

    joined = jnp.concatenate([hidden, skip_rows], axis=1).astype(F32)
    normed_skip = layer_norm(joined, sgain_f, sbias_f).astype(BF)
    stream_zero = plain_dot(normed_skip, skip_w) + rbias_f[6]
    first_in = with_other((layer_norm(stream_zero, ngain_f[0], rbias_f[0]) + shift_tokens).astype(BF))
    grad_ffn = with_other(cotangent)
    attention_gather.widen((first_in,))
    branch_gather.spread((attention_gather.low[0], attention_gather.low[1]))
    qk_w, vc_w = [attention_gather.finish(k, me).reshape(model_width, -1) for k in range(2)]
    v_w = vc_w[:, :local_width]
    query_w = vc_w[:, local_width:]
    qk_pre = by_head(turned_dot(qk_w, first_in) + col_bf[0:2].reshape(-1, 1), 2)
    v_pre = by_head(turned_dot(v_w, first_in) + col_bf[2].reshape(-1, 1), 1)
    branch_gather.widen((qk_pre, v_pre))
    up_shard = pin(up_weight.astype(BF), (attention_gather.low[1],))
    down_shard = pin(down_weight.astype(BF).T, (up_shard,))
    up_w = lax.all_gather(up_shard, "fsdp", axis=0, tiled=True)
    down_t = lax.all_gather(down_shard, "fsdp", axis=0, tiled=True)
    mixture, self_lse = attend(
        qk_pre,
        qk_pre,
        v_pre,
        (0, 1, 0),
        gains_column[0:2],
        biases_column[0:2],
        tables,
        SEQ,
        True,
        (branch_gather.low[0], branch_gather.low[1], down_shard),
    )
    proj_t, pair_w = [branch_gather.finish(k, me) for k in range(2)]
    proj_t = proj_t.reshape(model_width, -1)
    pair_w = pair_w.reshape(text_width, 2 * local_width)
    self_t = proj_t[:, :local_width]
    cross_t = proj_t[:, local_width:]
    mixture = mixture.reshape(local_width, -1)
    stream_one = stream_zero + turned_branch_sum(mixture, self_t, rows_local) + rbias_f[3]
    second_in = with_other(layer_norm(stream_one, ngain_f[1], rbias_f[1]).astype(BF))
    cross_pre = by_head(turned_dot(query_w, second_in) + col_bf[3].reshape(-1, 1), 1)
    pair_pre = by_head(turned_dot(pair_w, text_in) + col_bf[4:6].reshape(-1, 1), 2)
    cross_mixture, cross_lse = attend(
        cross_pre, pair_pre, pair_pre, (0, 0, 1), gains_column[2:4], biases_column[2:4], tables, text_len, False
    )
    cross_mixture = cross_mixture.reshape(local_width, -1)
    stream_two = stream_one + turned_branch_sum(cross_mixture, cross_t, rows_local) + rbias_f[4]
    third_in = with_other(layer_norm(stream_two, ngain_f[2], rbias_f[2]).astype(BF))
    hidden_act, slope = first_layer(third_in, up_w, up_bf)
    tile = 512 if ff_local % 512 == 0 else None
    down = Chain(products([(DOWN_ORDER, [(grad_ffn, hidden_act, False, 0, ff_local)])], me, tile=tile), DOWN_ORDER)

    grad_pre, upb_sums = first_layer_back(grad_ffn, down_t, slope, (down.high,))
    grad_upb = jnp.sum(upb_sums, axis=0)
    up = Chain(products([(UP_ORDER, [(third_in, grad_pre, False, 0, ff_local)])], me, tile=tile), UP_ORDER)
    third_part, third_got = branch_parts(grad_pre, up_w, rows_local)
    grad_two, low_two, sums_two = norm_back(third_part, third_got, stream_two, ngain_f[2], cotangent, 1, (up.high,))
    grad_cross = with_other(low_two)
    grad_cmix = lax.dot_general(cross_t, grad_cross, (((0,), (1,)), ((), ())), preferred_element_type=F32).astype(BF)
    grad_cq, grad_pair, cross_sums, cross_cols = attend_back(
        cross_pre,
        pair_pre,
        pair_pre,
        (0, 0, 1),
        by_head(grad_cmix, 1)[0],
        cross_lse,
        gains_column[2:4],
        biases_column[2:4],
        tables,
        text_len,
        False,
        False,
    )
    grad_cq = grad_cq.reshape(local_width, -1)
    grad_pair = grad_pair.reshape(2 * local_width, -1)
    second_part, second_got = turned_branch_parts(grad_cq, query_w, rows_local)
    down.step((grad_cq,))
    grad_one, low_one, sums_one = norm_back(
        second_part, second_got, stream_one, ngain_f[1], grad_two, 1, (down.high,)
    )
    grad_self = with_other(low_one)
    up.step((low_one,))
    halves = products(
        [
            ((1, 2), [(grad_cross, cross_mixture, True, 0, local_width), (second_in, grad_cq, True, 0, local_width)]),
            ((2, 1), [(text_in, grad_pair, True, 0, 2 * local_width)]),
        ],
        me,
        (up.high,),
    )
    cross_kept, cross_sent = halves[0::2], halves[1::2]
    down.step(cross_sent)
    cross_got = [hop(cross_sent[0], 1), hop(cross_sent[1], 2)]
    grad_mix = lax.dot_general(self_t, grad_self, (((0,), (1,)), ((), ())), preferred_element_type=F32).astype(BF)
    grad_qkv, self_sums, self_cols = attend_back(
        qk_pre,
        qk_pre,
        v_pre,
        (0, 1, 0),
        by_head(grad_mix, 1)[0],
        self_lse,
        gains_column[0:2],
        biases_column[0:2],
        tables,
        SEQ,
        True,
        True,
        (down.high,),
    )
    up.step((grad_qkv,))
    down.step((up.high,))
    cross_near = [add_near(v, g, (down.high,)) for v, g in zip(cross_kept, cross_got)]
    cross_got = [hop(cross_near[0][1], 2), hop(cross_near[1][1], 1)]
    grad_qkv = grad_qkv.reshape(3 * local_width, -1)
    halves = products(
        [
            ((1, 2), [(first_in, grad_qkv, True, 0, 2 * local_width)]),
            (
                (2, 1),
                [
                    (first_in, grad_qkv, True, 2 * local_width, local_width),
                    (grad_self, mixture, True, 0, local_width),
                ],
            ),
        ],
        me,
        (cross_near[0][1], cross_near[1][1]),
    )
    self_kept, self_sent = halves[0::2], halves[1::2]
    self_got = [hop(self_sent[0], 1), hop(self_sent[1], 2)]
    cross_far = FarSum([(v[0], g) for v, g in zip(cross_near, cross_got)], self_sent)
    grad_qk = grad_qkv[: 2 * local_width]
    grad_v = grad_qkv[2 * local_width :]
    first_part = turned_dot(grad_qk[:, rows_local:], qk_w) + turned_dot(grad_v[:, rows_local:], v_w)
    first_got = swap(first_part.astype(BF))
    first_part = turned_dot(grad_qk[:, :rows_local], qk_w) + turned_dot(grad_v[:, :rows_local], v_w)
    grad_zero, low_zero, sums_zero = norm_back(
        first_part, first_got, stream_zero, ngain_f[0], grad_one, own_images, (cross_far.high,)
    )
    skip_cut = model_width // 2
    skip_kept, skip_sent = products(
        [
            ((1, 2), [(normed_skip, low_zero, False, 0, skip_cut)]),
            ((2, 1), [(normed_skip, low_zero, False, skip_cut, skip_cut)]),
        ],
        me,
        paired=True,
    )
    skip_got = swap(skip_sent)
    self_near = [add_near(v, g, (skip_sent,)) for v, g in zip(self_kept, self_got)]
    self_got = [hop(self_near[0][1], 2), hop(self_near[1][1], 1)]
    skip_pair = [
        add_near(skip_kept, skip_got, (self_near[0][1], self_near[1][1]), part=k) for k in range(2)
    ]
    skip_got = [hop(skip_pair[0][1], 1), hop(skip_pair[1][1], 2)]
    up.step((skip_pair[0][1], skip_pair[1][1]))
    cross_far.step((up.high,))
    grad_normed = dot_last(low_zero, skip_w)
    input_grad, skip_grad, skip_sums = joined_back(grad_normed, hidden, skip_rows, sgain_f, (cross_far.high,))
    stream_three = stream_two + branch_sum(hidden_act, down_t, rows_local) + rbias_f[5]
    output = stream_three.astype(BF)
    text_half = text_width // 2
    pair_own = lax.dynamic_slice_in_dim(pair_w, t_index * text_half, text_half, 0)
    pair_other = lax.dynamic_slice_in_dim(pair_w, (1 - t_index) * text_half, text_half, 0)
    text_grad = turned_dot(grad_pair, pair_own) + swap(turned_dot(grad_pair, pair_other).astype(BF)).astype(F32)
    text_grad = text_grad.reshape(image_count, text_pad, -1)[:, :text_len].reshape(image_count * text_len, -1)
    text_grad = roll_images(text_grad, text_shift)

    shift_sums = jnp.sum(sums_zero[:, 1], axis=1)
    if image_count == 1:
        shift_local = shift_sums
    else:
        shift_local = lax.dynamic_update_slice_in_dim(
            jnp.zeros((image_count, model_width), F32), shift_sums, first_image, 0
        )
    shift_held = (shift_local + swap(shift_local))[None]
    shift_masks = [0]

    def shift_double(held, mask, after):
        held = pin(held, after)
        return jnp.concatenate([held, hop(held, mask)], axis=0), shift_masks + [m + mask for m in shift_masks]

    far_bits = [4 << b for b in range(30) if 4 << b < count]
    for mask in far_bits[:-1]:
        shift_held, shift_masks = shift_double(shift_held, mask, (skip_sent,))
    shift_held, shift_masks = shift_double(shift_held, far_bits[-1], (skip_pair[0][1],))
    sums_zero, sums_one, sums_two = (jnp.sum(v, axis=(0, 2)) for v in (sums_zero, sums_one, sums_two))
    skip_sums = jnp.sum(skip_sums, axis=1)
    grad_gains = jnp.stack([sums_zero[0], sums_one[0], sums_two[0]], axis=0)
    grad_biases = jnp.stack(
        [
            sums_zero[1],
            sums_one[1],
            sums_two[1],
            sums_one[2],
            sums_two[2],
            jnp.sum(cotangent.astype(F32), axis=0),
            sums_zero[2],
            sums_zero[1],
        ],
        axis=0,
    )
    self_columns = jnp.sum(self_cols, axis=(0, 4)).reshape(3, local_width)
    cross_columns = jnp.sum(cross_cols, axis=(0, 4)).reshape(3, local_width)
    grad_colb = jnp.concatenate([self_columns, cross_columns], axis=0)
    self_heads = jnp.sum(self_sums, axis=2)
    cross_heads = jnp.sum(cross_sums, axis=2)
    head_part = jnp.concatenate([self_heads[:2], cross_heads[:2], self_heads[2:], cross_heads[2:]]).reshape(-1)

    def by_device(values):
        shaped = values.reshape(values.shape[0], count, 2, -1).transpose(2, 1, 0, 3)
        return shaped.reshape(2, count, -1)

    def for_own(values):
        is_own = (jnp.arange(2) == t_index)[:, None, None]
        return jnp.where(is_own, values[None], 0.0)

    blocks = jnp.concatenate(
        [
            by_device(skip_sums[0:1]),
            by_device(skip_sums[1:2]),
            by_device(grad_gains),
            by_device(grad_biases),
            jnp.broadcast_to(head_part, (2, count, head_part.shape[0])),
            for_own(grad_colb.reshape(6, count, -1).transpose(1, 0, 2).reshape(count, -1)),
            for_own(grad_upb.reshape(count, -1)),
        ],
        axis=-1,
    )
    padded = 1024 * ((blocks.shape[-1] + 1023) // 1024)
    blocks = jnp.pad(blocks, ((0, 0), (0, 0), (0, padded - blocks.shape[-1])))
    blocks = blocks.transpose(1, 0, 2).reshape(2 * count, padded // 128, 128)
    small_kept, small_sent = halve([blocks], (1, 2), me, paired=True)
    small_pair = add_near(small_kept, swap(small_sent))
    small_got = hop(small_pair[1], 1)
    shift_held, shift_masks = shift_double(shift_held, 1, (small_pair[1],))

    skip_near = [add_near(v[0], g, (small_pair[1],)) for v, g in zip(skip_pair, skip_got)]
    skip_got = [hop(skip_near[0][1], 2), hop(skip_near[1][1], 1)]
    small_near = add_near(small_pair[0], small_got, (skip_near[0][1], skip_near[1][1]))
    small_got = hop(small_near[1], 2)
    self_far = FarSum([(v[0], g) for v, g in zip(self_near, self_got)], (small_near[1],))
    shift_held, shift_masks = shift_double(shift_held, 2, (self_far.high,))
    skip_far = FarSum([(v[0], g) for v, g in zip(skip_near, skip_got)], (self_far.high,))
    small_far = FarSum([(small_near[0], small_got)], (skip_far.high,))
    self_far.step((small_far.high,))
    skip_far.step((self_far.high,))
    small_far.step((skip_far.high,))
    cross_sum = cross_far.total()
    shift_all = order_from_masks(
        shift_held.reshape(count, image_count * model_width), np.array(shift_masks)
    ).reshape(count * image_count, model_width)
    sent_shift = lax.dot_general(
        activated_cut.astype(F32), shift_all, (((0,), (0,)), ((), ())), precision=PRECISE
    )
    self_sum = self_far.total()
    skip_sum = skip_far.total()
    small_sum = small_far.total().reshape(-1)
    sent_skip = jnp.concatenate([skip_sum[0, 0], skip_sum[1, 0]], axis=-1)
    sent_up, sent_down = up.total()[0], down.total()[0].T
    sent_cproj, sent_query = cross_sum[0, 0, :, :local_width], cross_sum[0, 0, :, local_width:]
    sent_pair = cross_sum[1, 0, : cross_kv.shape[0]].reshape(cross_kv.shape)
    sent_sproj = self_sum[1, 0, :, local_width:]
    lengths = [skip_gain.size, skip_bias.size, norm_gains.size, row_biases.size, head_gains.size, head_biases.size]
    lengths += [column_bias.size, up_bias.size]
    cuts = np.cumsum([0] + lengths)
    pieces = [small_sum[cuts[i] : cuts[i + 1]] for i in range(len(lengths))]

    sent_qkv = jnp.concatenate([self_sum[0, 0], self_sum[1, 0, :, :local_width]], axis=1).reshape(qkv_weight.shape)
    sent_proj = jnp.stack([sent_sproj.T, sent_cproj.T], axis=0)
    return (
        output,
        input_grad,
        skip_grad,
        text_grad,
        sent_skip,
        sent_shift,
        sent_qkv,
        sent_query,
        sent_pair,
        sent_proj,
        sent_up,
        sent_down,
        pieces[6].reshape(column_bias.shape),
        pieces[7].reshape(up_bias.shape),
        pieces[0],
        pieces[1],
        pieces[2].reshape(norm_gains.shape),
        pieces[3].reshape(row_biases.shape),
        pieces[4].reshape(head_gains.shape),
        pieces[5].reshape(head_biases.shape),
    )


def solution(mesh):
    in_specs = (
        P(("fsdp", "tp"), None),
        P(("fsdp", "tp"), None),
        P("fsdp", None),
        P("fsdp", None),
        P("fsdp", None),
        P(("fsdp", "tp"), None),
        P(("fsdp", "tp"), None),
        P(("fsdp", "tp"), None),
        P("fsdp", None, "tp"),
        P("fsdp", "tp"),
        P("fsdp", None, "tp"),
        P(None, "tp", "fsdp"),
        P("fsdp", "tp"),
        P("tp", "fsdp"),
        P(None, "tp", "fsdp"),
        P("tp", "fsdp"),
        P(("fsdp", "tp")),
        P(("fsdp", "tp")),
        P(None, ("fsdp", "tp")),
        P(None, ("fsdp", "tp")),
        P(),
        P(),
    )
    out_specs = (
        P(("fsdp", "tp"), None),
        P(("fsdp", "tp"), None),
        P(("fsdp", "tp"), None),
        P("fsdp", "tp"),
        P(("fsdp", "tp"), None),
        P(("fsdp", "tp"), None),
        P("fsdp", None, "tp"),
        P("fsdp", "tp"),
        P("fsdp", None, "tp"),
        P(None, "tp", "fsdp"),
        P("fsdp", "tp"),
        P("tp", "fsdp"),
        P(None, "tp", "fsdp"),
        P("tp", "fsdp"),
        P(("fsdp", "tp")),
        P(("fsdp", "tp")),
        P(None, ("fsdp", "tp")),
        P(None, ("fsdp", "tp")),
        P(),
        P(),
    )
    return jax.shard_map(body, mesh=mesh, in_specs=in_specs, out_specs=out_specs, check_vma=False)
```

```python
import functools

import jax
import jax.numpy as jnp
import numpy as np
from jax import lax
from jax.experimental import pallas as pl
from jax.experimental.pallas import tpu as pltpu
from jax.sharding import PartitionSpec as P

HEAD_DIM = 88
SEQ = 1024
EPS_NORM = 1e-06
PRECISE = lax.Precision.HIGHEST
BF = jnp.bfloat16
F32 = jnp.float32
LOG2E = 1.4426950408889634
UP_ORDER = (1, 2)
DOWN_ORDER = (4, 1, 2)
VMEM_LIMIT = 56 * 1024 * 1024


def hop(values, mask):
    count = lax.axis_size("fsdp")
    return lax.ppermute(values, "fsdp", [(i, i ^ mask) for i in range(count)])


def swap(values):
    return lax.ppermute(values, "tp", [(0, 1), (1, 0)])


def far_masks(count):
    return [4 * j for j in range(1, count // 4)]


def natural_masks(count):
    return np.array([(p // (count // 4) % 2) + 2 * (p // (count // 2)) + 4 * (p % (count // 4)) for p in range(count)])


def order_from_masks(values, masks):
    place = np.argsort(masks)
    table = jnp.asarray(place, jnp.int32)
    count = len(masks)
    wanted = jnp.arange(count, dtype=jnp.int32) ^ lax.axis_index("fsdp")
    return jnp.take(values, jnp.take(table, wanted), axis=0)


def gather_small(values):
    count = lax.axis_size("fsdp")
    parts = [values] + [hop(values, m) for m in far_masks(count)]
    held = jnp.stack(parts, axis=0)
    held = jnp.concatenate([held, hop(held, 1)], axis=0)
    held = jnp.concatenate([held, hop(held, 2)], axis=0)
    return order_from_masks(held, natural_masks(count))


def reduce_small(blocks):
    count = blocks.shape[0]
    masks = jnp.asarray(natural_masks(count), jnp.int32)
    held = jnp.take(blocks, masks ^ lax.axis_index("fsdp"), axis=0)
    half = count // 2
    held = held[:half] + hop(held[half:], 2)
    quarter = count // 4
    held = held[:quarter] + hop(held[quarter:], 1)
    total = held[0]
    for j, m in enumerate(far_masks(count)):
        total = total + hop(held[j + 1], m)
    return total


ANYWHERE = pl.BlockSpec(memory_space=pl.ANY)


def light(**work):
    return pl.CostEstimate(flops=1, bytes_accessed=1, transcendentals=0)


class Order:
    last = ()


def in_order(call):
    @functools.wraps(call)
    def ordered(*args, after=(), **kwargs):
        result = call(*args, after=tuple(after) + Order.last, **kwargs)
        Order.last = (result[0] if isinstance(result, (tuple, list)) else result,)
        return result

    return ordered


def steps_of(order, count):
    return tuple(order) + tuple(1 << b for b in range(30) if 1 << b < count and 1 << b not in order)


def near_mask(position, order):
    top = len(order) - 1
    return sum(((position >> (top - k)) & 1) * bit for k, bit in enumerate(order))


def place_of(mask, order):
    top = len(order) - 1
    return sum(((mask >> (bit.bit_length() - 1)) & 1) << (top - k) for k, bit in enumerate(order))


@in_order
def halve(arrays, order, me, after=(), paired=False):
    count = arrays[0].shape[0] // (2 if paired else 1)
    rows, columns = arrays[0].shape[1:]
    order = steps_of(order, count)
    many = len(arrays)
    total = 2 * count if paired else count
    half = total // 2

    def kernel(me_ref, *refs):
        sources = refs[:many]
        low, high, held, in_sems, out_sems = refs[many + len(after) :]
        own = me_ref[0]

        def load(p, k):
            block = own ^ near_mask(p % count, order)
            if paired:
                block = 2 * block + me_ref[1 + p // count]
            return pltpu.make_async_copy(sources[k].at[block], held.at[p, k], in_sems.at[p])

        def store(p):
            target = low if p < half else high
            return pltpu.make_async_copy(held.at[p], target.at[p % half], out_sems.at[p])

        for p in list(range(half, total)) + list(range(half)):
            for k in range(many):
                load(p, k).start()
        for p in list(range(half, total)) + list(range(half)):
            for k in range(many):
                load(p, k).wait()
            store(p).start()
        for p in range(total):
            store(p).wait()

    moved = total * many * rows * columns
    shape = jax.ShapeDtypeStruct((half, many, rows, columns), arrays[0].dtype)
    return pl.pallas_call(
        kernel,
        grid_spec=pltpu.PrefetchScalarGridSpec(
            num_scalar_prefetch=1,
            grid=(1,),
            in_specs=[ANYWHERE] * (many + len(after)),
            out_specs=[ANYWHERE] * 2,
            scratch_shapes=[
                pltpu.VMEM((total, many, rows, columns), arrays[0].dtype),
                pltpu.SemaphoreType.DMA((total,)),
                pltpu.SemaphoreType.DMA((total,)),
            ],
        ),
        out_shape=[shape, shape],
        compiler_params=pltpu.CompilerParams(vmem_limit_bytes=VMEM_LIMIT),
        cost_estimate=light(flops=0, bytes_accessed=4 * moved, transcendentals=0),
    )(me, *arrays, *after)


@in_order
def pin(values, after=()):
    def kernel(in_ref, *refs):
        refs[-1][...] = in_ref[...]

    whole = pl.BlockSpec(values.shape, lambda: (0,) * values.ndim)
    return pl.pallas_call(
        kernel,
        in_specs=[whole] + [ANYWHERE] * len(after),
        out_specs=whole,
        out_shape=jax.ShapeDtypeStruct(values.shape, values.dtype),
        cost_estimate=light(flops=0, bytes_accessed=4 * values.size, transcendentals=0),
    )(values, *after)


def tile_of(columns):
    return columns // 4 if columns % 512 == 0 else columns // 2 if columns % 256 == 0 else columns


@in_order
def add_near(kept, received, after=(), part=None):
    doubled, many, rows, columns = kept.shape[-4:]
    quarter = doubled // 2
    tile = columns // 2 if columns % 256 == 0 else columns
    group = max(quarter // 2, 1)

    def kernel(kept_low, kept_high, got_low, got_high, *refs):
        low, high = refs[len(after) :]
        for out, first, second in ((low, kept_low, got_low), (high, kept_high, got_high)):
            total = first[...].astype(F32) + second[...].astype(F32)
            out[...] = total.reshape(out.shape).astype(kept.dtype)

    block = (group, many, rows, tile)

    def spec(shift):
        if part is None:
            return pl.BlockSpec(block, lambda i, j: (i + shift, 0, 0, j))
        return pl.BlockSpec((1, *block), lambda i, j: (part, i + shift, 0, 0, j))

    out_spec = pl.BlockSpec(block, lambda i, j: (i, 0, 0, j))
    shape = jax.ShapeDtypeStruct((quarter, many, rows, columns), kept.dtype)
    size = doubled * many * rows * columns
    return pl.pallas_call(
        kernel,
        grid=(quarter // group, columns // tile),
        in_specs=[spec(0), spec(quarter // group), spec(0), spec(quarter // group)] + [ANYWHERE] * len(after),
        out_specs=[out_spec] * 2,
        out_shape=[shape, shape],
        compiler_params=pltpu.CompilerParams(vmem_limit_bytes=VMEM_LIMIT),
        cost_estimate=light(flops=size, bytes_accessed=6 * size, transcendentals=0),
    )(kept, kept, received, received, *after)


@in_order
def add_far(pairs, after=()):
    quarter, many, _, columns = pairs[0][0].shape
    heights = [pair[0].shape[2] for pair in pairs]
    rows = max(heights)
    half = quarter // 2
    parts = len(pairs)
    tile = tile_of(columns)
    arrays = [array for pair in pairs for array in pair]
    kind = arrays[0].dtype

    def kernel(*refs):
        outs = refs[2 * parts + len(after) :]
        for j in range(quarter):
            for p in range(parts):
                total = refs[2 * p][j].astype(F32) + refs[2 * p + 1][j].astype(F32)
                if heights[p] < rows:
                    total = jnp.concatenate([total, jnp.zeros((1, rows - heights[p], tile), F32)], axis=1)
                outs[j // half][p, j % half] = total.astype(kind)

    in_specs = [
        pl.BlockSpec((quarter, 1, height, tile), lambda k, i: (0, k, 0, i)) for height in heights for _ in range(2)
    ]
    out_spec = pl.BlockSpec((parts, half, 1, rows, tile), lambda k, i: (0, 0, k, 0, i))
    shape = (parts, half, many, rows, columns)
    size = parts * quarter * many * rows * columns
    return pl.pallas_call(
        kernel,
        grid=(many, columns // tile),
        in_specs=in_specs + [ANYWHERE] * len(after),
        out_specs=[out_spec] * 2,
        out_shape=[jax.ShapeDtypeStruct(shape, kind)] * 2,
        compiler_params=pltpu.CompilerParams(vmem_limit_bytes=VMEM_LIMIT),
        cost_estimate=light(flops=size, bytes_accessed=6 * size, transcendentals=0),
    )(*arrays, *after)


@in_order
def add_halves(kept, received, after=()):
    parts, quarter, many, rows, columns = kept.shape
    half = quarter // 2

    def kernel(kept_ref, got_ref, *refs):
        outs = refs[len(after) :]
        for j in range(quarter):
            total = kept_ref[:, j].astype(F32) + got_ref[:, j].astype(F32)
            outs[j // half][:, j % half] = total.astype(kept.dtype)

    tile = tile_of(columns)
    in_spec = pl.BlockSpec((parts, quarter, 1, rows, tile), lambda k, i: (0, 0, k, 0, i))
    out_spec = pl.BlockSpec((parts, half, 1, rows, tile), lambda k, i: (0, 0, k, 0, i))
    shape = jax.ShapeDtypeStruct((parts, half, many, rows, columns), kept.dtype)
    return pl.pallas_call(
        kernel,
        grid=(many, columns // tile),
        in_specs=[in_spec] * 2 + [ANYWHERE] * len(after),
        out_specs=[out_spec] * 2,
        out_shape=[shape] * 2,
        compiler_params=pltpu.CompilerParams(vmem_limit_bytes=VMEM_LIMIT),
        cost_estimate=light(flops=kept.size, bytes_accessed=6 * kept.size, transcendentals=0),
    )(kept, received, *after)


class FarSum:
    def __init__(self, pairs, after=()):
        self.low, self.high = add_far(pairs, after=after)
        self.mask = 4
        self.got = hop(self.high, self.mask)

    def step(self, after=()):
        self.low, self.high = add_halves(self.low, self.got, after=after)
        self.mask *= 2
        self.got = hop(self.high, self.mask)

    def total(self):
        while self.low.shape[1] > 1:
            self.step()
        return self.low[:, 0].astype(F32) + self.got[:, 0].astype(F32)


class Chain:
    def __init__(self, halves, order):
        self.order = steps_of(order, lax.axis_size("fsdp"))
        self.low, self.high = halves
        self.at = 0
        self.got = hop(self.high, self.order[0])

    def step(self, after=()):
        self.low, self.high = add_near(self.low, self.got, after=after)
        self.at += 1
        self.got = hop(self.high, self.order[self.at])

    def total(self):
        while self.low.shape[0] > 1:
            self.step()
        return self.low[0].astype(F32) + self.got[0].astype(F32)


@in_order
def join(first, second, after=()):
    count = first.shape[0]
    shape = (2 * count, *first.shape[1:])

    def kernel(first_ref, second_ref, *refs):
        out, held, sems = refs[len(after) :]

        def load(k):
            return pltpu.make_async_copy((first_ref, second_ref)[k], held.at[pl.ds(k * count, count)], sems.at[0, k])

        def store(k):
            part = pl.ds(k * count, count)
            return pltpu.make_async_copy(held.at[part], out.at[part], sems.at[1, k])

        for k in range(2):
            load(k).start()
        for k in range(2):
            load(k).wait()
            store(k).start()
        for k in range(2):
            store(k).wait()

    return pl.pallas_call(
        kernel,
        in_specs=[ANYWHERE] * (2 + len(after)),
        out_specs=ANYWHERE,
        out_shape=jax.ShapeDtypeStruct(shape, first.dtype),
        scratch_shapes=[pltpu.VMEM(shape, first.dtype), pltpu.SemaphoreType.DMA((2, 2))],
        compiler_params=pltpu.CompilerParams(vmem_limit_bytes=VMEM_LIMIT),
        cost_estimate=light(flops=0, bytes_accessed=8 * first.size, transcendentals=0),
    )(first, second, *after)


@in_order
def products(groups, me, after=(), paired=False, tile=None):
    devices = lax.axis_size("fsdp")
    total = 2 * devices if paired else devices
    half = total // 2
    lefts, rights = [], []
    plan = []
    for order, terms in groups:
        column = 0
        steps = []
        for left, right, turned, start, width in terms:
            for array, known in ((left, lefts), (right, rights)):
                if not any(array is other for other in known):
                    known.append(array)
            which = [k for k, other in enumerate(lefts) if other is left][0]
            where = [k for k, other in enumerate(rights) if other is right][0]
            steps.append((which, where, turned, start, width, column))
            column += width
        plan.append((steps_of(order, devices), steps, terms[0][0].shape[1], column))

    def kernel(me_ref, *refs):
        left_refs = refs[: len(lefts)]
        right_refs = refs[len(lefts) : len(lefts) + len(rights)]
        rest = refs[len(lefts) + len(rights) + len(after) :]
        outs = rest[: 2 if paired else 2 * len(plan)]
        sums = rest[len(outs)]
        turned_lefts = rest[len(outs) + 1 :]
        own = me_ref[0]

        @pl.when(pl.program_id(0) == 0)
        def _():
            for k, ref in enumerate(left_refs):
                turned_lefts[k][...] = ref[...].T

        for g, (order, steps, rows, columns) in enumerate(plan):
            height = rows // total
            for which, where, turned, start, width, column in steps:
                if turned:
                    value = lax.dot_general(
                        turned_lefts[which][...],
                        right_refs[where][start : start + width, :],
                        (((1,), (1,)), ((), ())),
                        preferred_element_type=F32,
                    )
                elif tile:
                    value = jnp.dot(turned_lefts[which][...], right_refs[where][...], preferred_element_type=F32)
                else:
                    value = jnp.dot(
                        turned_lefts[which][...],
                        right_refs[where][:, start : start + width],
                        preferred_element_type=F32,
                    )
                width = tile or width
                sums[:rows, column : column + width] = value
            columns = tile or columns
            for b in range(total):
                block = sums[b * height : (b + 1) * height, :columns].astype(BF)
                if paired:
                    place = place_of(own ^ (b // 2), order)
                    upper = me_ref[1] != b % 2
                else:
                    place = place_of(own ^ b, order)
                    upper = place >= half
                    place = place % half

                @pl.when(upper)
                def _(g=g, block=block, place=place):
                    if paired:
                        outs[1][g, place, 0] = block
                    else:
                        outs[2 * g + 1][place, 0] = block

                @pl.when(jnp.logical_not(upper))
                def _(g=g, block=block, place=place):
                    if paired:
                        outs[0][g, place, 0] = block
                    else:
                        outs[2 * g][place, 0] = block

    once = pl.Buffered(1)
    left_specs = [pl.BlockSpec(a.shape, lambda i, me: (0, 0), pipeline_mode=once) for a in lefts]
    if tile:
        tiles = plan[0][3] // tile
        right_specs = [pl.BlockSpec((rights[0].shape[0], tile), lambda i, me: (0, i))]
        rows = plan[0][2] // total
        out_specs = [pl.BlockSpec((half, 1, rows, tile), lambda i, me: (0, 0, 0, i))] * 2
        shapes = [(half, 1, rows, plan[0][3])] * 2
    else:
        tiles = 1
        right_specs = [pl.BlockSpec(a.shape, lambda i, me: (0, 0), pipeline_mode=once) for a in rights]
        if paired:
            shapes = [(len(plan), half, 1, plan[0][2] // total, plan[0][3])] * 2
        else:
            shapes = [(half, 1, rows // total, columns) for _, _, rows, columns in plan for _ in range(2)]
        out_specs = [
            pl.BlockSpec(shape, lambda i, me, n=len(shape): (0,) * n, pipeline_mode=once) for shape in shapes
        ]
    flops = sum(2 * left.shape[0] * rows * columns for (_, _, rows, columns), left in zip(plan, [lefts[0]] * len(plan)))
    moved = sum(2 * a.size for a in lefts + rights) + sum(2 * int(np.prod(shape)) for shape in shapes)
    return pl.pallas_call(
        kernel,
        grid_spec=pltpu.PrefetchScalarGridSpec(
            num_scalar_prefetch=1,
            grid=(tiles,),
            in_specs=left_specs + right_specs + [ANYWHERE] * len(after),
            out_specs=out_specs,
            scratch_shapes=[
                pltpu.VMEM((max(p[2] for p in plan), tile or max(p[3] for p in plan)), F32)
            ]
            + [pltpu.VMEM(a.shape[::-1], BF) for a in lefts],
        ),
        out_shape=[jax.ShapeDtypeStruct(shape, BF) for shape in shapes],
        compiler_params=pltpu.CompilerParams(vmem_limit_bytes=VMEM_LIMIT),
        cost_estimate=light(flops=flops, bytes_accessed=moved, transcendentals=0),
    )(me, *lefts, *rights, *after)


@in_order
def stack_near(halves, cut, after=()):
    half, rows, columns = halves[0].shape
    ranges = ((0, cut), (cut, columns - cut))

    def kernel(*refs):
        outs = refs[2 + len(after) : 4 + len(after)]
        held = refs[4 + len(after) : 6 + len(after)]
        sems = refs[-1]

        def load(p, k):
            source = refs[p].at[:, :, pl.ds(ranges[k][0], ranges[k][1])]
            return pltpu.make_async_copy(source, held[k].at[pl.ds(p * half, half)], sems.at[p, k])

        def store(p, k):
            part = pl.ds(p * half, half)
            return pltpu.make_async_copy(held[k].at[part], outs[k].at[part], sems.at[p, 2 + k])

        steps = [(p, k) for p in range(2) for k in range(2)]
        for step in steps:
            load(*step).start()
        for step in steps:
            load(*step).wait()
            store(*step).start()
        for step in steps:
            store(*step).wait()

    shapes = [(2 * half, rows, width) for _, width in ranges]
    return pl.pallas_call(
        kernel,
        in_specs=[ANYWHERE] * (2 + len(after)),
        out_specs=[ANYWHERE] * 2,
        out_shape=[jax.ShapeDtypeStruct(shape, BF) for shape in shapes],
        scratch_shapes=[pltpu.VMEM(shape, BF) for shape in shapes] + [pltpu.SemaphoreType.DMA((2, 4))],
        compiler_params=pltpu.CompilerParams(vmem_limit_bytes=VMEM_LIMIT),
        cost_estimate=light(flops=0, bytes_accessed=8 * half * rows * columns, transcendentals=0),
    )(*halves, *after)


@in_order
def assemble(low, high, order, me, after=()):
    half, rows, columns = low.shape
    count = 2 * half
    order = steps_of(order, count)

    def kernel(me_ref, *refs):
        out, held, in_sems, out_sems = refs[2 + len(after) :]
        own = me_ref[0]

        def load(k):
            return pltpu.make_async_copy(refs[k], held.at[k], in_sems.at[k])

        def store(k, p):
            block = own ^ near_mask(k * half + p, order)
            return pltpu.make_async_copy(held.at[k, p], out.at[block], out_sems.at[k, p])

        for k in range(2):
            load(k).start()
        for k in range(2):
            load(k).wait()
            for p in range(half):
                store(k, p).start()
        for k in range(2):
            for p in range(half):
                store(k, p).wait()

    return pl.pallas_call(
        kernel,
        grid_spec=pltpu.PrefetchScalarGridSpec(
            num_scalar_prefetch=1,
            grid=(1,),
            in_specs=[ANYWHERE] * (2 + len(after)),
            out_specs=ANYWHERE,
            scratch_shapes=[
                pltpu.VMEM((2, half, rows, columns), BF),
                pltpu.SemaphoreType.DMA((2,)),
                pltpu.SemaphoreType.DMA((2, half)),
            ],
        ),
        out_shape=jax.ShapeDtypeStruct((count, rows, columns), BF),
        compiler_params=pltpu.CompilerParams(vmem_limit_bytes=VMEM_LIMIT),
        cost_estimate=light(flops=0, bytes_accessed=4 * count * rows * columns, transcendentals=0),
    )(me, low, high, *after)


def cut_of(width):
    return 128 * ((width // 128 + 1) // 2)


class Gather:
    def __init__(self, shard, cut, first=False):
        self.cut = cut
        self.held = (shard if first else pin(shard))[None]
        self.mask = lax.axis_size("fsdp") // 2
        self.far = hop(self.held, self.mask)

    def double(self, after=()):
        self.held = join(self.held, self.far, after=after)
        self.mask //= 2
        self.far = hop(self.held, self.mask)

    def spread(self, after=()):
        while self.mask > 4:
            self.double(after)
        self.parts = stack_near((self.held, self.far), self.cut, after=after)
        self.near = [hop(self.parts[0], 1), hop(self.parts[1], 2)]

    def widen(self, after=()):
        self.low = [join(part, near, after=after) for part, near in zip(self.parts, self.near)]
        self.high = [hop(self.low[0], 2), hop(self.low[1], 1)]

    def finish(self, k, me, after=()):
        return assemble(self.low[k], self.high[k], ((2, 1), (1, 2))[k], me, after=after)


@in_order
def weave(own, other, me, after=()):
    count, rows, _ = own[0].shape
    widths = [v.shape[2] for v in own]
    starts = [0, widths[0]]

    def kernel(me_ref, *refs):
        out, held, in_sems, out_sem = refs[4 + len(after) :]

        def load(k):
            target = held.at[:, me_ref[1 + k // 2], :, pl.ds(starts[k % 2], widths[k % 2])]
            return pltpu.make_async_copy(refs[k], target, in_sems.at[k])

        for k in range(4):
            load(k).start()
        for k in range(4):
            load(k).wait()
        store = pltpu.make_async_copy(held, out, out_sem)
        store.start()
        store.wait()

    shape = (count, 2, rows, sum(widths))
    whole = pl.pallas_call(
        kernel,
        grid_spec=pltpu.PrefetchScalarGridSpec(
            num_scalar_prefetch=1,
            grid=(1,),
            in_specs=[ANYWHERE] * (4 + len(after)),
            out_specs=ANYWHERE,
            scratch_shapes=[
                pltpu.VMEM(shape, BF),
                pltpu.SemaphoreType.DMA((4,)),
                pltpu.SemaphoreType.DMA,
            ],
        ),
        out_shape=jax.ShapeDtypeStruct(shape, BF),
        compiler_params=pltpu.CompilerParams(vmem_limit_bytes=VMEM_LIMIT),
        cost_estimate=light(flops=0, bytes_accessed=8 * count * rows * sum(widths), transcendentals=0),
    )(me, *own, *other, *after)
    return whole.reshape(2 * count * rows, sum(widths))


def layer_norm(values, scales, offsets):
    center = values - jnp.mean(values, axis=-1, keepdims=True)
    spread = jnp.mean(center * center, axis=-1, keepdims=True)
    return center * lax.rsqrt(spread + EPS_NORM) * scales + offsets


def plain_dot(first_operand, second_operand):
    return jnp.dot(first_operand, second_operand, preferred_element_type=F32)


def dot_first(first_operand, second_operand):
    return lax.dot_general(first_operand, second_operand, (((0,), (0,)), ((), ())), preferred_element_type=F32)


def dot_last(first_operand, second_operand):
    return lax.dot_general(first_operand, second_operand, (((1,), (1,)), ((), ())), preferred_element_type=F32)


def turned_dot(first_operand, second_operand):
    return lax.dot_general(first_operand, second_operand, (((0,), (1,)), ((), ())), preferred_element_type=F32)


def fold_rows(values):
    return jnp.sum(values.reshape(-1, 8, values.shape[-1]), axis=0)


def row_block(rows):
    return 128 if rows % 128 == 0 else rows


@in_order
def norm_back(partial, received, stream, gain, residual, images, after=()):
    rows, width = stream.shape
    block = row_block(rows)
    per_image = rows // images // block

    def kernel(partial_ref, received_ref, stream_ref, gain_ref, residual_ref, *refs):
        out_ref, low_ref, sums_ref = refs[len(after) :]
        grad = partial_ref[...] + received_ref[...].astype(F32)
        values = stream_ref[...]
        center = values - jnp.mean(values, axis=-1, keepdims=True)
        inverse = lax.rsqrt(jnp.mean(center * center, axis=-1, keepdims=True) + EPS_NORM)
        normed = center * inverse
        scaled = grad * gain_ref[...]
        result = residual_ref[...].astype(F32) + inverse * (
            scaled
            - jnp.mean(scaled, axis=-1, keepdims=True)
            - normed * jnp.mean(scaled * normed, axis=-1, keepdims=True)
        )
        out_ref[...] = result
        low_ref[...] = result.astype(BF)

        @pl.when(pl.program_id(0) % per_image == 0)
        def _():
            sums_ref[...] = jnp.zeros_like(sums_ref)

        sums_ref[0, 0] += fold_rows(grad * normed)
        sums_ref[0, 1] += fold_rows(grad)
        sums_ref[0, 2] += fold_rows(result)

    rows_spec = pl.BlockSpec((block, width), lambda i: (i, 0))
    return pl.pallas_call(
        kernel,
        grid=(rows // block,),
        in_specs=[rows_spec, rows_spec, rows_spec, pl.BlockSpec((1, width), lambda i: (0, 0)), rows_spec]
        + [ANYWHERE] * len(after),
        out_specs=[rows_spec, rows_spec, pl.BlockSpec((1, 3, 8, width), lambda i: (i // per_image, 0, 0, 0))],
        out_shape=[
            jax.ShapeDtypeStruct((rows, width), F32),
            jax.ShapeDtypeStruct((rows, width), BF),
            jax.ShapeDtypeStruct((images, 3, 8, width), F32),
        ],
        compiler_params=pltpu.CompilerParams(vmem_limit_bytes=VMEM_LIMIT),
        cost_estimate=light(flops=20 * rows * width, bytes_accessed=20 * rows * width, transcendentals=0),
    )(partial, received, stream, gain.reshape(1, -1), residual, *after)


@in_order
def joined_back(low, weight, first, second, gain, after=()):
    rows, width = first.shape
    block = 256 if rows % 256 == 0 else rows

    def kernel(low_ref, weight_ref, first_ref, second_ref, gain_ref, *refs):
        first_out, second_out, sums_ref = refs[len(after) :]
        parts = [slice(0, width), slice(width, 2 * width)]
        values = [first_ref[...].astype(F32), second_ref[...].astype(F32)]
        grads = [
            lax.dot_general(low_ref[...], weight_ref[p, :], (((1,), (1,)), ((), ())), preferred_element_type=F32)
            for p in parts
        ]

        def mean(arrays):
            return sum(jnp.sum(a, axis=-1, keepdims=True) for a in arrays) * (0.5 / width)

        middle = mean(values)
        center = [v - middle for v in values]
        inverse = lax.rsqrt(mean([c * c for c in center]) + EPS_NORM)
        normed = [c * inverse for c in center]
        scaled = [g * gain_ref[:, p] for g, p in zip(grads, parts)]
        mean_scaled = mean(scaled)
        mean_product = mean([a * n for a, n in zip(scaled, normed)])
        results = [inverse * (a - mean_scaled - n * mean_product) for a, n in zip(scaled, normed)]
        first_out[...] = results[0]
        second_out[...] = results[1]

        @pl.when(pl.program_id(0) == 0)
        def _():
            sums_ref[...] = jnp.zeros_like(sums_ref)

        for p, g, n in zip(parts, grads, normed):
            sums_ref[0, :, p] += fold_rows(g * n)
            sums_ref[1, :, p] += fold_rows(g)

    rows_spec = pl.BlockSpec((block, width), lambda i: (i, 0))
    whole_spec = pl.BlockSpec(weight.shape, lambda i: (0, 0), pipeline_mode=pl.Buffered(1))
    return pl.pallas_call(
        kernel,
        grid=(rows // block,),
        in_specs=[rows_spec, whole_spec, rows_spec, rows_spec, pl.BlockSpec((1, 2 * width), lambda i: (0, 0))]
        + [ANYWHERE] * len(after),
        out_specs=[rows_spec, rows_spec, pl.BlockSpec((2, 8, 2 * width), lambda i: (0, 0, 0))],
        out_shape=[
            jax.ShapeDtypeStruct((rows, width), F32),
            jax.ShapeDtypeStruct((rows, width), F32),
            jax.ShapeDtypeStruct((2, 8, 2 * width), F32),
        ],
        compiler_params=pltpu.CompilerParams(vmem_limit_bytes=VMEM_LIMIT),
        cost_estimate=light(flops=40 * rows * width, bytes_accessed=20 * rows * width, transcendentals=0),
    )(low, weight, first, second, gain.reshape(1, -1), *after)


GELU_SCALE = 0.7978845608028654
GELU_CUBE = 0.044715


@in_order
def first_layer(rows_in, weight, bias, after=()):
    rows, depth = rows_in.shape
    width = weight.shape[1]
    tile = 512 if width % 512 == 0 else width
    block = 1024 if rows % 1024 == 0 else rows
    step = 256 if block % 256 == 0 else block

    def kernel(rows_ref, weight_ref, bias_ref, *refs):
        act_ref, slope_ref = refs[len(after) :]
        for start in range(0, block, step):
            part = pl.ds(start, step)
            h = jnp.dot(rows_ref[part, :], weight_ref[...], preferred_element_type=F32) + bias_ref[...]
            square = h * h
            t = jnp.tanh(GELU_SCALE * h * (1.0 + GELU_CUBE * square))
            both = 0.5 * (1.0 + t)
            act_ref[part, :] = (h * both).astype(BF)
            slope = both + 0.5 * h * (1.0 - t * t) * (GELU_SCALE * (1.0 + 3.0 * GELU_CUBE * square))
            slope_ref[part, :] = slope.astype(BF)

    out_spec = pl.BlockSpec((block, tile), lambda m, n: (m, n))
    shape = jax.ShapeDtypeStruct((rows, width), BF)
    return pl.pallas_call(
        kernel,
        grid=(rows // block, width // tile),
        in_specs=[
            pl.BlockSpec((block, depth), lambda m, n: (m, 0)),
            pl.BlockSpec((depth, tile), lambda m, n: (0, n)),
            pl.BlockSpec((1, tile), lambda m, n: (0, n)),
        ]
        + [ANYWHERE] * len(after),
        out_specs=[out_spec] * 2,
        out_shape=[shape] * 2,
        compiler_params=pltpu.CompilerParams(vmem_limit_bytes=VMEM_LIMIT),
        cost_estimate=light(
            flops=2 * rows * depth * width, bytes_accessed=2 * depth * width + 4 * rows * width, transcendentals=rows * width
        ),
    )(rows_in, weight, bias.reshape(1, -1), *after)


@in_order
def first_layer_back(grad, weight, slope, after=()):
    rows, depth = grad.shape
    width = weight.shape[1]
    tile = 512 if width % 512 == 0 else width
    block = 1024 if rows % 1024 == 0 else rows
    step = 256 if block % 256 == 0 else block

    def kernel(grad_ref, weight_ref, slope_ref, *refs):
        out_ref, sums_ref = refs[len(after) :]

        @pl.when(pl.program_id(1) == 0)
        def _():
            sums_ref[...] = jnp.zeros_like(sums_ref)

        for start in range(0, block, step):
            part = pl.ds(start, step)
            value = jnp.dot(grad_ref[part, :], weight_ref[...], preferred_element_type=F32)
            low = (value * slope_ref[part, :].astype(F32)).astype(BF)
            out_ref[part, :] = low
            sums_ref[...] += fold_rows(low.astype(F32))

    return pl.pallas_call(
        kernel,
        grid=(width // tile, rows // block),
        in_specs=[
            pl.BlockSpec((block, depth), lambda n, m: (m, 0)),
            pl.BlockSpec((depth, tile), lambda n, m: (0, n)),
            pl.BlockSpec((block, tile), lambda n, m: (m, n)),
        ]
        + [ANYWHERE] * len(after),
        out_specs=[pl.BlockSpec((block, tile), lambda n, m: (m, n)), pl.BlockSpec((8, tile), lambda n, m: (0, n))],
        out_shape=[jax.ShapeDtypeStruct((rows, width), BF), jax.ShapeDtypeStruct((8, width), F32)],
        compiler_params=pltpu.CompilerParams(vmem_limit_bytes=VMEM_LIMIT),
        cost_estimate=light(
            flops=2 * rows * depth * width, bytes_accessed=2 * depth * width + 4 * rows * width, transcendentals=0
        ),
    )(grad, weight, slope, *after)


def head_parts(values):
    center = values - jnp.sum(values, axis=0, keepdims=True) * (1.0 / HEAD_DIM)
    spread = jnp.sum(center * center, axis=0, keepdims=True) * (1.0 / HEAD_DIM)
    inverse = lax.rsqrt(spread + EPS_NORM)
    return center * inverse, inverse


def turn(values, up_table, down_table):
    up = pltpu.roll(values, HEAD_DIM - 1, 0)
    down = pltpu.roll(values, 1, 0)
    return up * up_table + down * down_table


def head_forward(values, gain, offset, tables):
    normed, _ = head_parts(values)
    result = normed * gain + offset
    if tables is not None:
        result = result * tables[0] + turn(result, tables[1], tables[2])
    return result.astype(BF)


def fold_lanes(values):
    total = values[:, :128]
    for start in range(128, values.shape[1], 128):
        total = total + values[:, start : start + 128]
    return total


def head_backward(grad, values, gain, tables):
    if tables is not None:
        grad = grad * tables[0] - turn(grad, tables[1], tables[2])
    normed, inverse = head_parts(values)
    scaled = grad * gain
    mean_scaled = jnp.sum(scaled, axis=0, keepdims=True) * (1.0 / HEAD_DIM)
    mean_product = jnp.sum(scaled * normed, axis=0, keepdims=True) * (1.0 / HEAD_DIM)
    result = inverse * (scaled - mean_scaled - normed * mean_product)
    return result, fold_lanes(grad * normed), fold_lanes(grad)


def score_mask(scores, valid):
    if valid == scores.shape[0]:
        return scores
    row = lax.broadcasted_iota(jnp.int32, scores.shape, 0)
    return jnp.where(row < valid, scores, -1e30)


CHUNK = 256


def attend_kernel(valid, turned, waits, q_ref, k_ref, v_ref, gain_ref, bias_ref, tab_ref, *refs):
    out_ref, lse_ref, q_s, kt_s, v_s = refs[waits:]
    scaling = HEAD_DIM ** (-0.5)
    tables = (tab_ref[0], tab_ref[1], tab_ref[2])
    q_s[...] = head_forward(q_ref[0, 0], gain_ref[0], bias_ref[0], tables)
    keys = head_forward(k_ref[0, 0], gain_ref[1], bias_ref[1], tables if turned else None)
    kt_s[...] = keys.T
    v_s[...] = v_ref[0, 0].astype(BF)
    for start in range(0, q_s.shape[1], CHUNK):
        cols = pl.ds(start, CHUNK)
        scores = jnp.dot(kt_s[...], q_s[:, cols], preferred_element_type=F32)
        scores = score_mask(scores, valid)
        peak = jnp.max(scores, axis=0, keepdims=True)
        exponent = jnp.exp2((scores - peak) * (scaling * LOG2E))
        summed = jnp.sum(exponent, axis=0, keepdims=True)
        mixed = jnp.dot(v_s[...], exponent.astype(BF), preferred_element_type=F32)
        out_ref[0, :, cols] = (mixed * (1.0 / summed)).astype(BF)
        lse_ref[0, :, cols] = peak * scaling + jnp.log(summed)


def head_specs(lead, length):
    return pl.BlockSpec((1, 1, HEAD_DIM, length), lambda i, h: (lead, h, 0, i))


@in_order
def attend(q_pre, k_pre, v_pre, leads, gains, biases, tables, valid, turned, after=()):
    heads = q_pre.shape[1]
    images = q_pre.shape[3] // SEQ
    key_len = k_pre.shape[3] // images
    per_head = pl.BlockSpec((2, HEAD_DIM, 1), lambda i, h: (0, 0, 0))
    work = images * heads * SEQ * key_len
    return pl.pallas_call(
        functools.partial(attend_kernel, valid, turned, len(after)),
        grid=(images, heads),
        in_specs=[
            head_specs(leads[0], SEQ),
            head_specs(leads[1], key_len),
            head_specs(leads[2], key_len),
            per_head,
            per_head,
            pl.BlockSpec((3, HEAD_DIM, SEQ), lambda i, h: (0, 0, i)),
        ]
        + [ANYWHERE] * len(after),
        out_specs=[
            pl.BlockSpec((1, HEAD_DIM, SEQ), lambda i, h: (h, 0, i)),
            pl.BlockSpec((1, 1, SEQ), lambda i, h: (h, 0, i)),
        ],
        out_shape=[
            jax.ShapeDtypeStruct((heads, HEAD_DIM, images * SEQ), BF),
            jax.ShapeDtypeStruct((heads, 1, images * SEQ), F32),
        ],
        scratch_shapes=[
            pltpu.VMEM((HEAD_DIM, SEQ), BF),
            pltpu.VMEM((key_len, HEAD_DIM), BF),
            pltpu.VMEM((HEAD_DIM, key_len), BF),
        ],
        compiler_params=pltpu.CompilerParams(vmem_limit_bytes=VMEM_LIMIT),
        cost_estimate=light(flops=4 * work * 128, bytes_accessed=12 * q_pre.size, transcendentals=work),
    )(q_pre, k_pre, v_pre, gains, biases, tables, *after)


def attend_back_kernel(
    valid, turned, joint, waits, q_ref, k_ref, v_ref, mix_ref, lse_ref, gain_ref, bias_ref, tab_ref, *rest
):
    rest = rest[waits:]
    if joint:
        g_ref, sums_ref, cols_ref, q_s, k_s, kt_s, vt_s, dq_s, dk_s, dv_s = rest
    else:
        gq_ref, gkv_ref, sums_ref, cols_ref, q_s, k_s, kt_s, vt_s, dq_s, dk_s, dv_s = rest
    scaling = HEAD_DIM ** (-0.5)
    tables = (tab_ref[0], tab_ref[1], tab_ref[2])
    key_tables = tables if turned else None
    q_s[...] = head_forward(q_ref[0, 0], gain_ref[0], bias_ref[0], tables)
    keys = head_forward(k_ref[0, 0], gain_ref[1], bias_ref[1], key_tables)
    k_s[...] = keys
    kt_s[...] = keys.T
    vt_s[...] = v_ref[0, 0].astype(BF).T
    last = (((1,), (1,)), ((), ()))
    for start in range(0, q_s.shape[1], CHUNK):
        cols = pl.ds(start, CHUNK)
        scores = jnp.dot(kt_s[...], q_s[:, cols], preferred_element_type=F32)
        scores = score_mask(scores, valid)
        chances = jnp.exp2(scores * (scaling * LOG2E) - lse_ref[0, :, cols] * LOG2E)
        grad_mix = mix_ref[0, :, cols]
        grad_chance = jnp.dot(vt_s[...], grad_mix, preferred_element_type=F32)
        row_sum = jnp.sum(grad_chance * chances, axis=0, keepdims=True)
        grad_low = (chances * (grad_chance - row_sum)).astype(BF)
        dq_s[:, cols] = jnp.dot(k_s[...], grad_low, preferred_element_type=F32) * scaling
        key_term = lax.dot_general(q_s[:, cols], grad_low, last, preferred_element_type=F32) * scaling
        value_term = lax.dot_general(grad_mix, chances.astype(BF), last, preferred_element_type=F32)
        if start == 0:
            dk_s[...] = key_term
            dv_s[...] = value_term
        else:
            dk_s[...] += key_term
            dv_s[...] += value_term
    grad_q, gain_q, bias_q = head_backward(dq_s[...], q_ref[0, 0], gain_ref[0], tables)
    grad_k, gain_k, bias_k = head_backward(dk_s[...], k_ref[0, 0], gain_ref[1], key_tables)
    outs = [grad_q.astype(BF), grad_k.astype(BF), dv_s[...].astype(BF)]
    if joint:
        for j in range(3):
            g_ref[j, 0] = outs[j]
    else:
        gq_ref[0, 0] = outs[0]
        gkv_ref[0, 0] = outs[1]
        gkv_ref[1, 0] = outs[2]

    @pl.when((pl.program_id(0) == 0) & (pl.program_id(1) == 0))
    def _():
        sums_ref[...] = jnp.zeros_like(sums_ref)

    for j, part in enumerate((gain_q, gain_k, bias_q, bias_k)):
        sums_ref[j] += part
    for j, part in enumerate(outs):
        cols_ref[0, j, 0] = fold_lanes(part.astype(F32))


@in_order
def attend_back(q_pre, k_pre, v_pre, leads, grad_mix, lse, gains, biases, tables, valid, turned, joint, after=()):
    heads = q_pre.shape[1]
    images = q_pre.shape[3] // SEQ
    key_len = k_pre.shape[3] // images
    per_head = pl.BlockSpec((2, HEAD_DIM, 1), lambda i, h: (0, 0, 0))
    work = images * heads * SEQ * key_len
    grads = [(3, SEQ)] if joint else [(1, SEQ), (2, key_len)]
    return pl.pallas_call(
        functools.partial(attend_back_kernel, valid, turned, joint, len(after)),
        grid=(images, heads),
        in_specs=[
            head_specs(leads[0], SEQ),
            head_specs(leads[1], key_len),
            head_specs(leads[2], key_len),
            pl.BlockSpec((1, HEAD_DIM, SEQ), lambda i, h: (h, 0, i)),
            pl.BlockSpec((1, 1, SEQ), lambda i, h: (h, 0, i)),
            per_head,
            per_head,
            pl.BlockSpec((3, HEAD_DIM, SEQ), lambda i, h: (0, 0, i)),
        ]
        + [ANYWHERE] * len(after),
        out_specs=[
            pl.BlockSpec((size, 1, HEAD_DIM, length), lambda i, h: (0, h, 0, i)) for size, length in grads
        ]
        + [
            pl.BlockSpec((4, HEAD_DIM, 128), lambda i, h: (0, 0, 0)),
            pl.BlockSpec((1, 3, 1, HEAD_DIM, 128), lambda i, h: (i, 0, h, 0, 0)),
        ],
        out_shape=[jax.ShapeDtypeStruct((size, heads, HEAD_DIM, images * length), BF) for size, length in grads]
        + [
            jax.ShapeDtypeStruct((4, HEAD_DIM, 128), F32),
            jax.ShapeDtypeStruct((images, 3, heads, HEAD_DIM, 128), F32),
        ],
        scratch_shapes=[
            pltpu.VMEM((HEAD_DIM, SEQ), BF),
            pltpu.VMEM((HEAD_DIM, key_len), BF),
            pltpu.VMEM((key_len, HEAD_DIM), BF),
            pltpu.VMEM((key_len, HEAD_DIM), BF),
            pltpu.VMEM((HEAD_DIM, SEQ), F32),
            pltpu.VMEM((HEAD_DIM, key_len), F32),
            pltpu.VMEM((HEAD_DIM, key_len), F32),
        ],
        compiler_params=pltpu.CompilerParams(vmem_limit_bytes=VMEM_LIMIT),
        cost_estimate=light(flops=10 * work * 128, bytes_accessed=20 * q_pre.size, transcendentals=work),
    )(q_pre, k_pre, v_pre, grad_mix, lse, gains, biases, tables, *after)


def rotary_columns(positions):
    quarter = HEAD_DIM // 4
    freqs = 10000.0 ** (-jnp.arange(quarter).astype(F32) / quarter)
    coords = positions.astype(F32).T
    angles = jnp.concatenate([freqs[:, None] * coords[0:1], freqs[:, None] * coords[1:2]], axis=0)
    angles = jnp.repeat(angles, 2, axis=0)
    even = (jnp.arange(HEAD_DIM) % 2 == 0)[:, None]
    sine = jnp.sin(angles)
    return jnp.stack([jnp.cos(angles), jnp.where(even, -sine, 0.0), jnp.where(even, 0.0, sine)])


def with_other(values):
    return jnp.concatenate([values, swap(values)], axis=0)


def branch_sum(operand, weight, rows_local):
    sent = swap(dot_last(operand[rows_local:], weight).astype(BF))
    return dot_last(operand[:rows_local], weight) + sent.astype(F32)


def branch_parts(operand, weight, rows_local):
    sent = swap(dot_last(operand[rows_local:], weight).astype(BF))
    return dot_last(operand[:rows_local], weight), sent


def turned_branch_parts(operand, weight, rows_local):
    sent = swap(turned_dot(operand[:, rows_local:], weight).astype(BF))
    return turned_dot(operand[:, :rows_local], weight), sent


def turned_branch_sum(operand, weight, rows_local):
    sent = swap(turned_dot(operand[:, rows_local:], weight).astype(BF))
    return turned_dot(operand[:, :rows_local], weight) + sent.astype(F32)


def body(
    hidden,
    skip_rows,
    timestep,
    text,
    grid_pos,
    cotangent,
    skip_weight,
    shift_weight,
    qkv_weight,
    cross_query,
    cross_kv,
    out_weight,
    up_weight,
    down_weight,
    column_bias,
    up_bias,
    skip_gain,
    skip_bias,
    norm_gains,
    row_biases,
    head_gains,
    head_biases,
):
    Order.last = ()
    count = lax.axis_size("fsdp")
    f_index = lax.axis_index("fsdp")
    t_index = lax.axis_index("tp")
    me = jnp.stack([f_index, t_index, 1 - t_index]).astype(jnp.int32)
    rows_local, model_width = hidden.shape
    image_count = timestep.shape[0]
    shard_rows = cross_query.shape[0]
    local_width = cross_query.shape[1]
    ff_local = up_weight.shape[1]
    text_width = cross_kv.shape[0] * count
    own_images = max(image_count // 2, 1)
    first_image = t_index * (image_count // 2)

    skip_gather = Gather(skip_weight.astype(BF), cut_of(model_width), first=True)
    attention_shard = jnp.concatenate(
        [qkv_weight.astype(BF).reshape(shard_rows, -1), cross_query.astype(BF)], axis=1
    )
    attention_gather = Gather(attention_shard, 2 * local_width, first=True)

    activated_own = jax.nn.silu(timestep.astype(F32)).astype(BF)
    small_parts = [column_bias, up_bias, skip_gain, skip_bias, norm_gains, row_biases]
    small = jnp.concatenate([p.astype(BF).reshape(-1) for p in small_parts] + [activated_own.reshape(-1)])
    small_own = gather_small(small)
    small_other = swap(small_own)
    first_is_own = t_index == 0
    small_both = jnp.stack(
        [jnp.where(first_is_own, small_own, small_other), jnp.where(first_is_own, small_other, small_own)], axis=1
    )
    edges = np.cumsum([0] + [p.size for p in small_parts])
    own_f = small_own.astype(F32)
    both_f = small_both.astype(F32)
    column_slice = column_bias.shape[2]
    col_bf = (
        own_f[:, edges[0] : edges[1]].reshape(count, 6, column_slice).transpose(1, 0, 2).reshape(6, local_width)
    )
    up_bf = own_f[:, edges[1] : edges[2]].reshape(-1)
    sgain_f = both_f[:, :, edges[2] : edges[3]].reshape(-1)
    sbias_f = both_f[:, :, edges[3] : edges[4]].reshape(-1)
    ngain_f = both_f[:, :, edges[4] : edges[5]].reshape(count, 2, 3, -1).transpose(2, 0, 1, 3).reshape(3, model_width)
    rbias_f = both_f[:, :, edges[5] : edges[6]].reshape(count, 2, 8, -1).transpose(2, 0, 1, 3).reshape(8, model_width)
    activated = small_own[:, edges[6] :].reshape(count * image_count, model_width)

    skip_gather.double()
    skip_gather.spread()
    attention_gather.double()
    skip_gather.widen()
    out_t = out_weight.astype(BF).transpose(2, 0, 1).reshape(shard_rows, -1)
    pair_shard = cross_kv.astype(BF).reshape(shard_rows, -1)
    attention_gather.spread()
    skip_own = [skip_gather.finish(k, me) for k in range(2)]
    branch_gather = Gather(jnp.concatenate([out_t, pair_shard], axis=1), 2 * local_width)
    skip_w = weave(skip_own, [swap(v) for v in skip_own], me)
    attention_gather.widen()
    branch_gather.double()
    ffn_shard = jnp.concatenate([up_weight.astype(BF), down_weight.astype(BF).T], axis=1)
    ffn_gather = Gather(ffn_shard, ff_local)
    branch_gather.spread()

    device_index = f_index * 2 + t_index
    shift_rows = shift_weight.shape[0]
    activated_cut = lax.dynamic_slice_in_dim(activated, device_index * shift_rows, shift_rows, 1)
    shift_term = plain_dot(activated_cut, shift_weight.astype(BF))
    shift_term = shift_term + swap(shift_term)
    shift_image = reduce_small(shift_term.reshape(count, -1)).reshape(image_count, model_width) + rbias_f[7]
    shift_own = lax.dynamic_slice_in_dim(shift_image, first_image, own_images, 0)
    shift_tokens = jnp.repeat(shift_own, rows_local // own_images, axis=0)

    text_shift = first_image

    def roll_images(values, shift):
        if image_count == 1:
            return values
        shaped = values.reshape(image_count, -1, values.shape[-1])
        return jnp.roll(shaped, shift, axis=0).reshape(values.shape)

    text_len = text.shape[0] // image_count
    text_pad = 128 * ((text_len + 127) // 128)
    text_in = roll_images(text, -text_shift).reshape(image_count, text_len, -1)
    text_in = jnp.pad(text_in, ((0, 0), (0, text_pad - text_len), (0, 0))).reshape(image_count * text_pad, -1)
    pos_own = lax.dynamic_slice_in_dim(grid_pos, t_index * rows_local, rows_local, 0)
    pos_other = lax.dynamic_slice_in_dim(grid_pos, (1 - t_index) * rows_local, rows_local, 0)
    tables = rotary_columns(jnp.concatenate([pos_own, pos_other], axis=0))
    gains_column = head_gains[:, :, None]
    biases_column = head_biases[:, :, None]
    heads = local_width // HEAD_DIM

    def by_head(values, lead):
        return values.reshape(lead, heads, HEAD_DIM, values.shape[-1])

    joined = jnp.concatenate([hidden, skip_rows], axis=1).astype(F32)
    normed_skip = layer_norm(joined, sgain_f, sbias_f).astype(BF)
    stream_zero = plain_dot(normed_skip, skip_w) + rbias_f[6]
    first_in = with_other((layer_norm(stream_zero, ngain_f[0], rbias_f[0]) + shift_tokens).astype(BF))
    grad_ffn = with_other(cotangent)
    qk_w, vc_w = [attention_gather.finish(k, me).reshape(model_width, -1) for k in range(2)]
    ffn_gather.double()
    branch_gather.widen()
    v_w = vc_w[:, :local_width]
    query_w = vc_w[:, local_width:]
    qk_pre = by_head(turned_dot(qk_w, first_in) + col_bf[0:2].reshape(-1, 1), 2)
    v_pre = by_head(turned_dot(v_w, first_in) + col_bf[2].reshape(-1, 1), 1)
    mixture, self_lse = attend(
        qk_pre,
        qk_pre,
        v_pre,
        (0, 1, 0),
        gains_column[0:2],
        biases_column[0:2],
        tables,
        SEQ,
        True,
    )
    pair_w = branch_gather.finish(1, me)
    ffn_gather.spread()
    proj_t = branch_gather.finish(0, me)
    proj_t = proj_t.reshape(model_width, -1)
    pair_w = pair_w.reshape(text_width, 2 * local_width)
    self_t = proj_t[:, :local_width]
    cross_t = proj_t[:, local_width:]
    mixture = mixture.reshape(local_width, -1)
    stream_one = stream_zero + turned_branch_sum(mixture, self_t, rows_local) + rbias_f[3]
    second_in = with_other(layer_norm(stream_one, ngain_f[1], rbias_f[1]).astype(BF))
    cross_pre = by_head(turned_dot(query_w, second_in) + col_bf[3].reshape(-1, 1), 1)
    pair_pre = by_head(turned_dot(pair_w, text_in) + col_bf[4:6].reshape(-1, 1), 2)
    cross_mixture, cross_lse = attend(
        cross_pre, pair_pre, pair_pre, (0, 0, 1), gains_column[2:4], biases_column[2:4], tables, text_len, False
    )
    ffn_gather.widen()
    cross_mixture = cross_mixture.reshape(local_width, -1)
    stream_two = stream_one + turned_branch_sum(cross_mixture, cross_t, rows_local) + rbias_f[4]
    third_in = with_other(layer_norm(stream_two, ngain_f[2], rbias_f[2]).astype(BF))
    up_w = ffn_gather.finish(0, me).reshape(model_width, -1)
    hidden_act, slope = first_layer(third_in, up_w, up_bf)
    down_t = ffn_gather.finish(1, me).reshape(model_width, -1)

    grad_pre, upb_sums = first_layer_back(grad_ffn, down_t, slope)
    grad_upb = jnp.sum(upb_sums, axis=0)
    tile = 512 if ff_local % 512 == 0 else None
    up = Chain(products([(UP_ORDER, [(third_in, grad_pre, False, 0, ff_local)])], me, tile=tile), UP_ORDER)
    down = Chain(products([(DOWN_ORDER, [(grad_ffn, hidden_act, False, 0, ff_local)])], me, tile=tile), DOWN_ORDER)
    third_part, third_got = branch_parts(grad_pre, up_w, rows_local)
    grad_two, low_two, sums_two = norm_back(third_part, third_got, stream_two, ngain_f[2], cotangent, 1)
    grad_cross = with_other(low_two)
    grad_cmix = lax.dot_general(cross_t, grad_cross, (((0,), (1,)), ((), ())), preferred_element_type=F32).astype(BF)
    grad_cq, grad_pair, cross_sums, cross_cols = attend_back(
        cross_pre,
        pair_pre,
        pair_pre,
        (0, 0, 1),
        by_head(grad_cmix, 1)[0],
        cross_lse,
        gains_column[2:4],
        biases_column[2:4],
        tables,
        text_len,
        False,
        False,
    )
    grad_cq = grad_cq.reshape(local_width, -1)
    grad_pair = grad_pair.reshape(2 * local_width, -1)
    second_part, second_got = turned_branch_parts(grad_cq, query_w, rows_local)
    up.step()
    grad_one, low_one, sums_one = norm_back(second_part, second_got, stream_one, ngain_f[1], grad_two, 1)
    down.step()
    grad_self = with_other(low_one)
    halves = products(
        [
            ((1, 2), [(grad_cross, cross_mixture, True, 0, local_width), (second_in, grad_cq, True, 0, local_width)]),
            ((2, 1), [(text_in, grad_pair, True, 0, 2 * local_width)]),
        ],
        me,
    )
    cross_kept, cross_sent = halves[0::2], halves[1::2]
    up.step()
    cross_got = [hop(cross_sent[0], 1), hop(cross_sent[1], 2)]
    grad_mix = lax.dot_general(self_t, grad_self, (((0,), (1,)), ((), ())), preferred_element_type=F32).astype(BF)
    grad_qkv, self_sums, self_cols = attend_back(
        qk_pre,
        qk_pre,
        v_pre,
        (0, 1, 0),
        by_head(grad_mix, 1)[0],
        self_lse,
        gains_column[0:2],
        biases_column[0:2],
        tables,
        SEQ,
        True,
        True,
    )
    down.step()
    cross_near = [add_near(v, g) for v, g in zip(cross_kept, cross_got)]
    cross_got = [hop(cross_near[0][1], 2), hop(cross_near[1][1], 1)]
    up.step()
    grad_qkv = grad_qkv.reshape(3 * local_width, -1)
    halves = products(
        [
            ((1, 2), [(first_in, grad_qkv, True, 0, 2 * local_width)]),
            (
                (2, 1),
                [
                    (first_in, grad_qkv, True, 2 * local_width, local_width),
                    (grad_self, mixture, True, 0, local_width),
                ],
            ),
        ],
        me,
    )
    self_kept, self_sent = halves[0::2], halves[1::2]
    self_got = [hop(self_sent[0], 1), hop(self_sent[1], 2)]
    cross_far = FarSum([(v[0], g) for v, g in zip(cross_near, cross_got)])
    down.step()
    grad_qk = grad_qkv[: 2 * local_width]
    grad_v = grad_qkv[2 * local_width :]
    first_part = turned_dot(grad_qk[:, rows_local:], qk_w) + turned_dot(grad_v[:, rows_local:], v_w)
    first_got = swap(first_part.astype(BF))
    first_part = turned_dot(grad_qk[:, :rows_local], qk_w) + turned_dot(grad_v[:, :rows_local], v_w)
    grad_zero, low_zero, sums_zero = norm_back(
        first_part, first_got, stream_zero, ngain_f[0], grad_one, own_images
    )
    skip_cut = model_width // 2
    skip_kept, skip_sent = products(
        [
            ((1, 2), [(normed_skip, low_zero, False, 0, skip_cut)]),
            ((2, 1), [(normed_skip, low_zero, False, skip_cut, skip_cut)]),
        ],
        me,
        paired=True,
    )
    skip_got = swap(skip_sent)
    skip_pair = [add_near(skip_kept, skip_got, part=k) for k in range(2)]
    skip_got = [hop(skip_pair[0][1], 1), hop(skip_pair[1][1], 2)]
    cross_far.step()
    input_grad, skip_grad, skip_sums = joined_back(low_zero, skip_w, hidden, skip_rows, sgain_f)
    self_near = [add_near(v, g) for v, g in zip(self_kept, self_got)]
    self_got = [hop(self_near[0][1], 2), hop(self_near[1][1], 1)]
    skip_near = [add_near(v[0], g) for v, g in zip(skip_pair, skip_got)]
    skip_got = [hop(skip_near[0][1], 2), hop(skip_near[1][1], 1)]
    stream_three = stream_two + branch_sum(hidden_act, down_t, rows_local) + rbias_f[5]
    output = stream_three.astype(BF)
    text_half = text_width // 2
    pair_own = lax.dynamic_slice_in_dim(pair_w, t_index * text_half, text_half, 0)
    pair_other = lax.dynamic_slice_in_dim(pair_w, (1 - t_index) * text_half, text_half, 0)
    text_grad = turned_dot(grad_pair, pair_own) + swap(turned_dot(grad_pair, pair_other).astype(BF)).astype(F32)
    text_grad = text_grad.reshape(image_count, text_pad, -1)[:, :text_len].reshape(image_count * text_len, -1)
    text_grad = roll_images(text_grad, text_shift)

    shift_sums = jnp.sum(sums_zero[:, 1], axis=1)
    if image_count == 1:
        shift_local = shift_sums
    else:
        shift_local = lax.dynamic_update_slice_in_dim(
            jnp.zeros((image_count, model_width), F32), shift_sums, first_image, 0
        )
    shift_held = (shift_local + swap(shift_local))[None]
    shift_masks = [0]

    def shift_double(held, mask):
        held = pin(held)
        return jnp.concatenate([held, hop(held, mask)], axis=0), shift_masks + [m + mask for m in shift_masks]

    far_bits = [4 << b for b in range(30) if 4 << b < count]
    for mask in far_bits:
        shift_held, shift_masks = shift_double(shift_held, mask)

    sums_zero, sums_one, sums_two = (jnp.sum(v, axis=(0, 2)) for v in (sums_zero, sums_one, sums_two))
    skip_sums = jnp.sum(skip_sums, axis=1)
    grad_gains = jnp.stack([sums_zero[0], sums_one[0], sums_two[0]], axis=0)
    grad_biases = jnp.stack(
        [
            sums_zero[1],
            sums_one[1],
            sums_two[1],
            sums_one[2],
            sums_two[2],
            jnp.sum(cotangent.astype(F32), axis=0),
            sums_zero[2],
            sums_zero[1],
        ],
        axis=0,
    )
    self_columns = jnp.sum(self_cols, axis=(0, 4)).reshape(3, local_width)
    cross_columns = jnp.sum(cross_cols, axis=(0, 4)).reshape(3, local_width)
    grad_colb = jnp.concatenate([self_columns, cross_columns], axis=0)
    self_heads = jnp.sum(self_sums, axis=2)
    cross_heads = jnp.sum(cross_sums, axis=2)
    head_part = jnp.concatenate([self_heads[:2], cross_heads[:2], self_heads[2:], cross_heads[2:]]).reshape(-1)

    def by_device(values):
        shaped = values.reshape(values.shape[0], count, 2, -1).transpose(2, 1, 0, 3)
        return shaped.reshape(2, count, -1)

    def for_own(values):
        is_own = (jnp.arange(2) == t_index)[:, None, None]
        return jnp.where(is_own, values[None], 0.0)

    blocks = jnp.concatenate(
        [
            by_device(skip_sums[0:1]),
            by_device(skip_sums[1:2]),
            by_device(grad_gains),
            by_device(grad_biases),
            jnp.broadcast_to(head_part, (2, count, head_part.shape[0])),
            for_own(grad_colb.reshape(6, count, -1).transpose(1, 0, 2).reshape(count, -1)),
            for_own(grad_upb.reshape(count, -1)),
        ],
        axis=-1,
    )
    padded = 1024 * ((blocks.shape[-1] + 1023) // 1024)
    blocks = jnp.pad(blocks, ((0, 0), (0, 0), (0, padded - blocks.shape[-1])))
    blocks = blocks.transpose(1, 0, 2).reshape(2 * count, padded // 128, 128)
    small_kept, small_sent = halve([blocks], (1, 2), me, paired=True)
    self_far = FarSum([(v[0], g) for v, g in zip(self_near, self_got)])
    skip_far = FarSum([(v[0], g) for v, g in zip(skip_near, skip_got)])
    small_pair = add_near(small_kept, swap(small_sent))
    small_got = hop(small_pair[1], 1)
    shift_held, shift_masks = shift_double(shift_held, 1)

    small_near = add_near(small_pair[0], small_got)
    small_got = hop(small_near[1], 2)
    self_far.step()
    skip_far.step()
    small_far = FarSum([(small_near[0], small_got)])
    shift_held, shift_masks = shift_double(shift_held, 2)
    small_far.step()
    cross_sum = cross_far.total()
    shift_all = order_from_masks(
        shift_held.reshape(count, image_count * model_width), np.array(shift_masks)
    ).reshape(count * image_count, model_width)
    sent_shift = lax.dot_general(
        activated_cut.astype(F32), shift_all, (((0,), (0,)), ((), ())), precision=PRECISE
    )
    self_sum = self_far.total()
    skip_sum = skip_far.total()
    small_sum = small_far.total().reshape(-1)
    sent_skip = jnp.concatenate([skip_sum[0, 0], skip_sum[1, 0]], axis=-1)
    sent_up, sent_down = up.total()[0], down.total()[0].T
    sent_cproj, sent_query = cross_sum[0, 0, :, :local_width], cross_sum[0, 0, :, local_width:]
    sent_pair = cross_sum[1, 0, : cross_kv.shape[0]].reshape(cross_kv.shape)
    sent_sproj = self_sum[1, 0, :, local_width:]
    lengths = [skip_gain.size, skip_bias.size, norm_gains.size, row_biases.size, head_gains.size, head_biases.size]
    lengths += [column_bias.size, up_bias.size]
    cuts = np.cumsum([0] + lengths)
    pieces = [small_sum[cuts[i] : cuts[i + 1]] for i in range(len(lengths))]

    sent_qkv = jnp.concatenate([self_sum[0, 0], self_sum[1, 0, :, :local_width]], axis=1).reshape(qkv_weight.shape)
    sent_proj = jnp.stack([sent_sproj.T, sent_cproj.T], axis=0)
    return (
        output,
        input_grad,
        skip_grad,
        text_grad,
        sent_skip,
        sent_shift,
        sent_qkv,
        sent_query,
        sent_pair,
        sent_proj,
        sent_up,
        sent_down,
        pieces[6].reshape(column_bias.shape),
        pieces[7].reshape(up_bias.shape),
        pieces[0],
        pieces[1],
        pieces[2].reshape(norm_gains.shape),
        pieces[3].reshape(row_biases.shape),
        pieces[4].reshape(head_gains.shape),
        pieces[5].reshape(head_biases.shape),
    )


def solution(mesh):
    in_specs = (
        P(("fsdp", "tp"), None),
        P(("fsdp", "tp"), None),
        P("fsdp", None),
        P("fsdp", None),
        P("fsdp", None),
        P(("fsdp", "tp"), None),
        P(("fsdp", "tp"), None),
        P(("fsdp", "tp"), None),
        P("fsdp", None, "tp"),
        P("fsdp", "tp"),
        P("fsdp", None, "tp"),
        P(None, "tp", "fsdp"),
        P("fsdp", "tp"),
        P("tp", "fsdp"),
        P(None, "tp", "fsdp"),
        P("tp", "fsdp"),
        P(("fsdp", "tp")),
        P(("fsdp", "tp")),
        P(None, ("fsdp", "tp")),
        P(None, ("fsdp", "tp")),
        P(),
        P(),
    )
    out_specs = (
        P(("fsdp", "tp"), None),
        P(("fsdp", "tp"), None),
        P(("fsdp", "tp"), None),
        P("fsdp", "tp"),
        P(("fsdp", "tp"), None),
        P(("fsdp", "tp"), None),
        P("fsdp", None, "tp"),
        P("fsdp", "tp"),
        P("fsdp", None, "tp"),
        P(None, "tp", "fsdp"),
        P("fsdp", "tp"),
        P("tp", "fsdp"),
        P(None, "tp", "fsdp"),
        P("tp", "fsdp"),
        P(("fsdp", "tp")),
        P(("fsdp", "tp")),
        P(None, ("fsdp", "tp")),
        P(None, ("fsdp", "tp")),
        P(),
        P(),
    )
    return jax.shard_map(body, mesh=mesh, in_specs=in_specs, out_specs=out_specs, check_vma=False)
```

```python
import functools

import jax
import jax.numpy as jnp
import numpy as np
from jax import lax
from jax.experimental import pallas as pl
from jax.experimental.pallas import tpu as pltpu
from jax.sharding import PartitionSpec as P

HEAD_DIM = 88
SEQ = 1024
EPS_NORM = 1e-06
PRECISE = lax.Precision.HIGHEST
BF = jnp.bfloat16
F32 = jnp.float32
LOG2E = 1.4426950408889634
UP_ORDER = (1, 2)
DOWN_ORDER = (4, 1, 2)
VMEM_LIMIT = 56 * 1024 * 1024


def hop(values, mask):
    count = lax.axis_size("fsdp")
    return lax.ppermute(values, "fsdp", [(i, i ^ mask) for i in range(count)])


def swap(values):
    return lax.ppermute(values, "tp", [(0, 1), (1, 0)])


def far_masks(count):
    return [4 * j for j in range(1, count // 4)]


def natural_masks(count):
    return np.array([(p // (count // 4) % 2) + 2 * (p // (count // 2)) + 4 * (p % (count // 4)) for p in range(count)])


def order_from_masks(values, masks):
    place = np.argsort(masks)
    table = jnp.asarray(place, jnp.int32)
    count = len(masks)
    wanted = jnp.arange(count, dtype=jnp.int32) ^ lax.axis_index("fsdp")
    return jnp.take(values, jnp.take(table, wanted), axis=0)


def gather_small(values):
    count = lax.axis_size("fsdp")
    parts = [values] + [hop(values, m) for m in far_masks(count)]
    held = jnp.stack(parts, axis=0)
    held = jnp.concatenate([held, hop(held, 1)], axis=0)
    held = jnp.concatenate([held, hop(held, 2)], axis=0)
    return order_from_masks(held, natural_masks(count))


def reduce_small(blocks):
    count = blocks.shape[0]
    masks = jnp.asarray(natural_masks(count), jnp.int32)
    held = jnp.take(blocks, masks ^ lax.axis_index("fsdp"), axis=0)
    half = count // 2
    held = held[:half] + hop(held[half:], 2)
    quarter = count // 4
    held = held[:quarter] + hop(held[quarter:], 1)
    total = held[0]
    for j, m in enumerate(far_masks(count)):
        total = total + hop(held[j + 1], m)
    return total


ANYWHERE = pl.BlockSpec(memory_space=pl.ANY)


def light(**work):
    return pl.CostEstimate(flops=1, bytes_accessed=1, transcendentals=0)


class Order:
    last = ()


def in_order(call):
    @functools.wraps(call)
    def ordered(*args, after=(), **kwargs):
        result = call(*args, after=tuple(after) + Order.last, **kwargs)
        Order.last = (result[0] if isinstance(result, (tuple, list)) else result,)
        return result

    return ordered


def steps_of(order, count):
    return tuple(order) + tuple(1 << b for b in range(30) if 1 << b < count and 1 << b not in order)


def near_mask(position, order):
    top = len(order) - 1
    return sum(((position >> (top - k)) & 1) * bit for k, bit in enumerate(order))


def place_of(mask, order):
    top = len(order) - 1
    return sum(((mask >> (bit.bit_length() - 1)) & 1) << (top - k) for k, bit in enumerate(order))


@in_order
def halve(arrays, order, me, after=(), paired=False):
    count = arrays[0].shape[0] // (2 if paired else 1)
    rows, columns = arrays[0].shape[1:]
    order = steps_of(order, count)
    many = len(arrays)
    total = 2 * count if paired else count
    half = total // 2

    def kernel(me_ref, *refs):
        sources = refs[:many]
        low, high, held, in_sems, out_sems = refs[many + len(after) :]
        own = me_ref[0]

        def load(p, k):
            block = own ^ near_mask(p % count, order)
            if paired:
                block = 2 * block + me_ref[1 + p // count]
            return pltpu.make_async_copy(sources[k].at[block], held.at[p, k], in_sems.at[p])

        def store(p):
            target = low if p < half else high
            return pltpu.make_async_copy(held.at[p], target.at[p % half], out_sems.at[p])

        for p in list(range(half, total)) + list(range(half)):
            for k in range(many):
                load(p, k).start()
        for p in list(range(half, total)) + list(range(half)):
            for k in range(many):
                load(p, k).wait()
            store(p).start()
        for p in range(total):
            store(p).wait()

    moved = total * many * rows * columns
    shape = jax.ShapeDtypeStruct((half, many, rows, columns), arrays[0].dtype)
    return pl.pallas_call(
        kernel,
        grid_spec=pltpu.PrefetchScalarGridSpec(
            num_scalar_prefetch=1,
            grid=(1,),
            in_specs=[ANYWHERE] * (many + len(after)),
            out_specs=[ANYWHERE] * 2,
            scratch_shapes=[
                pltpu.VMEM((total, many, rows, columns), arrays[0].dtype),
                pltpu.SemaphoreType.DMA((total,)),
                pltpu.SemaphoreType.DMA((total,)),
            ],
        ),
        out_shape=[shape, shape],
        compiler_params=pltpu.CompilerParams(vmem_limit_bytes=VMEM_LIMIT),
        cost_estimate=light(flops=0, bytes_accessed=4 * moved, transcendentals=0),
    )(me, *arrays, *after)


@in_order
def pin(values, after=()):
    def kernel(in_ref, *refs):
        refs[-1][...] = in_ref[...]

    whole = pl.BlockSpec(values.shape, lambda: (0,) * values.ndim)
    return pl.pallas_call(
        kernel,
        in_specs=[whole] + [ANYWHERE] * len(after),
        out_specs=whole,
        out_shape=jax.ShapeDtypeStruct(values.shape, values.dtype),
        cost_estimate=light(flops=0, bytes_accessed=4 * values.size, transcendentals=0),
    )(values, *after)


def tile_of(columns):
    return columns // 4 if columns % 512 == 0 else columns // 2 if columns % 256 == 0 else columns


@in_order
def add_near(kept, received, after=(), part=None):
    doubled, many, rows, columns = kept.shape[-4:]
    quarter = doubled // 2
    tile = columns // 2 if columns % 256 == 0 else columns
    group = max(quarter // 2, 1)

    def kernel(kept_low, kept_high, got_low, got_high, *refs):
        low, high = refs[len(after) :]
        for out, first, second in ((low, kept_low, got_low), (high, kept_high, got_high)):
            total = first[...].astype(F32) + second[...].astype(F32)
            out[...] = total.reshape(out.shape).astype(kept.dtype)

    block = (group, many, rows, tile)

    def spec(shift):
        if part is None:
            return pl.BlockSpec(block, lambda i, j: (i + shift, 0, 0, j))
        return pl.BlockSpec((1, *block), lambda i, j: (part, i + shift, 0, 0, j))

    out_spec = pl.BlockSpec(block, lambda i, j: (i, 0, 0, j))
    shape = jax.ShapeDtypeStruct((quarter, many, rows, columns), kept.dtype)
    size = doubled * many * rows * columns
    return pl.pallas_call(
        kernel,
        grid=(quarter // group, columns // tile),
        in_specs=[spec(0), spec(quarter // group), spec(0), spec(quarter // group)] + [ANYWHERE] * len(after),
        out_specs=[out_spec] * 2,
        out_shape=[shape, shape],
        compiler_params=pltpu.CompilerParams(vmem_limit_bytes=VMEM_LIMIT),
        cost_estimate=light(flops=size, bytes_accessed=6 * size, transcendentals=0),
    )(kept, kept, received, received, *after)


@in_order
def add_far(pairs, after=()):
    quarter, many, _, columns = pairs[0][0].shape
    heights = [pair[0].shape[2] for pair in pairs]
    rows = max(heights)
    half = quarter // 2
    parts = len(pairs)
    tile = tile_of(columns)
    arrays = [array for pair in pairs for array in pair]
    kind = arrays[0].dtype

    def kernel(*refs):
        outs = refs[2 * parts + len(after) :]
        for j in range(quarter):
            for p in range(parts):
                total = refs[2 * p][j].astype(F32) + refs[2 * p + 1][j].astype(F32)
                if heights[p] < rows:
                    total = jnp.concatenate([total, jnp.zeros((1, rows - heights[p], tile), F32)], axis=1)
                outs[j // half][p, j % half] = total.astype(kind)

    in_specs = [
        pl.BlockSpec((quarter, 1, height, tile), lambda k, i: (0, k, 0, i)) for height in heights for _ in range(2)
    ]
    out_spec = pl.BlockSpec((parts, half, 1, rows, tile), lambda k, i: (0, 0, k, 0, i))
    shape = (parts, half, many, rows, columns)
    size = parts * quarter * many * rows * columns
    return pl.pallas_call(
        kernel,
        grid=(many, columns // tile),
        in_specs=in_specs + [ANYWHERE] * len(after),
        out_specs=[out_spec] * 2,
        out_shape=[jax.ShapeDtypeStruct(shape, kind)] * 2,
        compiler_params=pltpu.CompilerParams(vmem_limit_bytes=VMEM_LIMIT),
        cost_estimate=light(flops=size, bytes_accessed=6 * size, transcendentals=0),
    )(*arrays, *after)


@in_order
def add_halves(kept, received, after=()):
    parts, quarter, many, rows, columns = kept.shape
    half = quarter // 2

    def kernel(kept_ref, got_ref, *refs):
        outs = refs[len(after) :]
        for j in range(quarter):
            total = kept_ref[:, j].astype(F32) + got_ref[:, j].astype(F32)
            outs[j // half][:, j % half] = total.astype(kept.dtype)

    tile = tile_of(columns)
    in_spec = pl.BlockSpec((parts, quarter, 1, rows, tile), lambda k, i: (0, 0, k, 0, i))
    out_spec = pl.BlockSpec((parts, half, 1, rows, tile), lambda k, i: (0, 0, k, 0, i))
    shape = jax.ShapeDtypeStruct((parts, half, many, rows, columns), kept.dtype)
    return pl.pallas_call(
        kernel,
        grid=(many, columns // tile),
        in_specs=[in_spec] * 2 + [ANYWHERE] * len(after),
        out_specs=[out_spec] * 2,
        out_shape=[shape] * 2,
        compiler_params=pltpu.CompilerParams(vmem_limit_bytes=VMEM_LIMIT),
        cost_estimate=light(flops=kept.size, bytes_accessed=6 * kept.size, transcendentals=0),
    )(kept, received, *after)


class FarSum:
    def __init__(self, pairs, after=()):
        self.low, self.high = add_far(pairs, after=after)
        self.mask = 4
        self.got = hop(self.high, self.mask)

    def step(self, after=()):
        self.low, self.high = add_halves(self.low, self.got, after=after)
        self.mask *= 2
        self.got = hop(self.high, self.mask)

    def total(self):
        while self.low.shape[1] > 1:
            self.step()
        return self.low[:, 0].astype(F32) + self.got[:, 0].astype(F32)


class Chain:
    def __init__(self, halves, order):
        self.order = steps_of(order, lax.axis_size("fsdp"))
        self.low, self.high = halves
        self.at = 0
        self.got = hop(self.high, self.order[0])

    def step(self, after=()):
        self.low, self.high = add_near(self.low, self.got, after=after)
        self.at += 1
        self.got = hop(self.high, self.order[self.at])

    def total(self):
        while self.low.shape[0] > 1:
            self.step()
        return self.low[0].astype(F32) + self.got[0].astype(F32)


@in_order
def join(first, second, after=()):
    count = first.shape[0]
    shape = (2 * count, *first.shape[1:])

    def kernel(first_ref, second_ref, *refs):
        out, held, sems = refs[len(after) :]

        def load(k):
            return pltpu.make_async_copy((first_ref, second_ref)[k], held.at[pl.ds(k * count, count)], sems.at[0, k])

        def store(k):
            part = pl.ds(k * count, count)
            return pltpu.make_async_copy(held.at[part], out.at[part], sems.at[1, k])

        for k in range(2):
            load(k).start()
        for k in range(2):
            load(k).wait()
            store(k).start()
        for k in range(2):
            store(k).wait()

    return pl.pallas_call(
        kernel,
        in_specs=[ANYWHERE] * (2 + len(after)),
        out_specs=ANYWHERE,
        out_shape=jax.ShapeDtypeStruct(shape, first.dtype),
        scratch_shapes=[pltpu.VMEM(shape, first.dtype), pltpu.SemaphoreType.DMA((2, 2))],
        compiler_params=pltpu.CompilerParams(vmem_limit_bytes=VMEM_LIMIT),
        cost_estimate=light(flops=0, bytes_accessed=8 * first.size, transcendentals=0),
    )(first, second, *after)


@in_order
def products(groups, me, after=(), paired=False, tile=None):
    devices = lax.axis_size("fsdp")
    total = 2 * devices if paired else devices
    half = total // 2
    lefts, rights = [], []
    plan = []
    for order, terms in groups:
        column = 0
        steps = []
        for left, right, turned, start, width in terms:
            for array, known in ((left, lefts), (right, rights)):
                if not any(array is other for other in known):
                    known.append(array)
            which = [k for k, other in enumerate(lefts) if other is left][0]
            where = [k for k, other in enumerate(rights) if other is right][0]
            steps.append((which, where, turned, start, width, column))
            column += width
        plan.append((steps_of(order, devices), steps, terms[0][0].shape[1], column))

    def kernel(me_ref, *refs):
        left_refs = refs[: len(lefts)]
        right_refs = refs[len(lefts) : len(lefts) + len(rights)]
        rest = refs[len(lefts) + len(rights) + len(after) :]
        outs = rest[: 2 if paired else 2 * len(plan)]
        sums = rest[len(outs)]
        turned_lefts = rest[len(outs) + 1 :]
        own = me_ref[0]

        @pl.when(pl.program_id(0) == 0)
        def _():
            for k, ref in enumerate(left_refs):
                turned_lefts[k][...] = ref[...].T

        for g, (order, steps, rows, columns) in enumerate(plan):
            height = rows // total
            for which, where, turned, start, width, column in steps:
                if turned:
                    value = lax.dot_general(
                        turned_lefts[which][...],
                        right_refs[where][start : start + width, :],
                        (((1,), (1,)), ((), ())),
                        preferred_element_type=F32,
                    )
                elif tile:
                    value = jnp.dot(turned_lefts[which][...], right_refs[where][...], preferred_element_type=F32)
                else:
                    value = jnp.dot(
                        turned_lefts[which][...],
                        right_refs[where][:, start : start + width],
                        preferred_element_type=F32,
                    )
                width = tile or width
                sums[:rows, column : column + width] = value
            columns = tile or columns
            for b in range(total):
                block = sums[b * height : (b + 1) * height, :columns].astype(BF)
                if paired:
                    place = place_of(own ^ (b // 2), order)
                    upper = me_ref[1] != b % 2
                else:
                    place = place_of(own ^ b, order)
                    upper = place >= half
                    place = place % half

                @pl.when(upper)
                def _(g=g, block=block, place=place):
                    if paired:
                        outs[1][g, place, 0] = block
                    else:
                        outs[2 * g + 1][place, 0] = block

                @pl.when(jnp.logical_not(upper))
                def _(g=g, block=block, place=place):
                    if paired:
                        outs[0][g, place, 0] = block
                    else:
                        outs[2 * g][place, 0] = block

    once = pl.Buffered(1)
    left_specs = [pl.BlockSpec(a.shape, lambda i, me: (0, 0), pipeline_mode=once) for a in lefts]
    if tile:
        tiles = plan[0][3] // tile
        right_specs = [pl.BlockSpec((rights[0].shape[0], tile), lambda i, me: (0, i))]
        rows = plan[0][2] // total
        out_specs = [pl.BlockSpec((half, 1, rows, tile), lambda i, me: (0, 0, 0, i))] * 2
        shapes = [(half, 1, rows, plan[0][3])] * 2
    else:
        tiles = 1
        right_specs = [pl.BlockSpec(a.shape, lambda i, me: (0, 0), pipeline_mode=once) for a in rights]
        if paired:
            shapes = [(len(plan), half, 1, plan[0][2] // total, plan[0][3])] * 2
        else:
            shapes = [(half, 1, rows // total, columns) for _, _, rows, columns in plan for _ in range(2)]
        out_specs = [
            pl.BlockSpec(shape, lambda i, me, n=len(shape): (0,) * n, pipeline_mode=once) for shape in shapes
        ]
    flops = sum(2 * left.shape[0] * rows * columns for (_, _, rows, columns), left in zip(plan, [lefts[0]] * len(plan)))
    moved = sum(2 * a.size for a in lefts + rights) + sum(2 * int(np.prod(shape)) for shape in shapes)
    return pl.pallas_call(
        kernel,
        grid_spec=pltpu.PrefetchScalarGridSpec(
            num_scalar_prefetch=1,
            grid=(tiles,),
            in_specs=left_specs + right_specs + [ANYWHERE] * len(after),
            out_specs=out_specs,
            scratch_shapes=[
                pltpu.VMEM((max(p[2] for p in plan), tile or max(p[3] for p in plan)), F32)
            ]
            + [pltpu.VMEM(a.shape[::-1], BF) for a in lefts],
        ),
        out_shape=[jax.ShapeDtypeStruct(shape, BF) for shape in shapes],
        compiler_params=pltpu.CompilerParams(vmem_limit_bytes=VMEM_LIMIT),
        cost_estimate=light(flops=flops, bytes_accessed=moved, transcendentals=0),
    )(me, *lefts, *rights, *after)


@in_order
def stack_near(halves, cut, after=()):
    half, rows, columns = halves[0].shape
    ranges = ((0, cut), (cut, columns - cut))

    def kernel(*refs):
        outs = refs[2 + len(after) : 4 + len(after)]
        held = refs[4 + len(after) : 6 + len(after)]
        sems = refs[-1]

        def load(p, k):
            source = refs[p].at[:, :, pl.ds(ranges[k][0], ranges[k][1])]
            return pltpu.make_async_copy(source, held[k].at[pl.ds(p * half, half)], sems.at[p, k])

        def store(p, k):
            part = pl.ds(p * half, half)
            return pltpu.make_async_copy(held[k].at[part], outs[k].at[part], sems.at[p, 2 + k])

        steps = [(p, k) for p in range(2) for k in range(2)]
        for step in steps:
            load(*step).start()
        for step in steps:
            load(*step).wait()
            store(*step).start()
        for step in steps:
            store(*step).wait()

    shapes = [(2 * half, rows, width) for _, width in ranges]
    return pl.pallas_call(
        kernel,
        in_specs=[ANYWHERE] * (2 + len(after)),
        out_specs=[ANYWHERE] * 2,
        out_shape=[jax.ShapeDtypeStruct(shape, BF) for shape in shapes],
        scratch_shapes=[pltpu.VMEM(shape, BF) for shape in shapes] + [pltpu.SemaphoreType.DMA((2, 4))],
        compiler_params=pltpu.CompilerParams(vmem_limit_bytes=VMEM_LIMIT),
        cost_estimate=light(flops=0, bytes_accessed=8 * half * rows * columns, transcendentals=0),
    )(*halves, *after)


@in_order
def assemble(low, high, order, me, after=()):
    half, rows, columns = low.shape
    count = 2 * half
    order = steps_of(order, count)

    def kernel(me_ref, *refs):
        out, held, in_sems, out_sems = refs[2 + len(after) :]
        own = me_ref[0]

        def load(k):
            return pltpu.make_async_copy(refs[k], held.at[k], in_sems.at[k])

        def store(k, p):
            block = own ^ near_mask(k * half + p, order)
            return pltpu.make_async_copy(held.at[k, p], out.at[block], out_sems.at[k, p])

        for k in range(2):
            load(k).start()
        for k in range(2):
            load(k).wait()
            for p in range(half):
                store(k, p).start()
        for k in range(2):
            for p in range(half):
                store(k, p).wait()

    return pl.pallas_call(
        kernel,
        grid_spec=pltpu.PrefetchScalarGridSpec(
            num_scalar_prefetch=1,
            grid=(1,),
            in_specs=[ANYWHERE] * (2 + len(after)),
            out_specs=ANYWHERE,
            scratch_shapes=[
                pltpu.VMEM((2, half, rows, columns), BF),
                pltpu.SemaphoreType.DMA((2,)),
                pltpu.SemaphoreType.DMA((2, half)),
            ],
        ),
        out_shape=jax.ShapeDtypeStruct((count, rows, columns), BF),
        compiler_params=pltpu.CompilerParams(vmem_limit_bytes=VMEM_LIMIT),
        cost_estimate=light(flops=0, bytes_accessed=4 * count * rows * columns, transcendentals=0),
    )(me, low, high, *after)


def cut_of(width):
    return 128 * ((width // 128 + 1) // 2)


class Gather:
    def __init__(self, shard, cut, first=False):
        self.cut = cut
        self.held = (shard if first else pin(shard))[None]
        self.mask = lax.axis_size("fsdp") // 2
        self.far = hop(self.held, self.mask)

    def double(self, after=()):
        self.held = join(self.held, self.far, after=after)
        self.mask //= 2
        self.far = hop(self.held, self.mask)

    def spread(self, after=()):
        while self.mask > 4:
            self.double(after)
        self.parts = stack_near((self.held, self.far), self.cut, after=after)
        self.near = [hop(self.parts[0], 1), hop(self.parts[1], 2)]

    def widen(self, after=()):
        self.low = [join(part, near, after=after) for part, near in zip(self.parts, self.near)]
        self.high = [hop(self.low[0], 2), hop(self.low[1], 1)]

    def finish(self, k, me, after=()):
        return assemble(self.low[k], self.high[k], ((2, 1), (1, 2))[k], me, after=after)


@in_order
def weave(own, other, me, after=()):
    count, rows, _ = own[0].shape
    widths = [v.shape[2] for v in own]
    starts = [0, widths[0]]

    def kernel(me_ref, *refs):
        out, held, in_sems, out_sem = refs[4 + len(after) :]

        def load(k):
            target = held.at[:, me_ref[1 + k // 2], :, pl.ds(starts[k % 2], widths[k % 2])]
            return pltpu.make_async_copy(refs[k], target, in_sems.at[k])

        for k in range(4):
            load(k).start()
        for k in range(4):
            load(k).wait()
        store = pltpu.make_async_copy(held, out, out_sem)
        store.start()
        store.wait()

    shape = (count, 2, rows, sum(widths))
    whole = pl.pallas_call(
        kernel,
        grid_spec=pltpu.PrefetchScalarGridSpec(
            num_scalar_prefetch=1,
            grid=(1,),
            in_specs=[ANYWHERE] * (4 + len(after)),
            out_specs=ANYWHERE,
            scratch_shapes=[
                pltpu.VMEM(shape, BF),
                pltpu.SemaphoreType.DMA((4,)),
                pltpu.SemaphoreType.DMA,
            ],
        ),
        out_shape=jax.ShapeDtypeStruct(shape, BF),
        compiler_params=pltpu.CompilerParams(vmem_limit_bytes=VMEM_LIMIT),
        cost_estimate=light(flops=0, bytes_accessed=8 * count * rows * sum(widths), transcendentals=0),
    )(me, *own, *other, *after)
    return whole.reshape(2 * count * rows, sum(widths))


def layer_norm(values, scales, offsets):
    center = values - jnp.mean(values, axis=-1, keepdims=True)
    spread = jnp.mean(center * center, axis=-1, keepdims=True)
    return center * lax.rsqrt(spread + EPS_NORM) * scales + offsets


def plain_dot(first_operand, second_operand):
    return jnp.dot(first_operand, second_operand, preferred_element_type=F32)


def dot_first(first_operand, second_operand):
    return lax.dot_general(first_operand, second_operand, (((0,), (0,)), ((), ())), preferred_element_type=F32)


def dot_last(first_operand, second_operand):
    return lax.dot_general(first_operand, second_operand, (((1,), (1,)), ((), ())), preferred_element_type=F32)


def turned_dot(first_operand, second_operand):
    return lax.dot_general(first_operand, second_operand, (((0,), (1,)), ((), ())), preferred_element_type=F32)


def fold_rows(values):
    return jnp.sum(values.reshape(-1, 8, values.shape[-1]), axis=0)


def row_block(rows):
    return 128 if rows % 128 == 0 else rows


@in_order
def norm_back(partial, received, stream, gain, residual, images, after=()):
    rows, width = stream.shape
    block = row_block(rows)
    per_image = rows // images // block

    def kernel(partial_ref, received_ref, stream_ref, gain_ref, residual_ref, *refs):
        out_ref, low_ref, sums_ref = refs[len(after) :]
        grad = partial_ref[...] + received_ref[...].astype(F32)
        values = stream_ref[...]
        center = values - jnp.mean(values, axis=-1, keepdims=True)
        inverse = lax.rsqrt(jnp.mean(center * center, axis=-1, keepdims=True) + EPS_NORM)
        normed = center * inverse
        scaled = grad * gain_ref[...]
        result = residual_ref[...].astype(F32) + inverse * (
            scaled
            - jnp.mean(scaled, axis=-1, keepdims=True)
            - normed * jnp.mean(scaled * normed, axis=-1, keepdims=True)
        )
        out_ref[...] = result
        low_ref[...] = result.astype(BF)

        @pl.when(pl.program_id(0) % per_image == 0)
        def _():
            sums_ref[...] = jnp.zeros_like(sums_ref)

        sums_ref[0, 0] += fold_rows(grad * normed)
        sums_ref[0, 1] += fold_rows(grad)
        sums_ref[0, 2] += fold_rows(result)

    rows_spec = pl.BlockSpec((block, width), lambda i: (i, 0))
    return pl.pallas_call(
        kernel,
        grid=(rows // block,),
        in_specs=[rows_spec, rows_spec, rows_spec, pl.BlockSpec((1, width), lambda i: (0, 0)), rows_spec]
        + [ANYWHERE] * len(after),
        out_specs=[rows_spec, rows_spec, pl.BlockSpec((1, 3, 8, width), lambda i: (i // per_image, 0, 0, 0))],
        out_shape=[
            jax.ShapeDtypeStruct((rows, width), F32),
            jax.ShapeDtypeStruct((rows, width), BF),
            jax.ShapeDtypeStruct((images, 3, 8, width), F32),
        ],
        compiler_params=pltpu.CompilerParams(vmem_limit_bytes=VMEM_LIMIT),
        cost_estimate=light(flops=20 * rows * width, bytes_accessed=20 * rows * width, transcendentals=0),
    )(partial, received, stream, gain.reshape(1, -1), residual, *after)


@in_order
def joined_back(low, weight, first, second, gain, after=()):
    rows, width = first.shape
    block = 256 if rows % 256 == 0 else rows

    def kernel(low_ref, weight_ref, first_ref, second_ref, gain_ref, *refs):
        first_out, second_out, sums_ref = refs[len(after) :]
        parts = [slice(0, width), slice(width, 2 * width)]
        values = [first_ref[...].astype(F32), second_ref[...].astype(F32)]
        grads = [
            lax.dot_general(low_ref[...], weight_ref[p, :], (((1,), (1,)), ((), ())), preferred_element_type=F32)
            for p in parts
        ]

        def mean(arrays):
            return sum(jnp.sum(a, axis=-1, keepdims=True) for a in arrays) * (0.5 / width)

        middle = mean(values)
        center = [v - middle for v in values]
        inverse = lax.rsqrt(mean([c * c for c in center]) + EPS_NORM)
        normed = [c * inverse for c in center]
        scaled = [g * gain_ref[:, p] for g, p in zip(grads, parts)]
        mean_scaled = mean(scaled)
        mean_product = mean([a * n for a, n in zip(scaled, normed)])
        results = [inverse * (a - mean_scaled - n * mean_product) for a, n in zip(scaled, normed)]
        first_out[...] = results[0]
        second_out[...] = results[1]

        @pl.when(pl.program_id(0) == 0)
        def _():
            sums_ref[...] = jnp.zeros_like(sums_ref)

        for p, g, n in zip(parts, grads, normed):
            sums_ref[0, :, p] += fold_rows(g * n)
            sums_ref[1, :, p] += fold_rows(g)

    rows_spec = pl.BlockSpec((block, width), lambda i: (i, 0))
    whole_spec = pl.BlockSpec(weight.shape, lambda i: (0, 0), pipeline_mode=pl.Buffered(1))
    return pl.pallas_call(
        kernel,
        grid=(rows // block,),
        in_specs=[rows_spec, whole_spec, rows_spec, rows_spec, pl.BlockSpec((1, 2 * width), lambda i: (0, 0))]
        + [ANYWHERE] * len(after),
        out_specs=[rows_spec, rows_spec, pl.BlockSpec((2, 8, 2 * width), lambda i: (0, 0, 0))],
        out_shape=[
            jax.ShapeDtypeStruct((rows, width), F32),
            jax.ShapeDtypeStruct((rows, width), F32),
            jax.ShapeDtypeStruct((2, 8, 2 * width), F32),
        ],
        compiler_params=pltpu.CompilerParams(vmem_limit_bytes=VMEM_LIMIT),
        cost_estimate=light(flops=40 * rows * width, bytes_accessed=20 * rows * width, transcendentals=0),
    )(low, weight, first, second, gain.reshape(1, -1), *after)


GELU_SCALE = 0.7978845608028654
GELU_CUBE = 0.044715


@in_order
def first_layer(rows_in, weight, bias, after=()):
    rows, depth = rows_in.shape
    width = weight.shape[1]
    tile = 512 if width % 512 == 0 else width
    block = 1024 if rows % 1024 == 0 else rows
    step = 256 if block % 256 == 0 else block

    def kernel(rows_ref, weight_ref, bias_ref, *refs):
        act_ref, slope_ref = refs[len(after) :]
        for start in range(0, block, step):
            part = pl.ds(start, step)
            h = jnp.dot(rows_ref[part, :], weight_ref[...], preferred_element_type=F32) + bias_ref[...]
            square = h * h
            t = jnp.tanh(GELU_SCALE * h * (1.0 + GELU_CUBE * square))
            both = 0.5 * (1.0 + t)
            act_ref[part, :] = (h * both).astype(BF)
            slope = both + 0.5 * h * (1.0 - t * t) * (GELU_SCALE * (1.0 + 3.0 * GELU_CUBE * square))
            slope_ref[part, :] = slope.astype(BF)

    out_spec = pl.BlockSpec((block, tile), lambda m, n: (m, n))
    shape = jax.ShapeDtypeStruct((rows, width), BF)
    return pl.pallas_call(
        kernel,
        grid=(rows // block, width // tile),
        in_specs=[
            pl.BlockSpec((block, depth), lambda m, n: (m, 0)),
            pl.BlockSpec((depth, tile), lambda m, n: (0, n)),
            pl.BlockSpec((1, tile), lambda m, n: (0, n)),
        ]
        + [ANYWHERE] * len(after),
        out_specs=[out_spec] * 2,
        out_shape=[shape] * 2,
        compiler_params=pltpu.CompilerParams(vmem_limit_bytes=VMEM_LIMIT),
        cost_estimate=light(
            flops=2 * rows * depth * width, bytes_accessed=2 * depth * width + 4 * rows * width, transcendentals=rows * width
        ),
    )(rows_in, weight, bias.reshape(1, -1), *after)


@in_order
def first_layer_back(grad, weight, slope, after=()):
    rows, depth = grad.shape
    width = weight.shape[1]
    tile = 512 if width % 512 == 0 else width
    block = 1024 if rows % 1024 == 0 else rows
    step = 256 if block % 256 == 0 else block

    def kernel(grad_ref, weight_ref, slope_ref, *refs):
        out_ref, sums_ref = refs[len(after) :]

        @pl.when(pl.program_id(1) == 0)
        def _():
            sums_ref[...] = jnp.zeros_like(sums_ref)

        for start in range(0, block, step):
            part = pl.ds(start, step)
            value = jnp.dot(grad_ref[part, :], weight_ref[...], preferred_element_type=F32)
            low = (value * slope_ref[part, :].astype(F32)).astype(BF)
            out_ref[part, :] = low
            sums_ref[...] += fold_rows(low.astype(F32))

    return pl.pallas_call(
        kernel,
        grid=(width // tile, rows // block),
        in_specs=[
            pl.BlockSpec((block, depth), lambda n, m: (m, 0)),
            pl.BlockSpec((depth, tile), lambda n, m: (0, n)),
            pl.BlockSpec((block, tile), lambda n, m: (m, n)),
        ]
        + [ANYWHERE] * len(after),
        out_specs=[pl.BlockSpec((block, tile), lambda n, m: (m, n)), pl.BlockSpec((8, tile), lambda n, m: (0, n))],
        out_shape=[jax.ShapeDtypeStruct((rows, width), BF), jax.ShapeDtypeStruct((8, width), F32)],
        compiler_params=pltpu.CompilerParams(vmem_limit_bytes=VMEM_LIMIT),
        cost_estimate=light(
            flops=2 * rows * depth * width, bytes_accessed=2 * depth * width + 4 * rows * width, transcendentals=0
        ),
    )(grad, weight, slope, *after)


def head_parts(values):
    center = values - jnp.sum(values, axis=0, keepdims=True) * (1.0 / HEAD_DIM)
    spread = jnp.sum(center * center, axis=0, keepdims=True) * (1.0 / HEAD_DIM)
    inverse = lax.rsqrt(spread + EPS_NORM)
    return center * inverse, inverse


def turn(values, up_table, down_table):
    up = pltpu.roll(values, HEAD_DIM - 1, 0)
    down = pltpu.roll(values, 1, 0)
    return up * up_table + down * down_table


def head_forward(values, gain, offset, tables):
    normed, _ = head_parts(values)
    result = normed * gain + offset
    if tables is not None:
        result = result * tables[0] + turn(result, tables[1], tables[2])
    return result.astype(BF)


def fold_lanes(values):
    total = values[:, :128]
    for start in range(128, values.shape[1], 128):
        total = total + values[:, start : start + 128]
    return total


def head_backward(grad, values, gain, tables):
    if tables is not None:
        grad = grad * tables[0] - turn(grad, tables[1], tables[2])
    normed, inverse = head_parts(values)
    scaled = grad * gain
    mean_scaled = jnp.sum(scaled, axis=0, keepdims=True) * (1.0 / HEAD_DIM)
    mean_product = jnp.sum(scaled * normed, axis=0, keepdims=True) * (1.0 / HEAD_DIM)
    result = inverse * (scaled - mean_scaled - normed * mean_product)
    return result, fold_lanes(grad * normed), fold_lanes(grad)


def score_mask(scores, valid):
    if valid == scores.shape[0]:
        return scores
    row = lax.broadcasted_iota(jnp.int32, scores.shape, 0)
    return jnp.where(row < valid, scores, -1e30)


CHUNK = 512


def attend_kernel(valid, turned, waits, q_ref, k_ref, v_ref, gain_ref, bias_ref, tab_ref, *refs):
    out_ref, lse_ref, q_s, kt_s, v_s = refs[waits:]
    scaling = HEAD_DIM ** (-0.5)
    tables = (tab_ref[0], tab_ref[1], tab_ref[2])
    q_s[...] = head_forward(q_ref[0, 0], gain_ref[0], bias_ref[0], tables)
    keys = head_forward(k_ref[0, 0], gain_ref[1], bias_ref[1], tables if turned else None)
    kt_s[...] = keys.T
    v_s[...] = v_ref[0, 0].astype(BF)
    for start in range(0, q_s.shape[1], CHUNK):
        cols = pl.ds(start, CHUNK)
        scores = jnp.dot(kt_s[...], q_s[:, cols], preferred_element_type=F32)
        scores = score_mask(scores, valid)
        peak = jnp.max(scores, axis=0, keepdims=True)
        exponent = jnp.exp2((scores - peak) * (scaling * LOG2E))
        summed = jnp.sum(exponent, axis=0, keepdims=True)
        mixed = jnp.dot(v_s[...], exponent.astype(BF), preferred_element_type=F32)
        out_ref[0, :, cols] = (mixed * (1.0 / summed)).astype(BF)
        lse_ref[0, :, cols] = peak * scaling + jnp.log(summed)


def head_specs(lead, length):
    return pl.BlockSpec((1, 1, HEAD_DIM, length), lambda i, h: (lead, h, 0, i))


@in_order
def attend(q_pre, k_pre, v_pre, leads, gains, biases, tables, valid, turned, after=()):
    heads = q_pre.shape[1]
    images = q_pre.shape[3] // SEQ
    key_len = k_pre.shape[3] // images
    per_head = pl.BlockSpec((2, HEAD_DIM, 1), lambda i, h: (0, 0, 0))
    work = images * heads * SEQ * key_len
    return pl.pallas_call(
        functools.partial(attend_kernel, valid, turned, len(after)),
        grid=(images, heads),
        in_specs=[
            head_specs(leads[0], SEQ),
            head_specs(leads[1], key_len),
            head_specs(leads[2], key_len),
            per_head,
            per_head,
            pl.BlockSpec((3, HEAD_DIM, SEQ), lambda i, h: (0, 0, i)),
        ]
        + [ANYWHERE] * len(after),
        out_specs=[
            pl.BlockSpec((1, HEAD_DIM, SEQ), lambda i, h: (h, 0, i)),
            pl.BlockSpec((1, 1, SEQ), lambda i, h: (h, 0, i)),
        ],
        out_shape=[
            jax.ShapeDtypeStruct((heads, HEAD_DIM, images * SEQ), BF),
            jax.ShapeDtypeStruct((heads, 1, images * SEQ), F32),
        ],
        scratch_shapes=[
            pltpu.VMEM((HEAD_DIM, SEQ), BF),
            pltpu.VMEM((key_len, HEAD_DIM), BF),
            pltpu.VMEM((HEAD_DIM, key_len), BF),
        ],
        compiler_params=pltpu.CompilerParams(vmem_limit_bytes=VMEM_LIMIT),
        cost_estimate=light(flops=4 * work * 128, bytes_accessed=12 * q_pre.size, transcendentals=work),
    )(q_pre, k_pre, v_pre, gains, biases, tables, *after)


def attend_back_kernel(
    valid, turned, joint, waits, q_ref, k_ref, v_ref, mix_ref, lse_ref, gain_ref, bias_ref, tab_ref, *rest
):
    rest = rest[waits:]
    if joint:
        g_ref, sums_ref, cols_ref, q_s, k_s, kt_s, vt_s, dq_s, dk_s, dv_s = rest
    else:
        gq_ref, gkv_ref, sums_ref, cols_ref, q_s, k_s, kt_s, vt_s, dq_s, dk_s, dv_s = rest
    scaling = HEAD_DIM ** (-0.5)
    tables = (tab_ref[0], tab_ref[1], tab_ref[2])
    key_tables = tables if turned else None
    q_s[...] = head_forward(q_ref[0, 0], gain_ref[0], bias_ref[0], tables)
    keys = head_forward(k_ref[0, 0], gain_ref[1], bias_ref[1], key_tables)
    k_s[...] = keys
    kt_s[...] = keys.T
    vt_s[...] = v_ref[0, 0].astype(BF).T
    last = (((1,), (1,)), ((), ()))
    for start in range(0, q_s.shape[1], CHUNK):
        cols = pl.ds(start, CHUNK)
        scores = jnp.dot(kt_s[...], q_s[:, cols], preferred_element_type=F32)
        scores = score_mask(scores, valid)
        chances = jnp.exp2(scores * (scaling * LOG2E) - lse_ref[0, :, cols] * LOG2E)
        grad_mix = mix_ref[0, :, cols]
        grad_chance = jnp.dot(vt_s[...], grad_mix, preferred_element_type=F32)
        row_sum = jnp.sum(grad_chance * chances, axis=0, keepdims=True)
        grad_low = (chances * (grad_chance - row_sum)).astype(BF)
        dq_s[:, cols] = jnp.dot(k_s[...], grad_low, preferred_element_type=F32) * scaling
        key_term = lax.dot_general(q_s[:, cols], grad_low, last, preferred_element_type=F32) * scaling
        value_term = lax.dot_general(grad_mix, chances.astype(BF), last, preferred_element_type=F32)
        if start == 0:
            dk_s[...] = key_term
            dv_s[...] = value_term
        else:
            dk_s[...] += key_term
            dv_s[...] += value_term
    grad_q, gain_q, bias_q = head_backward(dq_s[...], q_ref[0, 0], gain_ref[0], tables)
    grad_k, gain_k, bias_k = head_backward(dk_s[...], k_ref[0, 0], gain_ref[1], key_tables)
    outs = [grad_q.astype(BF), grad_k.astype(BF), dv_s[...].astype(BF)]
    if joint:
        for j in range(3):
            g_ref[j, 0] = outs[j]
    else:
        gq_ref[0, 0] = outs[0]
        gkv_ref[0, 0] = outs[1]
        gkv_ref[1, 0] = outs[2]

    @pl.when((pl.program_id(0) == 0) & (pl.program_id(1) == 0))
    def _():
        sums_ref[...] = jnp.zeros_like(sums_ref)

    for j, part in enumerate((gain_q, gain_k, bias_q, bias_k)):
        sums_ref[j] += part
    for j, part in enumerate(outs):
        cols_ref[0, j, 0] = fold_lanes(part.astype(F32))


@in_order
def attend_back(q_pre, k_pre, v_pre, leads, grad_mix, lse, gains, biases, tables, valid, turned, joint, after=()):
    heads = q_pre.shape[1]
    images = q_pre.shape[3] // SEQ
    key_len = k_pre.shape[3] // images
    per_head = pl.BlockSpec((2, HEAD_DIM, 1), lambda i, h: (0, 0, 0))
    work = images * heads * SEQ * key_len
    grads = [(3, SEQ)] if joint else [(1, SEQ), (2, key_len)]
    return pl.pallas_call(
        functools.partial(attend_back_kernel, valid, turned, joint, len(after)),
        grid=(images, heads),
        in_specs=[
            head_specs(leads[0], SEQ),
            head_specs(leads[1], key_len),
            head_specs(leads[2], key_len),
            pl.BlockSpec((1, HEAD_DIM, SEQ), lambda i, h: (h, 0, i)),
            pl.BlockSpec((1, 1, SEQ), lambda i, h: (h, 0, i)),
            per_head,
            per_head,
            pl.BlockSpec((3, HEAD_DIM, SEQ), lambda i, h: (0, 0, i)),
        ]
        + [ANYWHERE] * len(after),
        out_specs=[
            pl.BlockSpec((size, 1, HEAD_DIM, length), lambda i, h: (0, h, 0, i)) for size, length in grads
        ]
        + [
            pl.BlockSpec((4, HEAD_DIM, 128), lambda i, h: (0, 0, 0)),
            pl.BlockSpec((1, 3, 1, HEAD_DIM, 128), lambda i, h: (i, 0, h, 0, 0)),
        ],
        out_shape=[jax.ShapeDtypeStruct((size, heads, HEAD_DIM, images * length), BF) for size, length in grads]
        + [
            jax.ShapeDtypeStruct((4, HEAD_DIM, 128), F32),
            jax.ShapeDtypeStruct((images, 3, heads, HEAD_DIM, 128), F32),
        ],
        scratch_shapes=[
            pltpu.VMEM((HEAD_DIM, SEQ), BF),
            pltpu.VMEM((HEAD_DIM, key_len), BF),
            pltpu.VMEM((key_len, HEAD_DIM), BF),
            pltpu.VMEM((key_len, HEAD_DIM), BF),
            pltpu.VMEM((HEAD_DIM, SEQ), F32),
            pltpu.VMEM((HEAD_DIM, key_len), F32),
            pltpu.VMEM((HEAD_DIM, key_len), F32),
        ],
        compiler_params=pltpu.CompilerParams(vmem_limit_bytes=VMEM_LIMIT),
        cost_estimate=light(flops=10 * work * 128, bytes_accessed=20 * q_pre.size, transcendentals=work),
    )(q_pre, k_pre, v_pre, grad_mix, lse, gains, biases, tables, *after)


def rotary_columns(positions):
    quarter = HEAD_DIM // 4
    freqs = 10000.0 ** (-jnp.arange(quarter).astype(F32) / quarter)
    coords = positions.astype(F32).T
    angles = jnp.concatenate([freqs[:, None] * coords[0:1], freqs[:, None] * coords[1:2]], axis=0)
    angles = jnp.repeat(angles, 2, axis=0)
    even = (jnp.arange(HEAD_DIM) % 2 == 0)[:, None]
    sine = jnp.sin(angles)
    return jnp.stack([jnp.cos(angles), jnp.where(even, -sine, 0.0), jnp.where(even, 0.0, sine)])


def with_other(values):
    return jnp.concatenate([values, swap(values)], axis=0)


def branch_sum(operand, weight, rows_local):
    sent = swap(dot_last(operand[rows_local:], weight).astype(BF))
    return dot_last(operand[:rows_local], weight) + sent.astype(F32)


def branch_parts(operand, weight, rows_local):
    sent = swap(dot_last(operand[rows_local:], weight).astype(BF))
    return dot_last(operand[:rows_local], weight), sent


def turned_branch_parts(operand, weight, rows_local):
    sent = swap(turned_dot(operand[:, rows_local:], weight).astype(BF))
    return turned_dot(operand[:, :rows_local], weight), sent


def turned_branch_sum(operand, weight, rows_local):
    sent = swap(turned_dot(operand[:, rows_local:], weight).astype(BF))
    return turned_dot(operand[:, :rows_local], weight) + sent.astype(F32)


def body(
    hidden,
    skip_rows,
    timestep,
    text,
    grid_pos,
    cotangent,
    skip_weight,
    shift_weight,
    qkv_weight,
    cross_query,
    cross_kv,
    out_weight,
    up_weight,
    down_weight,
    column_bias,
    up_bias,
    skip_gain,
    skip_bias,
    norm_gains,
    row_biases,
    head_gains,
    head_biases,
):
    Order.last = ()
    count = lax.axis_size("fsdp")
    f_index = lax.axis_index("fsdp")
    t_index = lax.axis_index("tp")
    me = jnp.stack([f_index, t_index, 1 - t_index]).astype(jnp.int32)
    rows_local, model_width = hidden.shape
    image_count = timestep.shape[0]
    shard_rows = cross_query.shape[0]
    local_width = cross_query.shape[1]
    ff_local = up_weight.shape[1]
    text_width = cross_kv.shape[0] * count
    own_images = max(image_count // 2, 1)
    first_image = t_index * (image_count // 2)

    skip_gather = Gather(skip_weight.astype(BF), cut_of(model_width), first=True)
    attention_shard = jnp.concatenate(
        [qkv_weight.astype(BF).reshape(shard_rows, -1), cross_query.astype(BF)], axis=1
    )
    attention_gather = Gather(attention_shard, 2 * local_width, first=True)

    activated_own = jax.nn.silu(timestep.astype(F32)).astype(BF)
    small_parts = [column_bias, up_bias, skip_gain, skip_bias, norm_gains, row_biases]
    small = jnp.concatenate([p.astype(BF).reshape(-1) for p in small_parts] + [activated_own.reshape(-1)])
    small_own = gather_small(small)
    small_other = swap(small_own)
    first_is_own = t_index == 0
    small_both = jnp.stack(
        [jnp.where(first_is_own, small_own, small_other), jnp.where(first_is_own, small_other, small_own)], axis=1
    )
    edges = np.cumsum([0] + [p.size for p in small_parts])
    own_f = small_own.astype(F32)
    both_f = small_both.astype(F32)
    column_slice = column_bias.shape[2]
    col_bf = (
        own_f[:, edges[0] : edges[1]].reshape(count, 6, column_slice).transpose(1, 0, 2).reshape(6, local_width)
    )
    up_bf = own_f[:, edges[1] : edges[2]].reshape(-1)
    sgain_f = both_f[:, :, edges[2] : edges[3]].reshape(-1)
    sbias_f = both_f[:, :, edges[3] : edges[4]].reshape(-1)
    ngain_f = both_f[:, :, edges[4] : edges[5]].reshape(count, 2, 3, -1).transpose(2, 0, 1, 3).reshape(3, model_width)
    rbias_f = both_f[:, :, edges[5] : edges[6]].reshape(count, 2, 8, -1).transpose(2, 0, 1, 3).reshape(8, model_width)
    activated = small_own[:, edges[6] :].reshape(count * image_count, model_width)

    skip_gather.double()
    skip_gather.spread()
    attention_gather.double()
    skip_gather.widen()
    out_t = out_weight.astype(BF).transpose(2, 0, 1).reshape(shard_rows, -1)
    pair_shard = cross_kv.astype(BF).reshape(shard_rows, -1)
    attention_gather.spread()
    skip_own = [skip_gather.finish(k, me) for k in range(2)]
    branch_gather = Gather(jnp.concatenate([out_t, pair_shard], axis=1), 2 * local_width)
    skip_w = weave(skip_own, [swap(v) for v in skip_own], me)
    attention_gather.widen()
    branch_gather.double()
    ffn_shard = jnp.concatenate([up_weight.astype(BF), down_weight.astype(BF).T], axis=1)
    ffn_gather = Gather(ffn_shard, ff_local)
    branch_gather.spread()

    device_index = f_index * 2 + t_index
    shift_rows = shift_weight.shape[0]
    activated_cut = lax.dynamic_slice_in_dim(activated, device_index * shift_rows, shift_rows, 1)
    shift_term = plain_dot(activated_cut, shift_weight.astype(BF))
    shift_term = shift_term + swap(shift_term)
    shift_image = reduce_small(shift_term.reshape(count, -1)).reshape(image_count, model_width) + rbias_f[7]
    shift_own = lax.dynamic_slice_in_dim(shift_image, first_image, own_images, 0)
    shift_tokens = jnp.repeat(shift_own, rows_local // own_images, axis=0)

    text_shift = first_image

    def roll_images(values, shift):
        if image_count == 1:
            return values
        shaped = values.reshape(image_count, -1, values.shape[-1])
        return jnp.roll(shaped, shift, axis=0).reshape(values.shape)

    text_len = text.shape[0] // image_count
    text_pad = 128 * ((text_len + 127) // 128)
    text_in = roll_images(text, -text_shift).reshape(image_count, text_len, -1)
    text_in = jnp.pad(text_in, ((0, 0), (0, text_pad - text_len), (0, 0))).reshape(image_count * text_pad, -1)
    pos_own = lax.dynamic_slice_in_dim(grid_pos, t_index * rows_local, rows_local, 0)
    pos_other = lax.dynamic_slice_in_dim(grid_pos, (1 - t_index) * rows_local, rows_local, 0)
    tables = rotary_columns(jnp.concatenate([pos_own, pos_other], axis=0))
    gains_column = head_gains[:, :, None]
    biases_column = head_biases[:, :, None]
    heads = local_width // HEAD_DIM

    def by_head(values, lead):
        return values.reshape(lead, heads, HEAD_DIM, values.shape[-1])

    joined = jnp.concatenate([hidden, skip_rows], axis=1).astype(F32)
    normed_skip = layer_norm(joined, sgain_f, sbias_f).astype(BF)
    stream_zero = plain_dot(normed_skip, skip_w) + rbias_f[6]
    first_in = with_other((layer_norm(stream_zero, ngain_f[0], rbias_f[0]) + shift_tokens).astype(BF))
    grad_ffn = with_other(cotangent)
    qk_w, vc_w = [attention_gather.finish(k, me).reshape(model_width, -1) for k in range(2)]
    ffn_gather.double()
    branch_gather.widen()
    v_w = vc_w[:, :local_width]
    query_w = vc_w[:, local_width:]
    qk_pre = by_head(turned_dot(qk_w, first_in) + col_bf[0:2].reshape(-1, 1), 2)
    v_pre = by_head(turned_dot(v_w, first_in) + col_bf[2].reshape(-1, 1), 1)
    mixture, self_lse = attend(
        qk_pre,
        qk_pre,
        v_pre,
        (0, 1, 0),
        gains_column[0:2],
        biases_column[0:2],
        tables,
        SEQ,
        True,
    )
    pair_w = branch_gather.finish(1, me)
    ffn_gather.spread()
    proj_t = branch_gather.finish(0, me)
    proj_t = proj_t.reshape(model_width, -1)
    pair_w = pair_w.reshape(text_width, 2 * local_width)
    self_t = proj_t[:, :local_width]
    cross_t = proj_t[:, local_width:]
    mixture = mixture.reshape(local_width, -1)
    stream_one = stream_zero + turned_branch_sum(mixture, self_t, rows_local) + rbias_f[3]
    second_in = with_other(layer_norm(stream_one, ngain_f[1], rbias_f[1]).astype(BF))
    cross_pre = by_head(turned_dot(query_w, second_in) + col_bf[3].reshape(-1, 1), 1)
    pair_pre = by_head(turned_dot(pair_w, text_in) + col_bf[4:6].reshape(-1, 1), 2)
    cross_mixture, cross_lse = attend(
        cross_pre, pair_pre, pair_pre, (0, 0, 1), gains_column[2:4], biases_column[2:4], tables, text_len, False
    )
    ffn_gather.widen()
    cross_mixture = cross_mixture.reshape(local_width, -1)
    stream_two = stream_one + turned_branch_sum(cross_mixture, cross_t, rows_local) + rbias_f[4]
    third_in = with_other(layer_norm(stream_two, ngain_f[2], rbias_f[2]).astype(BF))
    up_w = ffn_gather.finish(0, me).reshape(model_width, -1)
    hidden_act, slope = first_layer(third_in, up_w, up_bf)
    down_t = ffn_gather.finish(1, me).reshape(model_width, -1)

    grad_pre, upb_sums = first_layer_back(grad_ffn, down_t, slope)
    grad_upb = jnp.sum(upb_sums, axis=0)
    tile = 512 if ff_local % 512 == 0 else None
    up = Chain(products([(UP_ORDER, [(third_in, grad_pre, False, 0, ff_local)])], me, tile=tile), UP_ORDER)
    down = Chain(products([(DOWN_ORDER, [(grad_ffn, hidden_act, False, 0, ff_local)])], me, tile=tile), DOWN_ORDER)
    third_part, third_got = branch_parts(grad_pre, up_w, rows_local)
    grad_two, low_two, sums_two = norm_back(third_part, third_got, stream_two, ngain_f[2], cotangent, 1)
    grad_cross = with_other(low_two)
    grad_cmix = lax.dot_general(cross_t, grad_cross, (((0,), (1,)), ((), ())), preferred_element_type=F32).astype(BF)
    grad_cq, grad_pair, cross_sums, cross_cols = attend_back(
        cross_pre,
        pair_pre,
        pair_pre,
        (0, 0, 1),
        by_head(grad_cmix, 1)[0],
        cross_lse,
        gains_column[2:4],
        biases_column[2:4],
        tables,
        text_len,
        False,
        False,
    )
    grad_cq = grad_cq.reshape(local_width, -1)
    grad_pair = grad_pair.reshape(2 * local_width, -1)
    second_part, second_got = turned_branch_parts(grad_cq, query_w, rows_local)
    up.step()
    grad_one, low_one, sums_one = norm_back(second_part, second_got, stream_one, ngain_f[1], grad_two, 1)
    down.step()
    grad_self = with_other(low_one)
    halves = products(
        [
            ((1, 2), [(grad_cross, cross_mixture, True, 0, local_width), (second_in, grad_cq, True, 0, local_width)]),
            ((2, 1), [(text_in, grad_pair, True, 0, 2 * local_width)]),
        ],
        me,
    )
    cross_kept, cross_sent = halves[0::2], halves[1::2]
    up.step()
    cross_got = [hop(cross_sent[0], 1), hop(cross_sent[1], 2)]
    grad_mix = lax.dot_general(self_t, grad_self, (((0,), (1,)), ((), ())), preferred_element_type=F32).astype(BF)
    grad_qkv, self_sums, self_cols = attend_back(
        qk_pre,
        qk_pre,
        v_pre,
        (0, 1, 0),
        by_head(grad_mix, 1)[0],
        self_lse,
        gains_column[0:2],
        biases_column[0:2],
        tables,
        SEQ,
        True,
        True,
    )
    down.step()
    cross_near = [add_near(v, g) for v, g in zip(cross_kept, cross_got)]
    cross_got = [hop(cross_near[0][1], 2), hop(cross_near[1][1], 1)]
    up.step()
    grad_qkv = grad_qkv.reshape(3 * local_width, -1)
    halves = products(
        [
            ((1, 2), [(first_in, grad_qkv, True, 0, 2 * local_width)]),
            (
                (2, 1),
                [
                    (first_in, grad_qkv, True, 2 * local_width, local_width),
                    (grad_self, mixture, True, 0, local_width),
                ],
            ),
        ],
        me,
    )
    self_kept, self_sent = halves[0::2], halves[1::2]
    self_got = [hop(self_sent[0], 1), hop(self_sent[1], 2)]
    cross_far = FarSum([(v[0], g) for v, g in zip(cross_near, cross_got)])
    down.step()
    grad_qk = grad_qkv[: 2 * local_width]
    grad_v = grad_qkv[2 * local_width :]
    first_part = turned_dot(grad_qk[:, rows_local:], qk_w) + turned_dot(grad_v[:, rows_local:], v_w)
    first_got = swap(first_part.astype(BF))
    first_part = turned_dot(grad_qk[:, :rows_local], qk_w) + turned_dot(grad_v[:, :rows_local], v_w)
    grad_zero, low_zero, sums_zero = norm_back(
        first_part, first_got, stream_zero, ngain_f[0], grad_one, own_images
    )
    skip_cut = model_width // 2
    skip_kept, skip_sent = products(
        [
            ((1, 2), [(normed_skip, low_zero, False, 0, skip_cut)]),
            ((2, 1), [(normed_skip, low_zero, False, skip_cut, skip_cut)]),
        ],
        me,
        paired=True,
    )
    skip_got = swap(skip_sent)
    skip_pair = [add_near(skip_kept, skip_got, part=k) for k in range(2)]
    skip_got = [hop(skip_pair[0][1], 1), hop(skip_pair[1][1], 2)]
    cross_far.step()
    input_grad, skip_grad, skip_sums = joined_back(low_zero, skip_w, hidden, skip_rows, sgain_f)
    self_near = [add_near(v, g) for v, g in zip(self_kept, self_got)]
    self_got = [hop(self_near[0][1], 2), hop(self_near[1][1], 1)]
    skip_near = [add_near(v[0], g) for v, g in zip(skip_pair, skip_got)]
    skip_got = [hop(skip_near[0][1], 2), hop(skip_near[1][1], 1)]
    stream_three = stream_two + branch_sum(hidden_act, down_t, rows_local) + rbias_f[5]
    output = stream_three.astype(BF)
    text_half = text_width // 2
    pair_own = lax.dynamic_slice_in_dim(pair_w, t_index * text_half, text_half, 0)
    pair_other = lax.dynamic_slice_in_dim(pair_w, (1 - t_index) * text_half, text_half, 0)
    text_grad = turned_dot(grad_pair, pair_own) + swap(turned_dot(grad_pair, pair_other).astype(BF)).astype(F32)
    text_grad = text_grad.reshape(image_count, text_pad, -1)[:, :text_len].reshape(image_count * text_len, -1)
    text_grad = roll_images(text_grad, text_shift)

    shift_sums = jnp.sum(sums_zero[:, 1], axis=1)
    if image_count == 1:
        shift_local = shift_sums
    else:
        shift_local = lax.dynamic_update_slice_in_dim(
            jnp.zeros((image_count, model_width), F32), shift_sums, first_image, 0
        )
    shift_held = (shift_local + swap(shift_local))[None]
    shift_masks = [0]

    def shift_double(held, mask):
        held = pin(held)
        return jnp.concatenate([held, hop(held, mask)], axis=0), shift_masks + [m + mask for m in shift_masks]

    far_bits = [4 << b for b in range(30) if 4 << b < count]
    for mask in far_bits:
        shift_held, shift_masks = shift_double(shift_held, mask)

    sums_zero, sums_one, sums_two = (jnp.sum(v, axis=(0, 2)) for v in (sums_zero, sums_one, sums_two))
    skip_sums = jnp.sum(skip_sums, axis=1)
    grad_gains = jnp.stack([sums_zero[0], sums_one[0], sums_two[0]], axis=0)
    grad_biases = jnp.stack(
        [
            sums_zero[1],
            sums_one[1],
            sums_two[1],
            sums_one[2],
            sums_two[2],
            jnp.sum(cotangent.astype(F32), axis=0),
            sums_zero[2],
            sums_zero[1],
        ],
        axis=0,
    )
    self_columns = jnp.sum(self_cols, axis=(0, 4)).reshape(3, local_width)
    cross_columns = jnp.sum(cross_cols, axis=(0, 4)).reshape(3, local_width)
    grad_colb = jnp.concatenate([self_columns, cross_columns], axis=0)
    self_heads = jnp.sum(self_sums, axis=2)
    cross_heads = jnp.sum(cross_sums, axis=2)
    head_part = jnp.concatenate([self_heads[:2], cross_heads[:2], self_heads[2:], cross_heads[2:]]).reshape(-1)

    def by_device(values):
        shaped = values.reshape(values.shape[0], count, 2, -1).transpose(2, 1, 0, 3)
        return shaped.reshape(2, count, -1)

    def for_own(values):
        is_own = (jnp.arange(2) == t_index)[:, None, None]
        return jnp.where(is_own, values[None], 0.0)

    blocks = jnp.concatenate(
        [
            by_device(skip_sums[0:1]),
            by_device(skip_sums[1:2]),
            by_device(grad_gains),
            by_device(grad_biases),
            jnp.broadcast_to(head_part, (2, count, head_part.shape[0])),
            for_own(grad_colb.reshape(6, count, -1).transpose(1, 0, 2).reshape(count, -1)),
            for_own(grad_upb.reshape(count, -1)),
        ],
        axis=-1,
    )
    padded = 1024 * ((blocks.shape[-1] + 1023) // 1024)
    blocks = jnp.pad(blocks, ((0, 0), (0, 0), (0, padded - blocks.shape[-1])))
    blocks = blocks.transpose(1, 0, 2).reshape(2 * count, padded // 128, 128)
    small_kept, small_sent = halve([blocks], (1, 2), me, paired=True)
    self_far = FarSum([(v[0], g) for v, g in zip(self_near, self_got)])
    skip_far = FarSum([(v[0], g) for v, g in zip(skip_near, skip_got)])
    small_pair = add_near(small_kept, swap(small_sent))
    small_got = hop(small_pair[1], 1)
    shift_held, shift_masks = shift_double(shift_held, 1)

    small_near = add_near(small_pair[0], small_got)
    small_got = hop(small_near[1], 2)
    self_far.step()
    skip_far.step()
    small_far = FarSum([(small_near[0], small_got)])
    shift_held, shift_masks = shift_double(shift_held, 2)
    small_far.step()
    cross_sum = cross_far.total()
    shift_all = order_from_masks(
        shift_held.reshape(count, image_count * model_width), np.array(shift_masks)
    ).reshape(count * image_count, model_width)
    sent_shift = lax.dot_general(
        activated_cut.astype(F32), shift_all, (((0,), (0,)), ((), ())), precision=PRECISE
    )
    self_sum = self_far.total()
    skip_sum = skip_far.total()
    small_sum = small_far.total().reshape(-1)
    sent_skip = jnp.concatenate([skip_sum[0, 0], skip_sum[1, 0]], axis=-1)
    sent_up, sent_down = up.total()[0], down.total()[0].T
    sent_cproj, sent_query = cross_sum[0, 0, :, :local_width], cross_sum[0, 0, :, local_width:]
    sent_pair = cross_sum[1, 0, : cross_kv.shape[0]].reshape(cross_kv.shape)
    sent_sproj = self_sum[1, 0, :, local_width:]
    lengths = [skip_gain.size, skip_bias.size, norm_gains.size, row_biases.size, head_gains.size, head_biases.size]
    lengths += [column_bias.size, up_bias.size]
    cuts = np.cumsum([0] + lengths)
    pieces = [small_sum[cuts[i] : cuts[i + 1]] for i in range(len(lengths))]

    sent_qkv = jnp.concatenate([self_sum[0, 0], self_sum[1, 0, :, :local_width]], axis=1).reshape(qkv_weight.shape)
    sent_proj = jnp.stack([sent_sproj.T, sent_cproj.T], axis=0)
    return (
        output,
        input_grad,
        skip_grad,
        text_grad,
        sent_skip,
        sent_shift,
        sent_qkv,
        sent_query,
        sent_pair,
        sent_proj,
        sent_up,
        sent_down,
        pieces[6].reshape(column_bias.shape),
        pieces[7].reshape(up_bias.shape),
        pieces[0],
        pieces[1],
        pieces[2].reshape(norm_gains.shape),
        pieces[3].reshape(row_biases.shape),
        pieces[4].reshape(head_gains.shape),
        pieces[5].reshape(head_biases.shape),
    )


def solution(mesh):
    in_specs = (
        P(("fsdp", "tp"), None),
        P(("fsdp", "tp"), None),
        P("fsdp", None),
        P("fsdp", None),
        P("fsdp", None),
        P(("fsdp", "tp"), None),
        P(("fsdp", "tp"), None),
        P(("fsdp", "tp"), None),
        P("fsdp", None, "tp"),
        P("fsdp", "tp"),
        P("fsdp", None, "tp"),
        P(None, "tp", "fsdp"),
        P("fsdp", "tp"),
        P("tp", "fsdp"),
        P(None, "tp", "fsdp"),
        P("tp", "fsdp"),
        P(("fsdp", "tp")),
        P(("fsdp", "tp")),
        P(None, ("fsdp", "tp")),
        P(None, ("fsdp", "tp")),
        P(),
        P(),
    )
    out_specs = (
        P(("fsdp", "tp"), None),
        P(("fsdp", "tp"), None),
        P(("fsdp", "tp"), None),
        P("fsdp", "tp"),
        P(("fsdp", "tp"), None),
        P(("fsdp", "tp"), None),
        P("fsdp", None, "tp"),
        P("fsdp", "tp"),
        P("fsdp", None, "tp"),
        P(None, "tp", "fsdp"),
        P("fsdp", "tp"),
        P("tp", "fsdp"),
        P(None, "tp", "fsdp"),
        P("tp", "fsdp"),
        P(("fsdp", "tp")),
        P(("fsdp", "tp")),
        P(None, ("fsdp", "tp")),
        P(None, ("fsdp", "tp")),
        P(),
        P(),
    )
    return jax.shard_map(body, mesh=mesh, in_specs=in_specs, out_specs=out_specs, check_vma=False)
```
